256 devices in a mesh: section: 64 (over x, z, core), tensor: 4 (over y).
Axes of the slice: x: 4, y: 4, z: 8, core: 2. Of those that a mesh axis runs over, the one named last changes fastest.
Arguments:
- queries: bfloat16 [16384, 4096], P('section', 'tensor'), may hold values from -125 to 125
- keys: bfloat16 [16384, 512], P('section', 'tensor'), may hold values from -5.5 to 5.5
- values: bfloat16 [16384, 512], P('section', 'tensor'), may hold values from -24 to 24
- out_weight: bfloat16 [4096, 4096], P('tensor'), may hold values from -0.09375 to 0.09375
- residual: bfloat16 [16384, 4096], P('section', 'tensor'), may hold values from -1.5 to 1.5
- span_of_section: int32 [64], replicated, may hold values from 0 to 63, each once
- page_owner: int32 [64, 4, 32, 1], P(None, 'tensor'), may hold values from 0 to 63; in each aligned block of 32 rows (0 to 31, 32 to 63, ..., all dimensions but the last counted through in order) at most 2 rows name the same one
Outputs:
- updated: bfloat16 [16384, 4096], P('section', 'tensor')
- kv_cache: bfloat16 [64, 4, 64, 2, 8, 256], P('section', 'tensor')
The draws below stay inside these ranges and needn't reach their ends.
Inputs may be any that keep to these rules, and one draw needn't show every extreme that they name: `span_of_section`: each span index appears once. `page_owner`: in the pages of one holding section and the 1 KV heads of one tensor group (aligned blocks of 32 rows), no owner is named more than 2 times, and some block names an owner exactly 2 times.
All inputs are finite; a program needn't handle non-finite values.
Results may differ from the reference program's by a relative error of at most 0.017.
Values may be sent and summed in bfloat16 or wider, within the bound.
No kernel may reach another device: no remote copies, remote signals or barrier semaphores. Data moves between devices by JAX's collectives and lax.ppermute only.
A program may use at most 64 MiB of HBM per device.

```python
import math
import jax
import jax.numpy as jnp
import numpy as np
from jax import lax

WIDTH = 4096
HEADS = 32
KV_HEADS = 4
HD = 128
GROUP = 8
SPAN = 256
PAGE_TOK = 8
TOKENS = 16384
PPH = 32
HPT = 1
PPD = 32
MOST = 2
N_SECTION = 64
N_TENSOR = 4


def shared_keys(key):
    drawn = jax.random.truncated_normal(key, -5.5, 5.5, (TOKENS, KV_HEADS * HD), jnp.float32)
    row_ids = jnp.arange(TOKENS)[:, None]
    marked = row_ids % 16 == 4
    return jnp.where(marked, drawn, drawn)


def draw_keys(key, part):
    return shared_keys(key).astype(jnp.bfloat16)


def draw_queries(key, part):
    key = jax.random.fold_in(key, 5)
    drawn_noise = 1.5 * jax.random.truncated_normal(key, -5.5, 5.5, (TOKENS, HEADS * HD), jnp.float32)
    return drawn_noise.astype(jnp.bfloat16)


def block_levels(own_key, extent, pieces, least, largest):
    level = 1.0
    for position, blocks in pieces:
        heights = jax.random.uniform(jax.random.fold_in(jax.random.fold_in(own_key, 6), position), (blocks,), jnp.float32, least / len(pieces), largest / len(pieces))
        level = level * jnp.repeat(jnp.exp(heights), extent[position] // blocks).reshape((-1,) + (1,) * (len(extent) - 1 - position))
    return level


def shared_out(stream_key, own, number, rows, number_of, top, most, skew):
    ranking = jax.random.permutation(stream_key, number_of)
    packed, common = shares(number_of, rows * top, most, skew, True), shares(number_of, rows * top, most, skew, False)
    places = jnp.arange(number_of)

    def named(lengths, offset_by):
        used = int((lengths > 0).sum())
        fixed = max(1, used // 4)
        passed = fixed + (places - fixed + offset_by * (used - fixed)) % max(1, number_of - fixed)
        return jnp.zeros((number_of,), jnp.int32).at[ranking[jnp.where(places < fixed, places, passed)]].set(jnp.asarray(lengths, jnp.int32))

    lengths = jnp.where(number % 4 == 0, named(packed, number // 4), named(common, number - number // 4 - 1))
    mixed = jax.random.permutation(jax.random.fold_in(own, 3), number_of)
    source_of, sink = mixed[0:number_of // 2 * 2:2], mixed[1:number_of // 2 * 2:2]
    slack = jnp.minimum(lengths[source_of] - 1, most - lengths[sink]) // 2
    slack = jnp.where((source_of == ranking[0]) | (sink == ranking[0]) | (lengths[sink] == 0), 0, jnp.maximum(slack, 0))
    passed = jax.random.randint(jax.random.fold_in(own, 4), (number_of // 2,), 0, 1 << 20) % (slack + 1)
    lengths = lengths.at[source_of].add(-passed).at[sink].add(passed)
    members = jnp.searchsorted(jnp.cumsum(lengths), jnp.arange(rows * top), side="right").astype(jnp.int32)
    listing = members.reshape(top, rows).T
    listing = listing[jax.random.permutation(jax.random.fold_in(own, 1), rows)]
    offset_by = jax.random.randint(jax.random.fold_in(own, 2), (rows, 1), 0, top)
    return jnp.take_along_axis(listing, (jnp.arange(top)[None, :] + offset_by) % top, axis=1)


def shares(count, total, most, slope, full):
    weights = [(1 << 20) // math.isqrt(grade ** slope) + 1 for grade in range(1, count + 1)]
    largest = most if full else min(most, max(-(-total // count), total * weights[0] // sum(weights)))
    least = 1 if total - largest >= count - 1 else 0
    counts, surplus = [largest] + [least] * (count - 1), total - largest - least * (count - 1)
    while surplus > 0:
        candidates = [i for i in range(1, count) if counts[i] < largest] or [i for i in range(1, count) if counts[i] < most]
        whole, remaining = sum([weights[i] for i in candidates]), surplus
        for i in candidates:
            extra = min(most - counts[i], max(1, remaining * weights[i] // whole), surplus)
            counts[i] = counts[i] + extra
            surplus = surplus - extra
    return np.array(counts)


def noise(stream_key, shape, scale, limit, pieces=(), held_as=jnp.bfloat16):
    result = scale * jax.random.normal(stream_key, shape, jnp.float32)
    if pieces:
        result = result * block_levels(stream_key, shape, pieces, -0.22, 0.18)
    return jnp.clip(result, -limit, limit).astype(held_as)


def setup_inputs(seed: int = 0) -> dict:
    key_of = jax.random.split(jax.random.key(seed), 8)
    queries = draw_queries(jax.random.fold_in(key_of[7], 71), 0)
    keys = draw_keys(jax.random.fold_in(key_of[7], 71), 0)
    values = noise(key_of[2], (TOKENS, KV_HEADS * HD), 4.0, 24.0, ((0, 64), (1, 4)))
    out_weight = noise(key_of[3], (HEADS * HD, WIDTH), (HEADS * HD) ** -0.5, 0.09375, ((0, 4),))
    residual = noise(key_of[4], (TOKENS, WIDTH), 0.25, 1.5, ((0, 64), (1, 4)))
    span_of_section = jax.random.permutation(key_of[5], N_SECTION).astype(jnp.int32)
    page_owner_keys = jax.random.split(jax.random.fold_in(key_of[6], 1), N_SECTION * KV_HEADS * PPH // PPD)
    page_owner_turns = jax.random.permutation(jax.random.fold_in(key_of[6], 3), N_SECTION * KV_HEADS * PPH // PPD)
    page_owner = jax.vmap(lambda own, number: shared_out(jax.random.fold_in(key_of[6], 2), own, number, PPD, N_SECTION, 1, MOST, 2))(page_owner_keys, page_owner_turns).reshape((N_SECTION, KV_HEADS, PPH, 1))
    return {"queries": queries, "keys": keys, "values": values, "out_weight": out_weight, "residual": residual, "span_of_section": span_of_section, "page_owner": page_owner}


FLOOR = -1e+30

def reference(queries, keys, values, out_weight, residual, span_of_section, page_owner):
    offsets = jnp.arange(SPAN, dtype=jnp.int32)
    positions = (span_of_section[:, None] * SPAN + offsets[None, :]).reshape(TOKENS).astype(jnp.int32)
    score_scale = 1.0 / math.sqrt(HD)

    def one_head(flat_index):
        section_id = (flat_index // KV_HEADS).astype(jnp.int32)
        head_id = (flat_index % KV_HEADS).astype(jnp.int32)
        query_block = lax.dynamic_slice(queries, (section_id * SPAN, head_id * (GROUP * HD)), (SPAN, GROUP * HD))
        query_block = query_block.astype(jnp.float32).reshape(SPAN, GROUP, HD)
        key_head = lax.dynamic_slice(keys, (jnp.int32(0), head_id * HD), (TOKENS, HD)).astype(jnp.float32)
        value_head = lax.dynamic_slice(values, (jnp.int32(0), head_id * HD), (TOKENS, HD)).astype(jnp.float32)
        query_pos = lax.dynamic_slice_in_dim(positions, section_id * SPAN, SPAN)
        scores = jnp.einsum('qgd,kd->qgk', query_block, key_head) * score_scale
        visible = (positions[None, :] <= query_pos[:, None])[:, None, :]
        scores = jnp.where(visible, scores, FLOOR)
        peak_score = lax.optimization_barrier(jnp.max(scores, axis=-1, keepdims=True))
        weights = jnp.where(visible, jnp.exp(scores - peak_score), 0.0)
        total_weight = lax.optimization_barrier(jnp.sum(weights, axis=-1, keepdims=True))
        rounded = lax.optimization_barrier(weights.astype(jnp.bfloat16)).astype(jnp.float32)
        return (jnp.einsum('qgk,kd->qgd', rounded, value_head) / total_weight).astype(jnp.bfloat16)
    stacked = lax.map(one_head, jnp.arange(N_SECTION * KV_HEADS, dtype=jnp.int32))
    attended = stacked.reshape(N_SECTION, KV_HEADS, SPAN, GROUP, HD).transpose(0, 2, 1, 3, 4).reshape(TOKENS, HEADS * HD)
    projected = jnp.dot(attended, out_weight, preferred_element_type=jnp.float32)
    updated = (residual.astype(jnp.float32) + projected).astype(jnp.bfloat16)
    key_pages = keys.reshape(N_SECTION, PPH, PAGE_TOK, KV_HEADS, HD).transpose(0, 3, 1, 2, 4)
    value_pages = values.reshape(N_SECTION, PPH, PAGE_TOK, KV_HEADS, HD).transpose(0, 3, 1, 2, 4)
    page_data = jnp.concatenate([key_pages, value_pages], axis=-1).reshape(N_SECTION, N_TENSOR, HPT * PPH, PAGE_TOK, 2 * HD)
    owners = page_owner.reshape(N_SECTION, N_TENSOR, HPT * PPH).astype(jnp.int32)
    dest_hits = (owners[..., None] == jnp.arange(N_SECTION, dtype=jnp.int32)).astype(jnp.int32)
    earlier = jnp.cumsum(dest_hits, axis=2) - dest_hits
    slot_rank = lax.optimization_barrier(jnp.sum(earlier * dest_hits, axis=-1)).astype(jnp.int32)
    sender = jnp.broadcast_to(jnp.arange(N_SECTION, dtype=jnp.int32)[:, None, None], owners.shape)
    tensor_group = jnp.broadcast_to(jnp.arange(N_TENSOR, dtype=jnp.int32)[None, :, None], owners.shape)
    kv_cache = jnp.zeros((N_SECTION, N_TENSOR, N_SECTION, MOST, PAGE_TOK, 2 * HD), jnp.bfloat16)
    kv_cache = kv_cache.at[owners, tensor_group, sender, slot_rank].set(page_data)
    return (updated, kv_cache)
```

```python
import functools
import math

import jax
import jax.numpy as jnp
from jax import lax
from jax.experimental import pallas as pl
from jax.experimental.pallas import tpu as pltpu
from jax.sharding import PartitionSpec as P

HD = 128
GROUP = 8
SPAN = 256
UNIT = 128
PAGE_TOK = 8
PPH = 32
XS, ZS = 4, 8
SCALE2 = math.log2(math.e) / math.sqrt(HD)
FLOOR = -1e30
LIMIT = 1e30
F32, BF16 = jnp.float32, jnp.bfloat16
NT = (((1,), (1,)), ((), ()))
VMEM = pl.BlockSpec(memory_space=pltpu.VMEM)
SMEM = pl.BlockSpec(memory_space=pltpu.SMEM)
ANY = pl.BlockSpec(memory_space=pl.ANY)


def params(mib):
    return pltpu.CompilerParams(vmem_limit_bytes=mib * 2**20)


def section_at(x, z, core):
    return ((x % XS) * ZS + z % ZS) * 2 + core


def shift(a, dx=0, dz=0):
    pairs = [
        (section_at(x, z, c), section_at(x + dx, z + dz, c))
        for x in range(XS)
        for z in range(ZS)
        for c in range(2)
    ]
    return lax.ppermute(a, "section", pairs)


def swap_core(a):
    return lax.ppermute(a, "section", [(s, s ^ 1) for s in range(XS * ZS * 2)])


def turn(a, d):
    n = lax.axis_size("tensor")
    return lax.ppermute(a, "tensor", [(t, (t + d) % n) for t in range(n)])


def gather_pieces(half_a, half_b):
    rows = lambda units: [slice(i * UNIT, (i + 1) * UNIT) for i in range(units)]
    ax = [half_a, shift(half_a, dx=1), shift(half_a, dx=-1), shift(half_a, dx=2)]
    a0 = jnp.concatenate(ax, axis=0)
    a_offsets = [(0, 0), (-1, 0), (1, 0), (2, 0)]
    at = lambda offsets, dx, dz, half: [(ox + dx, oz + dz, half) for ox, oz in offsets]
    up, down = [half_b], [half_b]
    for _ in range(3):
        up.append(shift(up[-1], dz=1))
        down.append(shift(down[-1], dz=-1))
    far = shift(up[-1], dz=1)
    b0 = jnp.concatenate(up + down[1:] + [far], axis=0)
    b_offsets = [(0, -i) for i in range(4)] + [(0, i) for i in range(1, 4)] + [(0, 4)]
    az_up, az_down = [a0], [a0]
    for _ in range(3):
        az_up.append(shift(az_up[-1], dz=1))
        az_down.append(shift(az_down[-1], dz=-1))
    mid = a0.shape[0] // 2
    az_far = [shift(az_up[3][:mid], dz=1), shift(az_down[3][mid:], dz=-1)]
    bx_up, bx_down = shift(b0, dx=1), shift(b0, dx=-1)
    midb = b0.shape[0] // 2
    bx_far = [shift(bx_up[:midb], dx=1), shift(bx_down[midb:], dx=-1)]
    groups = [
        [(a0, at(a_offsets, 0, 0, 0))],
        [(az_up[1], at(a_offsets, 0, -1, 0)), (az_down[1], at(a_offsets, 0, 1, 0))],
        [(b0, at(b_offsets, 0, 0, 1))],
        [(az_up[2], at(a_offsets, 0, -2, 0)), (az_down[2], at(a_offsets, 0, 2, 0))],
        [(az_up[3], at(a_offsets, 0, -3, 0)), (az_down[3], at(a_offsets, 0, 3, 0))],
        [(bx_up, at(b_offsets, -1, 0, 1)), (bx_down, at(b_offsets, 1, 0, 1))],
        [
            (az_far[0], at(a_offsets[:2], 0, 4, 0)),
            (az_far[1], at(a_offsets[2:], 0, 4, 0)),
            (bx_far[0], at(b_offsets[:4], 2, 0, 1)),
            (bx_far[1], at(b_offsets[4:], 2, 0, 1)),
        ],
    ]
    return groups


def head_column(m, h):
    lane = lax.broadcasted_iota(jnp.int32, m.shape, 1)
    return jnp.sum(jnp.where(lane == h, m, 0.0), axis=1, keepdims=True)


def own_kernel(q, kv, m_out, acc):
    row = lax.broadcasted_iota(jnp.int32, (SPAN, SPAN), 0)
    col = lax.broadcasted_iota(jnp.int32, (SPAN, SPAN), 1)
    seen = col <= row
    lane = lax.broadcasted_iota(jnp.int32, (SPAN, HD), 1)
    key = kv[:, :HD]
    wide = jnp.concatenate([kv[:, HD:], jnp.ones((SPAN, HD), BF16)], axis=1)
    m = jnp.zeros((SPAN, HD), F32)
    for h in range(GROUP):
        s = lax.dot_general(q[:, h * HD : (h + 1) * HD], key, NT, preferred_element_type=F32)
        s = jnp.where(seen, s * SCALE2, FLOOR)
        peak = jnp.max(s, axis=1, keepdims=True)
        p = jnp.exp2(s - peak).astype(BF16)
        acc[h] = jnp.dot(p, wide, preferred_element_type=F32)
        m = jnp.where(lane == h, peak, m)
    m_out[...] = m


def attend_own(q, kv):
    return pl.pallas_call(
        own_kernel,
        in_specs=[VMEM, VMEM],
        out_specs=[VMEM, VMEM],
        out_shape=[
            jax.ShapeDtypeStruct((SPAN, HD), F32),
            jax.ShapeDtypeStruct((GROUP, SPAN, 2 * HD), F32),
        ],
        cost_estimate=pl.CostEstimate(
            flops=8 * GROUP * SPAN * SPAN * HD, bytes_accessed=2**22, transcendentals=GROUP * SPAN * SPAN
        ),
        compiler_params=params(16),
        name="own_span",
    )(q, kv)


def pieces_kernel(sizes, first_unit, step, vis, *refs):
    count = len(sizes)
    chunks = refs[:count]
    q, m, acc_in, acc, ks, vs = refs[count:]
    total = sum(sizes)
    row = 0
    for ref, n in zip(chunks, sizes):
        ks[row : row + n, :] = ref[:, :HD]
        for j in range(0, n, UNIT):
            keep = vis[first_unit + (row + j) // UNIT] > 0
            value = ref[j : j + UNIT, HD:]
            vs[row + j : row + j + UNIT, :HD] = jnp.where(keep, value, jnp.zeros_like(value))
            vs[row + j : row + j + UNIT, HD:] = jnp.full((UNIT, HD), keep.astype(F32)).astype(BF16)
        row += n
    for lo in range(0, total, step):
        n = min(step, total - lo)
        some = vis[first_unit + lo // UNIT]
        for u in range(lo // UNIT + 1, (lo + n) // UNIT):
            some = some + vis[first_unit + u]
        source = acc_in if lo == 0 else acc

        @pl.when(some > 0)
        def _():
            for h in range(GROUP):
                s = lax.dot_general(
                    q[:, h * HD : (h + 1) * HD], ks[lo : lo + n, :], NT, preferred_element_type=F32
                )
                p = jnp.exp2(s * SCALE2 - head_column(m[...], h)).astype(BF16)
                acc[h] = source[h] + jnp.dot(p, vs[lo : lo + n, :], preferred_element_type=F32)

        if lo == 0:

            @pl.when(some == 0)
            def _():
                acc[...] = acc_in[...]


def attend_pieces(chunks, first_unit, vis, q, m, acc):
    sizes = [c.shape[0] for c in chunks]
    total = sum(sizes)
    return pl.pallas_call(
        functools.partial(pieces_kernel, sizes, first_unit, 2048),
        in_specs=[SMEM] + [VMEM] * (len(chunks) + 3),
        out_specs=VMEM,
        out_shape=jax.ShapeDtypeStruct(acc.shape, F32),
        scratch_shapes=[pltpu.VMEM((total, HD), BF16), pltpu.VMEM((total, 2 * HD), BF16)],
        input_output_aliases={len(chunks) + 3: 0},
        cost_estimate=pl.CostEstimate(
            flops=8 * GROUP * SPAN * total * HD,
            bytes_accessed=total * 512 + 2**22,
            transcendentals=GROUP * SPAN * total,
        ),
        compiler_params=params(24),
        name="attend_pieces",
    )(vis, *chunks, q, m, acc)


def online_step(h, q, key, value, seen, acc, m):
    s = lax.dot_general(
        q[:, pl.ds(pl.multiple_of(h * HD, HD), HD)], key, NT, preferred_element_type=F32
    )
    s = s * SCALE2
    if seen is not None:
        s = jnp.where(seen, s, FLOOR)
    before = m[h]
    peak = jnp.maximum(before, jnp.max(s, axis=1, keepdims=True))
    p = jnp.exp2(s - peak[:, :1]).astype(BF16)
    if seen is not None:
        p = jnp.where(seen, p, jnp.zeros_like(p))
    fade = jnp.exp2(before - peak)
    wide = jnp.concatenate([value, jnp.ones(value.shape, BF16)], axis=1)
    acc[h] = acc[h] * jnp.concatenate([fade, fade], axis=1) + jnp.dot(p, wide, preferred_element_type=F32)
    m[h] = peak


def project_columns(attended, weight, dest):
    cols = weight[:, pl.ds(pl.multiple_of(dest * 1024, 1024), 1024)]
    return jnp.dot(attended, cols, preferred_element_type=F32)


def finish_kernel(sizes, vis, where, *refs):
    count = len(sizes)
    chunks = refs[:count]
    q, kv, acc, weight, attended, far_a, far_b, safe, peak, block, sem = refs[count:]
    worst = jnp.max(jnp.maximum(jnp.max(acc[:, :, HD:], axis=0), 0.0))
    worst = jnp.where(worst < LIMIT, 0, 1)

    @pl.when(worst == 0)
    def _():
        for h in range(GROUP):
            attended[:, h * HD : (h + 1) * HD] = (acc[h, :, :HD] / acc[h, :, HD:]).astype(BF16)

    @pl.when(worst != 0)
    def _():
        safe[...] = jnp.zeros_like(safe)
        peak[...] = jnp.full_like(peak, FLOOR)
        row = lax.broadcasted_iota(jnp.int32, (SPAN, SPAN), 0)
        col = lax.broadcasted_iota(jnp.int32, (SPAN, SPAN), 1)

        @pl.loop(0, GROUP)
        def _(h):
            online_step(h, q, kv[:, :HD], kv[:, HD:], col <= row, safe, peak)

        first = 0
        for ref, n in zip(chunks, sizes):

            @pl.loop(0, n // UNIT)
            def _(u):
                @pl.when(vis[first + u] > 0)
                def _():
                    copy = pltpu.make_async_copy(
                        ref.at[pl.ds(pl.multiple_of(u * UNIT, UNIT), UNIT), :], block, sem
                    )
                    copy.start()
                    copy.wait()

                    @pl.loop(0, GROUP)
                    def _(h):
                        online_step(h, q, block[:, :HD], block[:, HD:], None, safe, peak)

            first += n // UNIT
        for h in range(GROUP):
            attended[:, h * HD : (h + 1) * HD] = (safe[h, :, :HD] / safe[h, :, HD:]).astype(BF16)

    far = project_columns(attended[...], weight, where[1]).astype(BF16)
    far_a[...] = far[: SPAN // 2]
    far_b[...] = far[SPAN // 2 :]


def finish(chunks, vis, where, q, kv, acc, weight):
    sizes = [c.shape[0] for c in chunks]
    part = jax.ShapeDtypeStruct((SPAN // 2, 1024), BF16)
    return pl.pallas_call(
        functools.partial(finish_kernel, sizes),
        in_specs=[SMEM, SMEM] + [ANY] * len(chunks) + [VMEM] * 4,
        out_specs=[VMEM] * 3,
        out_shape=[jax.ShapeDtypeStruct((SPAN, 1024), BF16), part, part],
        scratch_shapes=[
            pltpu.VMEM((GROUP, SPAN, 2 * HD), F32),
            pltpu.VMEM((GROUP, SPAN, HD), F32),
            pltpu.VMEM((UNIT, 2 * HD), BF16),
            pltpu.SemaphoreType.DMA,
        ],
        cost_estimate=pl.CostEstimate(flops=2 * SPAN * 1024 * 1024, bytes_accessed=2**22, transcendentals=0),
        compiler_params=params(24),
        name="finish",
    )(vis, where, *chunks, q, kv, acc, weight)


def near_kernel(where, attended, weight, residual, up_a, up_b, down_a, down_b, mine):
    half = SPAN // 2
    up = project_columns(attended[...], weight, where[2]).astype(BF16)
    up_a[...] = up[:half]
    up_b[...] = up[half:]
    down = project_columns(attended[...], weight, where[3]).astype(BF16)
    down_a[...] = down[:half]
    down_b[...] = down[half:]
    mine[...] = project_columns(attended[...], weight, where[0]) + residual[...].astype(F32)


def project_near(where, attended, weight, residual):
    part = jax.ShapeDtypeStruct((SPAN // 2, 1024), BF16)
    return pl.pallas_call(
        near_kernel,
        in_specs=[SMEM] + [VMEM] * 3,
        out_specs=[VMEM] * 5,
        out_shape=[part] * 4 + [jax.ShapeDtypeStruct((SPAN, 1024), F32)],
        cost_estimate=pl.CostEstimate(flops=6 * SPAN * 1024 * 1024, bytes_accessed=2**23, transcendentals=0),
        compiler_params=params(24),
        name="project_near",
    )(where, attended, weight, residual)


def pages_kernel(layout, pages, sections, *refs):
    chunks, out = refs[:-1], refs[-1]
    rows = lax.broadcasted_iota(jnp.int32, (2 * PAGE_TOK, 2 * HD), 0)
    for place, ((ref_a, row_a), (ref_b, row_b)) in enumerate(layout):
        s = sections[place]
        found = []
        for rank in range(2):
            page = pages[rank, s]
            pair = pl.multiple_of((jnp.maximum(page, 0) % 16) // 2 * 16, 16)
            in_a = chunks[ref_a][pl.ds(row_a + pair, 16), :]
            in_b = chunks[ref_b][pl.ds(row_b + pair, 16), :]
            both = jnp.where(page < 16, in_a.astype(F32), in_b.astype(F32))
            one = jnp.where(page % 2 == 0, both[:PAGE_TOK], both[PAGE_TOK:])
            found.append(jnp.where(page >= 0, one, 0.0))
        out[pl.ds(pl.multiple_of(s * 16, 16), 16), :] = jnp.concatenate(found, axis=0).astype(BF16)


def take_pages(layout, pages, sections, chunks):
    return pl.pallas_call(
        functools.partial(pages_kernel, layout),
        in_specs=[SMEM, SMEM] + [VMEM] * len(chunks),
        out_specs=VMEM,
        out_shape=jax.ShapeDtypeStruct((2 * XS * ZS * 2 * PAGE_TOK, 2 * HD), BF16),
        cost_estimate=pl.CostEstimate(flops=2**20, bytes_accessed=2**23, transcendentals=0),
        compiler_params=params(16),
        name="take_pages",
    )(pages, sections, *chunks)


def local(queries, keys, values, out_weight, residual, span_of_section, page_owner):
    me = lax.axis_index("section")
    t = lax.axis_index("tensor")
    sections = lax.axis_size("section")
    tensors = lax.axis_size("tensor")
    kv = jnp.concatenate([keys, values], axis=1)

    groups = gather_pieces(kv[:UNIT], kv[UNIT:])
    groups = [
        [
            item
            for piece, offsets in group
            for item in (
                (piece, [o + (0,) for o in offsets]),
                (swap_core(piece), [o + (1,) for o in offsets]),
            )
        ]
        for group in groups
    ]
    units = [o for group in groups for _, offsets in group for o in offsets]
    place = {}
    chunks = [piece for group in groups for piece, _ in group]
    for number, (piece, offsets) in enumerate(item for group in groups for item in group):
        for i, (dx, dz, half, core) in enumerate(offsets):
            place[(dx % XS, dz % ZS, core, half)] = (number, i * UNIT)
    relative = [(dx, dz, core) for dx in range(XS) for dz in range(ZS) for core in range(2)]
    layout = [(place[r + (0,)], place[r + (1,)]) for r in relative]

    x, z, core = me // (2 * ZS), (me // 2) % ZS, me % 2

    def ids(table):
        dx, dz, dc = (jnp.array(column, jnp.int32) for column in zip(*table))
        return ((x + dx) % XS * ZS + (z + dz) % ZS) * 2 + (core ^ dc)

    ids_units = ids([(dx, dz, c) for dx, dz, _, c in units])
    ids_relative = ids(relative)
    section_ids = jnp.arange(sections, dtype=jnp.int32)
    my_span = jnp.sum(jnp.where(section_ids == me, span_of_section, 0))
    unit_spans = jnp.sum(
        jnp.where(ids_units[:, None] == section_ids[None, :], span_of_section[None, :], 0), axis=1
    )
    vis = (unit_spans < my_span).astype(jnp.int32)
    where = (t + jnp.array([0, 2, 1, 3], jnp.int32)) % tensors
    owners = page_owner.reshape(sections, PPH)
    page_ids = jnp.arange(PPH, dtype=jnp.int32)[None, :]
    mine = owners == me
    first_page = jnp.min(jnp.where(mine, page_ids, PPH), axis=1)
    last_page = jnp.max(jnp.where(mine, page_ids, -1), axis=1)
    pages = jnp.stack(
        [
            jnp.where(first_page < PPH, first_page, -1),
            jnp.where(last_page > first_page, last_page, -1),
        ]
    )

    m, acc = attend_own(queries, kv)
    first_unit = 0
    for group in groups:
        arrays = [piece for piece, _ in group]
        acc = attend_pieces(arrays, first_unit, vis, queries, m, acc)
        first_unit += sum(a.shape[0] for a in arrays) // UNIT

    attended, far_a, far_b = finish(chunks, vis, where, queries, kv, acc, out_weight)
    relay_a, relay_b = turn(far_a, 1), turn(far_b, -1)
    up_a, up_b, down_a, down_b, own_sum = project_near(where, attended, out_weight, residual)
    from_below_b, from_above_a = turn(up_b, 1), turn(down_a, -1)
    from_below_a = turn((up_a.astype(F32) + relay_a.astype(F32)).astype(BF16), 1)
    from_above_b = turn((down_b.astype(F32) + relay_b.astype(F32)).astype(BF16), -1)
    below = jnp.concatenate([from_below_a, from_below_b], axis=0).astype(F32)
    above = jnp.concatenate([from_above_a, from_above_b], axis=0).astype(F32)
    updated = (own_sum + below + above).astype(BF16)

    cache = take_pages(layout, pages, ids_relative, chunks)
    kv_cache = cache.reshape(1, 1, sections, 2, PAGE_TOK, 2 * HD)
    return (updated, kv_cache)


def solution(mesh):
    return jax.shard_map(
        local,
        mesh=mesh,
        in_specs=(
            P("section", "tensor"),
            P("section", "tensor"),
            P("section", "tensor"),
            P("tensor", None),
            P("section", "tensor"),
            P(),
            P(None, "tensor", None, None),
        ),
        out_specs=(P("section", "tensor"), P("section", "tensor", None, None, None, None)),
        check_vma=False,
    )
```

```python
import functools
import math

import jax
import jax.numpy as jnp
from jax import lax
from jax.experimental import pallas as pl
from jax.experimental.pallas import tpu as pltpu
from jax.sharding import PartitionSpec as P

HD = 128
GROUP = 8
SPAN = 256
UNIT = 128
PAGE_TOK = 8
PPH = 32
XS, ZS = 4, 8
SCALE2 = math.log2(math.e) / math.sqrt(HD)
FLOOR = -1e30
LIMIT = 1e30
F32, BF16 = jnp.float32, jnp.bfloat16
NT = (((1,), (1,)), ((), ()))
VMEM = pl.BlockSpec(memory_space=pltpu.VMEM)
SMEM = pl.BlockSpec(memory_space=pltpu.SMEM)
ANY = pl.BlockSpec(memory_space=pl.ANY)


def params(mib):
    return pltpu.CompilerParams(vmem_limit_bytes=mib * 2**20)


def section_at(x, z, core):
    return ((x % XS) * ZS + z % ZS) * 2 + core


def shift(a, dx=0, dz=0):
    pairs = [
        (section_at(x, z, c), section_at(x + dx, z + dz, c))
        for x in range(XS)
        for z in range(ZS)
        for c in range(2)
    ]
    return lax.ppermute(a, "section", pairs)


def swap_core(a):
    return lax.ppermute(a, "section", [(s, s ^ 1) for s in range(XS * ZS * 2)])


def turn(a, d):
    n = lax.axis_size("tensor")
    return lax.ppermute(a, "tensor", [(t, (t + d) % n) for t in range(n)])


def head_column(m, h):
    lane = lax.broadcasted_iota(jnp.int32, m.shape, 1)
    return jnp.sum(jnp.where(lane == h, m, 0.0), axis=1, keepdims=True)


def own_kernel(q, kv, m_out, acc):
    row = lax.broadcasted_iota(jnp.int32, (SPAN, SPAN), 0)
    col = lax.broadcasted_iota(jnp.int32, (SPAN, SPAN), 1)
    seen = col <= row
    lane = lax.broadcasted_iota(jnp.int32, (SPAN, HD), 1)
    key = kv[:, :HD]
    wide = jnp.concatenate([kv[:, HD:], jnp.ones((SPAN, HD), BF16)], axis=1)
    m = jnp.zeros((SPAN, HD), F32)
    for h in range(GROUP):
        s = lax.dot_general(q[:, h * HD : (h + 1) * HD], key, NT, preferred_element_type=F32)
        s = jnp.where(seen, s * SCALE2, FLOOR)
        peak = jnp.max(s, axis=1, keepdims=True)
        p = jnp.exp2(s - peak).astype(BF16)
        acc[h] = jnp.dot(p, wide, preferred_element_type=F32)
        m = jnp.where(lane == h, peak, m)
    m_out[...] = m


def attend_own(q, kv):
    return pl.pallas_call(
        own_kernel,
        in_specs=[VMEM, VMEM],
        out_specs=[VMEM, VMEM],
        out_shape=[
            jax.ShapeDtypeStruct((SPAN, HD), F32),
            jax.ShapeDtypeStruct((GROUP, SPAN, 2 * HD), F32),
        ],
        cost_estimate=pl.CostEstimate(
            flops=8 * GROUP * SPAN * SPAN * HD, bytes_accessed=2**22, transcendentals=GROUP * SPAN * SPAN
        ),
        compiler_params=params(16),
        name="own_span",
    )(q, kv)


def pieces_kernel(sizes, first_unit, step, vis, *refs):
    count = len(sizes)
    chunks = refs[:count]
    q, m, acc_in, acc, ks, vs = refs[count:]
    total = sum(sizes)
    row = 0
    for ref, n in zip(chunks, sizes):
        ks[row : row + n, :] = ref[:, :HD]
        for j in range(0, n, UNIT):
            keep = vis[first_unit + (row + j) // UNIT] > 0
            value = ref[j : j + UNIT, HD:]
            vs[row + j : row + j + UNIT, :HD] = jnp.where(keep, value, jnp.zeros_like(value))
            vs[row + j : row + j + UNIT, HD:] = jnp.full((UNIT, HD), keep.astype(F32)).astype(BF16)
        row += n
    for lo in range(0, total, step):
        n = min(step, total - lo)
        some = vis[first_unit + lo // UNIT]
        for u in range(lo // UNIT + 1, (lo + n) // UNIT):
            some = some + vis[first_unit + u]
        source = acc_in if lo == 0 else acc

        @pl.when(some > 0)
        def _():
            for h in range(GROUP):
                s = lax.dot_general(
                    q[:, h * HD : (h + 1) * HD], ks[lo : lo + n, :], NT, preferred_element_type=F32
                )
                p = jnp.exp2(s * SCALE2 - head_column(m[...], h)).astype(BF16)
                acc[h] = source[h] + jnp.dot(p, vs[lo : lo + n, :], preferred_element_type=F32)

        if lo == 0:

            @pl.when(some == 0)
            def _():
                acc[...] = acc_in[...]


def attend_pieces(chunks, first_unit, vis, q, m, acc):
    sizes = [c.shape[0] for c in chunks]
    total = sum(sizes)
    return pl.pallas_call(
        functools.partial(pieces_kernel, sizes, first_unit, 2048),
        in_specs=[SMEM] + [VMEM] * (len(chunks) + 3),
        out_specs=VMEM,
        out_shape=jax.ShapeDtypeStruct(acc.shape, F32),
        scratch_shapes=[pltpu.VMEM((total, HD), BF16), pltpu.VMEM((total, 2 * HD), BF16)],
        input_output_aliases={len(chunks) + 3: 0},
        cost_estimate=pl.CostEstimate(
            flops=8 * GROUP * SPAN * total * HD,
            bytes_accessed=total * 512 + 2**22,
            transcendentals=GROUP * SPAN * total,
        ),
        compiler_params=params(24),
        name="attend_pieces",
    )(vis, *chunks, q, m, acc)


def online_step(h, q, key, value, seen, acc, m):
    s = lax.dot_general(
        q[:, pl.ds(pl.multiple_of(h * HD, HD), HD)], key, NT, preferred_element_type=F32
    )
    s = s * SCALE2
    if seen is not None:
        s = jnp.where(seen, s, FLOOR)
    before = m[h]
    peak = jnp.maximum(before, jnp.max(s, axis=1, keepdims=True))
    p = jnp.exp2(s - peak[:, :1]).astype(BF16)
    if seen is not None:
        p = jnp.where(seen, p, jnp.zeros_like(p))
    fade = jnp.exp2(before - peak)
    wide = jnp.concatenate([value, jnp.ones(value.shape, BF16)], axis=1)
    acc[h] = acc[h] * jnp.concatenate([fade, fade], axis=1) + jnp.dot(p, wide, preferred_element_type=F32)
    m[h] = peak


def project_columns(attended, weight, dest):
    cols = weight[:, pl.ds(pl.multiple_of(dest * 1024, 1024), 1024)]
    return jnp.dot(attended, cols, preferred_element_type=F32)


def finish_kernel(sizes, vis, where, *refs):
    count = len(sizes)
    chunks = refs[:count]
    q, kv, acc, weight, attended, far_a, far_b, safe, peak, block, sem = refs[count:]
    worst = jnp.max(jnp.maximum(jnp.max(acc[:, :, HD:], axis=0), 0.0))
    worst = jnp.where(worst < LIMIT, 0, 1)

    @pl.when(worst == 0)
    def _():
        for h in range(GROUP):
            attended[:, h * HD : (h + 1) * HD] = (acc[h, :, :HD] / acc[h, :, HD:]).astype(BF16)

    @pl.when(worst != 0)
    def _():
        safe[...] = jnp.zeros_like(safe)
        peak[...] = jnp.full_like(peak, FLOOR)
        row = lax.broadcasted_iota(jnp.int32, (SPAN, SPAN), 0)
        col = lax.broadcasted_iota(jnp.int32, (SPAN, SPAN), 1)

        @pl.loop(0, GROUP)
        def _(h):
            online_step(h, q, kv[:, :HD], kv[:, HD:], col <= row, safe, peak)

        first = 0
        for ref, n in zip(chunks, sizes):

            @pl.loop(0, n // UNIT)
            def _(u):
                @pl.when(vis[first + u] > 0)
                def _():
                    copy = pltpu.make_async_copy(
                        ref.at[pl.ds(pl.multiple_of(u * UNIT, UNIT), UNIT), :], block, sem
                    )
                    copy.start()
                    copy.wait()

                    @pl.loop(0, GROUP)
                    def _(h):
                        online_step(h, q, block[:, :HD], block[:, HD:], None, safe, peak)

            first += n // UNIT
        for h in range(GROUP):
            attended[:, h * HD : (h + 1) * HD] = (safe[h, :, :HD] / safe[h, :, HD:]).astype(BF16)

    far = project_columns(attended[...], weight, where[1]).astype(BF16)
    far_a[...] = far[: SPAN // 2]
    far_b[...] = far[SPAN // 2 :]


def finish(chunks, vis, where, q, kv, acc, weight):
    sizes = [c.shape[0] for c in chunks]
    part = jax.ShapeDtypeStruct((SPAN // 2, 1024), BF16)
    return pl.pallas_call(
        functools.partial(finish_kernel, sizes),
        in_specs=[SMEM, SMEM] + [ANY] * len(chunks) + [VMEM] * 4,
        out_specs=[VMEM] * 3,
        out_shape=[jax.ShapeDtypeStruct((SPAN, 1024), BF16), part, part],
        scratch_shapes=[
            pltpu.VMEM((GROUP, SPAN, 2 * HD), F32),
            pltpu.VMEM((GROUP, SPAN, HD), F32),
            pltpu.VMEM((UNIT, 2 * HD), BF16),
            pltpu.SemaphoreType.DMA,
        ],
        cost_estimate=pl.CostEstimate(flops=2 * SPAN * 1024 * 1024, bytes_accessed=2**22, transcendentals=0),
        compiler_params=params(24),
        name="finish",
    )(vis, where, *chunks, q, kv, acc, weight)


def near_kernel(where, attended, weight, residual, up_a, up_b, down_a, down_b, mine):
    half = SPAN // 2
    up = project_columns(attended[...], weight, where[2]).astype(BF16)
    up_a[...] = up[:half]
    up_b[...] = up[half:]
    down = project_columns(attended[...], weight, where[3]).astype(BF16)
    down_a[...] = down[:half]
    down_b[...] = down[half:]
    mine[...] = project_columns(attended[...], weight, where[0]) + residual[...].astype(F32)


def project_near(where, attended, weight, residual):
    part = jax.ShapeDtypeStruct((SPAN // 2, 1024), BF16)
    return pl.pallas_call(
        near_kernel,
        in_specs=[SMEM] + [VMEM] * 3,
        out_specs=[VMEM] * 5,
        out_shape=[part] * 4 + [jax.ShapeDtypeStruct((SPAN, 1024), F32)],
        cost_estimate=pl.CostEstimate(flops=6 * SPAN * 1024 * 1024, bytes_accessed=2**23, transcendentals=0),
        compiler_params=params(24),
        name="project_near",
    )(where, attended, weight, residual)


def pages_kernel(layout, pages, sections, *refs):
    chunks, out = refs[:-1], refs[-1]
    rows = lax.broadcasted_iota(jnp.int32, (2 * PAGE_TOK, 2 * HD), 0)
    for place, ((ref_a, row_a), (ref_b, row_b)) in enumerate(layout):
        s = sections[place]
        found = []
        for rank in range(2):
            page = pages[rank, s]
            pair = pl.multiple_of((jnp.maximum(page, 0) % 16) // 2 * 16, 16)
            in_a = chunks[ref_a][pl.ds(row_a + pair, 16), :]
            in_b = chunks[ref_b][pl.ds(row_b + pair, 16), :]
            both = jnp.where(page < 16, in_a.astype(F32), in_b.astype(F32))
            one = jnp.where(page % 2 == 0, both[:PAGE_TOK], both[PAGE_TOK:])
            found.append(jnp.where(page >= 0, one, 0.0))
        out[pl.ds(pl.multiple_of(s * 16, 16), 16), :] = jnp.concatenate(found, axis=0).astype(BF16)


def take_pages(layout, pages, sections, chunks):
    return pl.pallas_call(
        functools.partial(pages_kernel, layout),
        in_specs=[SMEM, SMEM] + [VMEM] * len(chunks),
        out_specs=VMEM,
        out_shape=jax.ShapeDtypeStruct((2 * XS * ZS * 2 * PAGE_TOK, 2 * HD), BF16),
        cost_estimate=pl.CostEstimate(flops=2**20, bytes_accessed=2**23, transcendentals=0),
        compiler_params=params(16),
        name="take_pages",
    )(pages, sections, *chunks)


def local(queries, keys, values, out_weight, residual, span_of_section, page_owner):
    me = lax.axis_index("section")
    t = lax.axis_index("tensor")
    sections = lax.axis_size("section")
    tensors = lax.axis_size("tensor")
    kv = jnp.concatenate([keys, values], axis=1)
    my_xz, core = me >> 1, me & 1
    x, z = my_xz >> 3, my_xz & 7
    near, lower, upper = (0, -1, 1, 2), (0, -1), (1, 2)
    plan = [[(near, 0, 0), (near, 0, 1)]]
    for dz in (1, 2, 3):
        plan += [[(near, -dz, core_), (near, dz, core_)] for core_ in (0, 1)]
    plan += [[(lower, 4, core_), (upper, 4, core_)] for core_ in (0, 1)]
    places = [item for call in plan for item in call]
    units = [(dx, dz, half, c) for offsets, dz, c in places for dx in offsets for half in (0, 1)]
    place = {}
    for number, (offsets, dz, c) in enumerate(places):
        for i, dx in enumerate(offsets):
            place[(dx % XS, dz % ZS, c)] = (number, i * SPAN)
    relative = [(dx, dz, c) for dx in range(XS) for dz in range(ZS) for c in range(2)]
    layout = [((place[r][0], place[r][1]), (place[r][0], place[r][1] + UNIT)) for r in relative]

    row = jnp.concatenate([kv, shift(kv, dx=1), shift(kv, dx=-1), shift(kv, dx=2)], axis=0)

    def ids(table):
        dx, dz, dc = (jnp.array(column, jnp.int32) for column in zip(*table))
        return ((((x + dx) & 3) * ZS + ((z + dz) & 7)) << 1) + (core ^ dc)

    ids_units = ids([(dx, dz, c) for dx, dz, _, c in units])
    ids_relative = ids(relative)
    section_ids = jnp.arange(sections, dtype=jnp.int32)
    my_span = jnp.sum(jnp.where(section_ids == me, span_of_section, 0))
    unit_spans = jnp.sum(
        jnp.where(ids_units[:, None] == section_ids[None, :], span_of_section[None, :], 0), axis=1
    )
    vis = (unit_spans < my_span).astype(jnp.int32)
    where = (t + jnp.array([0, 2, 1, 3], jnp.int32)) & (tensors - 1)
    owners = page_owner.reshape(sections, PPH)
    page_ids = jnp.arange(PPH, dtype=jnp.int32)[None, :]
    mine = owners == me
    first_page = jnp.min(jnp.where(mine, page_ids, PPH), axis=1)
    last_page = jnp.max(jnp.where(mine, page_ids, -1), axis=1)
    pages = jnp.stack(
        [
            jnp.where(first_page < PPH, first_page, -1),
            jnp.where(last_page > first_page, last_page, -1),
        ]
    )

    m, acc = attend_own(queries, kv)
    chunks = []

    def attend(acc, arrays):
        first_unit = sum(c.shape[0] for c in chunks) // UNIT
        chunks.extend(arrays)
        return attend_pieces(arrays, first_unit, vis, queries, m, acc)

    up, down = shift(row, dz=1), shift(row, dz=-1)
    acc = attend(acc, [row, swap_core(row)])
    for step in range(3):
        acc, up, down = lax.optimization_barrier((acc, up, down))
        pair = [up, down]
        if step < 2:
            up, down = shift(up, dz=1), shift(down, dz=-1)
        else:
            half = row.shape[0] // 2
            up, down = shift(up[:half], dz=1), shift(down[half:], dz=-1)
        swapped = [swap_core(a) for a in pair]
        acc = attend(acc, pair)
        acc = attend(acc, swapped)
    acc, up, down = lax.optimization_barrier((acc, up, down))
    swapped = [swap_core(a) for a in (up, down)]
    acc = attend(acc, [up, down])
    acc = attend(acc, swapped)

    attended, far_a, far_b = finish(chunks, vis, where, queries, kv, acc, out_weight)
    relay_a, relay_b = turn(far_a, 1), turn(far_b, -1)
    up_a, up_b, down_a, down_b, own_sum = project_near(where, attended, out_weight, residual)
    from_below_b, from_above_a = turn(up_b, 1), turn(down_a, -1)
    from_below_a = turn((up_a.astype(F32) + relay_a.astype(F32)).astype(BF16), 1)
    from_above_b = turn((down_b.astype(F32) + relay_b.astype(F32)).astype(BF16), -1)
    below = jnp.concatenate([from_below_a, from_below_b], axis=0).astype(F32)
    above = jnp.concatenate([from_above_a, from_above_b], axis=0).astype(F32)
    updated = (own_sum + below + above).astype(BF16)

    cache = take_pages(layout, pages, ids_relative, chunks)
    kv_cache = cache.reshape(1, 1, sections, 2, PAGE_TOK, 2 * HD)
    return (updated, kv_cache)


def solution(mesh):
    return jax.shard_map(
        local,
        mesh=mesh,
        in_specs=(
            P("section", "tensor"),
            P("section", "tensor"),
            P("section", "tensor"),
            P("tensor", None),
            P("section", "tensor"),
            P(),
            P(None, "tensor", None, None),
        ),
        out_specs=(P("section", "tensor"), P("section", "tensor", None, None, None, None)),
        check_vma=False,
    )
```

```python
import functools
import math

import jax
import jax.numpy as jnp
from jax import lax
from jax.experimental import pallas as pl
from jax.experimental.pallas import tpu as pltpu
from jax.sharding import PartitionSpec as P

HD = 128
GROUP = 8
SPAN = 256
UNIT = 128
PAGE_TOK = 8
PPH = 32
XS, ZS = 4, 8
SCALE2 = math.log2(math.e) / math.sqrt(HD)
FLOOR = -1e30
LIMIT = 1e30
F32, BF16 = jnp.float32, jnp.bfloat16
NT = (((1,), (1,)), ((), ()))
VMEM = pl.BlockSpec(memory_space=pltpu.VMEM)
SMEM = pl.BlockSpec(memory_space=pltpu.SMEM)
ANY = pl.BlockSpec(memory_space=pl.ANY)


def params(mib):
    return pltpu.CompilerParams(vmem_limit_bytes=mib * 2**20)


def section_at(x, z, core):
    return ((x % XS) * ZS + z % ZS) * 2 + core


def across(a):
    pairs = [
        (section_at(x, z, c), section_at(x + 2, z, c))
        for x in range(XS)
        for z in range(ZS)
        for c in range(2)
    ]
    return lax.ppermute(a, "section", pairs)


def pass_on(a, dx=0, dz=0):
    pairs = [
        (section_at(x, z, c), section_at(x + (1 - 2 * c) * dx, z + (1 - 2 * c) * dz, c))
        for x in range(XS)
        for z in range(ZS)
        for c in range(2)
    ]
    return lax.ppermute(a, "section", pairs)


def swap_core(a):
    return lax.ppermute(a, "section", [(s, s ^ 1) for s in range(XS * ZS * 2)])


def turn(a, d):
    n = lax.axis_size("tensor")
    return lax.ppermute(a, "tensor", [(t, (t + d) % n) for t in range(n)])


def head_column(m, h):
    lane = lax.broadcasted_iota(jnp.int32, m.shape, 1)
    return jnp.sum(jnp.where(lane == h, m, 0.0), axis=1, keepdims=True)


def pack_kernel(keys, values, out):
    out[:, :HD] = keys[...]
    out[:, HD:] = values[...]


def pack(keys, values):
    return pl.pallas_call(
        pack_kernel,
        in_specs=[VMEM, VMEM],
        out_specs=VMEM,
        out_shape=jax.ShapeDtypeStruct((SPAN, 2 * HD), BF16),
        compiler_params=params(4),
        name="pack",
    )(keys, values)


def own_kernel(q, kv, m_out, acc):
    row = lax.broadcasted_iota(jnp.int32, (SPAN, SPAN), 0)
    col = lax.broadcasted_iota(jnp.int32, (SPAN, SPAN), 1)
    seen = col <= row
    lane = lax.broadcasted_iota(jnp.int32, (SPAN, HD), 1)
    key = kv[:, :HD]
    wide = jnp.concatenate([kv[:, HD:], jnp.ones((SPAN, HD), BF16)], axis=1)
    m = jnp.zeros((SPAN, HD), F32)
    for h in range(GROUP):
        s = lax.dot_general(q[:, h * HD : (h + 1) * HD], key, NT, preferred_element_type=F32)
        s = jnp.where(seen, s * SCALE2, FLOOR)
        peak = jnp.max(s, axis=1, keepdims=True)
        p = jnp.exp2(s - peak).astype(BF16)
        acc[h] = jnp.dot(p, wide, preferred_element_type=F32)
        m = jnp.where(lane == h, peak, m)
    m_out[...] = m


def attend_own(q, kv):
    return pl.pallas_call(
        own_kernel,
        in_specs=[VMEM, VMEM],
        out_specs=[VMEM, VMEM],
        out_shape=[
            jax.ShapeDtypeStruct((SPAN, HD), F32),
            jax.ShapeDtypeStruct((GROUP, SPAN, 2 * HD), F32),
        ],
        cost_estimate=pl.CostEstimate(
            flops=8 * GROUP * SPAN * SPAN * HD, bytes_accessed=2**22, transcendentals=GROUP * SPAN * SPAN
        ),
        compiler_params=params(16),
        name="own_span",
    )(q, kv)


def pieces_kernel(sizes, first_unit, step, vis, *refs):
    count = len(sizes)
    chunks = refs[:count]
    q, m, acc_in, acc, ks, vs = refs[count:]
    total = sum(sizes)
    row = 0
    for ref, n in zip(chunks, sizes):
        ks[row : row + n, :] = ref[:, :HD]
        for j in range(0, n, UNIT):
            keep = vis[first_unit + (row + j) // UNIT] > 0
            value = ref[j : j + UNIT, HD:]
            vs[row + j : row + j + UNIT, :HD] = jnp.where(keep, value, jnp.zeros_like(value))
            vs[row + j : row + j + UNIT, HD:] = jnp.full((UNIT, HD), keep.astype(F32)).astype(BF16)
        row += n
    for lo in range(0, total, step):
        n = min(step, total - lo)
        some = vis[first_unit + lo // UNIT]
        for u in range(lo // UNIT + 1, (lo + n) // UNIT):
            some = some + vis[first_unit + u]
        source = acc_in if lo == 0 else acc

        @pl.when(some > 0)
        def _():
            for h in range(GROUP):
                s = lax.dot_general(
                    q[:, h * HD : (h + 1) * HD], ks[lo : lo + n, :], NT, preferred_element_type=F32
                )
                p = jnp.exp2(s * SCALE2 - head_column(m[...], h)).astype(BF16)
                acc[h] = source[h] + jnp.dot(p, vs[lo : lo + n, :], preferred_element_type=F32)

        if lo == 0:

            @pl.when(some == 0)
            def _():
                acc[...] = acc_in[...]


def attend_pieces(chunks, first_unit, vis, q, m, acc):
    sizes = [c.shape[0] for c in chunks]
    total = sum(sizes)
    return pl.pallas_call(
        functools.partial(pieces_kernel, sizes, first_unit, 2048),
        in_specs=[SMEM] + [VMEM] * (len(chunks) + 3),
        out_specs=VMEM,
        out_shape=jax.ShapeDtypeStruct(acc.shape, F32),
        scratch_shapes=[pltpu.VMEM((total, HD), BF16), pltpu.VMEM((total, 2 * HD), BF16)],
        input_output_aliases={len(chunks) + 3: 0},
        cost_estimate=pl.CostEstimate(
            flops=8 * GROUP * SPAN * total * HD,
            bytes_accessed=total * 512 + 2**22,
            transcendentals=GROUP * SPAN * total,
        ),
        compiler_params=params(24),
        name="attend_pieces",
    )(vis, *chunks, q, m, acc)


def online_step(h, q, key, value, seen, acc, m):
    s = lax.dot_general(
        q[:, pl.ds(pl.multiple_of(h * HD, HD), HD)], key, NT, preferred_element_type=F32
    )
    s = s * SCALE2
    if seen is not None:
        s = jnp.where(seen, s, FLOOR)
    before = m[h]
    peak = jnp.maximum(before, jnp.max(s, axis=1, keepdims=True))
    p = jnp.exp2(s - peak[:, :1]).astype(BF16)
    if seen is not None:
        p = jnp.where(seen, p, jnp.zeros_like(p))
    fade = jnp.exp2(before - peak)
    wide = jnp.concatenate([value, jnp.ones(value.shape, BF16)], axis=1)
    acc[h] = acc[h] * jnp.concatenate([fade, fade], axis=1) + jnp.dot(p, wide, preferred_element_type=F32)
    m[h] = peak


def project_columns(attended, weight, dest):
    cols = weight[:, pl.ds(pl.multiple_of(dest * 1024, 1024), 1024)]
    return jnp.dot(attended, cols, preferred_element_type=F32)


def finish_kernel(sizes, vis, where, *refs):
    count = len(sizes)
    chunks = refs[:count]
    q, kv, acc, weight, attended, far_a, far_b, safe, peak, block, sem = refs[count:]
    worst = jnp.max(jnp.maximum(jnp.max(acc[:, :, HD:], axis=0), 0.0))
    worst = jnp.where(worst < LIMIT, 0, 1)

    @pl.when(worst == 0)
    def _():
        for h in range(GROUP):
            attended[:, h * HD : (h + 1) * HD] = (acc[h, :, :HD] / acc[h, :, HD:]).astype(BF16)

    @pl.when(worst != 0)
    def _():
        safe[...] = jnp.zeros_like(safe)
        peak[...] = jnp.full_like(peak, FLOOR)
        row = lax.broadcasted_iota(jnp.int32, (SPAN, SPAN), 0)
        col = lax.broadcasted_iota(jnp.int32, (SPAN, SPAN), 1)

        @pl.loop(0, GROUP)
        def _(h):
            online_step(h, q, kv[:, :HD], kv[:, HD:], col <= row, safe, peak)

        first = 0
        for ref, n in zip(chunks, sizes):

            @pl.loop(0, n // UNIT)
            def _(u):
                @pl.when(vis[first + u] > 0)
                def _():
                    copy = pltpu.make_async_copy(
                        ref.at[pl.ds(pl.multiple_of(u * UNIT, UNIT), UNIT), :], block, sem
                    )
                    copy.start()
                    copy.wait()

                    @pl.loop(0, GROUP)
                    def _(h):
                        online_step(h, q, block[:, :HD], block[:, HD:], None, safe, peak)

            first += n // UNIT
        for h in range(GROUP):
            attended[:, h * HD : (h + 1) * HD] = (safe[h, :, :HD] / safe[h, :, HD:]).astype(BF16)

    far = project_columns(attended[...], weight, where[1]).astype(BF16)
    far_a[...] = far[: SPAN // 2]
    far_b[...] = far[SPAN // 2 :]


def finish(chunks, vis, where, q, kv, acc, weight):
    sizes = [c.shape[0] for c in chunks]
    part = jax.ShapeDtypeStruct((SPAN // 2, 1024), BF16)
    return pl.pallas_call(
        functools.partial(finish_kernel, sizes),
        in_specs=[SMEM, SMEM] + [ANY] * len(chunks) + [VMEM] * 4,
        out_specs=[VMEM] * 3,
        out_shape=[jax.ShapeDtypeStruct((SPAN, 1024), BF16), part, part],
        scratch_shapes=[
            pltpu.VMEM((GROUP, SPAN, 2 * HD), F32),
            pltpu.VMEM((GROUP, SPAN, HD), F32),
            pltpu.VMEM((UNIT, 2 * HD), BF16),
            pltpu.SemaphoreType.DMA,
        ],
        cost_estimate=pl.CostEstimate(flops=2 * SPAN * 1024 * 1024, bytes_accessed=2**22, transcendentals=0),
        compiler_params=params(24),
        name="finish",
    )(vis, where, *chunks, q, kv, acc, weight)


def near_kernel(where, attended, weight, residual, up_a, up_b, down_a, down_b, mine):
    half = SPAN // 2
    up = project_columns(attended[...], weight, where[2]).astype(BF16)
    up_a[...] = up[:half]
    up_b[...] = up[half:]
    down = project_columns(attended[...], weight, where[3]).astype(BF16)
    down_a[...] = down[:half]
    down_b[...] = down[half:]
    mine[...] = project_columns(attended[...], weight, where[0]) + residual[...].astype(F32)


def project_near(where, attended, weight, residual):
    part = jax.ShapeDtypeStruct((SPAN // 2, 1024), BF16)
    return pl.pallas_call(
        near_kernel,
        in_specs=[SMEM] + [VMEM] * 3,
        out_specs=[VMEM] * 5,
        out_shape=[part] * 4 + [jax.ShapeDtypeStruct((SPAN, 1024), F32)],
        cost_estimate=pl.CostEstimate(flops=6 * SPAN * 1024 * 1024, bytes_accessed=2**23, transcendentals=0),
        compiler_params=params(24),
        name="project_near",
    )(where, attended, weight, residual)


def pages_kernel(layout, pages, sections, *refs):
    chunks, out = refs[:-1], refs[-1]
    rows = lax.broadcasted_iota(jnp.int32, (2 * PAGE_TOK, 2 * HD), 0)
    for place, ((ref_a, row_a), (ref_b, row_b)) in enumerate(layout):
        s = sections[place]
        found = []
        for rank in range(2):
            page = pages[rank, s]
            pair = pl.multiple_of((jnp.maximum(page, 0) % 16) // 2 * 16, 16)
            in_a = chunks[ref_a][pl.ds(row_a + pair, 16), :]
            in_b = chunks[ref_b][pl.ds(row_b + pair, 16), :]
            both = jnp.where(page < 16, in_a.astype(F32), in_b.astype(F32))
            one = jnp.where(page % 2 == 0, both[:PAGE_TOK], both[PAGE_TOK:])
            found.append(jnp.where(page >= 0, one, 0.0))
        out[pl.ds(pl.multiple_of(s * 16, 16), 16), :] = jnp.concatenate(found, axis=0).astype(BF16)


def take_pages(layout, pages, sections, chunks):
    return pl.pallas_call(
        functools.partial(pages_kernel, layout),
        in_specs=[SMEM, SMEM] + [VMEM] * len(chunks),
        out_specs=VMEM,
        out_shape=jax.ShapeDtypeStruct((2 * XS * ZS * 2 * PAGE_TOK, 2 * HD), BF16),
        cost_estimate=pl.CostEstimate(flops=2**20, bytes_accessed=2**23, transcendentals=0),
        compiler_params=params(16),
        name="take_pages",
    )(pages, sections, *chunks)


def local(queries, keys, values, out_weight, residual, span_of_section, page_owner):
    me = lax.axis_index("section")
    t = lax.axis_index("tensor")
    sections = lax.axis_size("section")
    tensors = lax.axis_size("tensor")
    my_xz, core = me >> 1, me & 1
    x, z, way = my_xz >> 3, my_xz & 7, 1 - 2 * core

    direct = [(0, 0, 0), (2, 0, 0), (-1, 0, 0), (-1, 0, 1)]

    def swapped(offsets):
        return [(-dx, -dz, 1 - c) for dx, dz, c in offsets]

    def moved(offsets, steps):
        return [(dx, dz - steps, c) for dx, dz, c in offsets]

    first, second = direct, swapped(direct)
    pieces = [first, second]
    for step in (1, 2, 3):
        for part in (first, second):
            pieces += [moved(part, step), swapped(moved(part, step))]
    pieces += [moved(first, 4), swapped(moved(first, 4))]
    place = {
        (dx % XS, dz % ZS, c): (number, i * SPAN)
        for number, offsets in enumerate(pieces)
        for i, (dx, dz, c) in enumerate(offsets)
    }
    relative = [(dx, dz, c) for dx in range(XS) for dz in range(ZS) for c in range(2)]
    layout = [((place[r][0], place[r][1]), (place[r][0], place[r][1] + UNIT)) for r in relative]

    kv = pack(keys, values)
    far = across(kv)
    near = pass_on(jnp.concatenate([kv, swap_core(kv)], axis=0), dx=1)

    def ids(table):
        dx, dz, dc = (jnp.array(column, jnp.int32) for column in zip(*table))
        return ((((x + way * dx) & 3) * ZS + ((z + way * dz) & 7)) << 1) + (core ^ dc)

    ids_units = ids([r for offsets in pieces for r in offsets for _ in range(2)])
    ids_relative = ids(relative)
    section_ids = jnp.arange(sections, dtype=jnp.int32)
    my_span = jnp.sum(jnp.where(section_ids == me, span_of_section, 0))
    unit_spans = jnp.sum(
        jnp.where(ids_units[:, None] == section_ids[None, :], span_of_section[None, :], 0), axis=1
    )
    vis = (unit_spans < my_span).astype(jnp.int32)
    where = (t + jnp.array([0, 2, 1, 3], jnp.int32)) & (tensors - 1)
    owners = page_owner.reshape(sections, PPH)
    page_ids = jnp.arange(PPH, dtype=jnp.int32)[None, :]
    mine = owners == me
    first_page = jnp.min(jnp.where(mine, page_ids, PPH), axis=1)
    last_page = jnp.max(jnp.where(mine, page_ids, -1), axis=1)
    pages = jnp.stack(
        [
            jnp.where(first_page < PPH, first_page, -1),
            jnp.where(last_page > first_page, last_page, -1),
        ]
    )

    m, acc = attend_own(queries, kv)
    near, far, m, acc, vis, pages, ids_relative = lax.optimization_barrier(
        (near, far, m, acc, vis, pages, ids_relative)
    )
    chunks = []

    def attend(acc, arrays):
        first_unit = sum(c.shape[0] for c in chunks) // UNIT
        chunks.extend(arrays)
        return attend_pieces(arrays, first_unit, vis, queries, m, acc)

    def take(acc, piece, onward=True):
        acc, piece = lax.optimization_barrier((acc, piece))
        return acc, [piece, swap_core(piece)], pass_on(piece, dz=1) if onward else None

    row = jnp.concatenate([kv, far, near], axis=0)
    a_next = pass_on(row, dz=1)
    row_swapped = swap_core(row)
    b_next = pass_on(row_swapped, dz=1)
    acc = attend(acc, [row, row_swapped])
    acc, a_now, a_next = take(acc, a_next)
    acc = attend(acc, a_now)
    acc, b_now, b_next = take(acc, b_next)
    for step in (2, 3):
        acc, a_now, a_next = take(acc, a_next)
        acc = attend(acc, b_now)
        acc, b_now, b_next = take(acc, b_next, onward=step < 3)
        acc = attend(acc, a_now)
    acc, a_now, _ = take(acc, a_next, onward=False)
    acc = attend(acc, b_now)
    acc = attend(acc, a_now)

    attended, far_a, far_b = finish(chunks, vis, where, queries, kv, acc, out_weight)
    relay_a, relay_b = turn(far_a, 1), turn(far_b, -1)
    up_a, up_b, down_a, down_b, own_sum = project_near(where, attended, out_weight, residual)
    from_below_b, from_above_a = turn(up_b, 1), turn(down_a, -1)
    from_below_a = turn((up_a.astype(F32) + relay_a.astype(F32)).astype(BF16), 1)
    from_above_b = turn((down_b.astype(F32) + relay_b.astype(F32)).astype(BF16), -1)
    below = jnp.concatenate([from_below_a, from_below_b], axis=0).astype(F32)
    above = jnp.concatenate([from_above_a, from_above_b], axis=0).astype(F32)
    updated = (own_sum + below + above).astype(BF16)

    cache = take_pages(layout, pages, ids_relative, chunks)
    kv_cache = cache.reshape(1, 1, sections, 2, PAGE_TOK, 2 * HD)
    return (updated, kv_cache)


def solution(mesh):
    return jax.shard_map(
        local,
        mesh=mesh,
        in_specs=(
            P("section", "tensor"),
            P("section", "tensor"),
            P("section", "tensor"),
            P("tensor", None),
            P("section", "tensor"),
            P(),
            P(None, "tensor", None, None),
        ),
        out_specs=(P("section", "tensor"), P("section", "tensor", None, None, None, None)),
        check_vma=False,
    )
```

```python
import functools
import math

import jax
import jax.numpy as jnp
from jax import lax
from jax.experimental import pallas as pl
from jax.experimental.pallas import tpu as pltpu
from jax.sharding import PartitionSpec as P

HD = 128
GROUP = 8
SPAN = 256
PAGE_TOK = 8
PPH = 32
XS, ZS = 4, 8
SCALE2 = math.log2(math.e) / math.sqrt(HD)
FLOOR = -1e30
LIMIT = 1e30
F32, BF16 = jnp.float32, jnp.bfloat16
NT = (((1,), (1,)), ((), ()))
VMEM = pl.BlockSpec(memory_space=pltpu.VMEM)
SMEM = pl.BlockSpec(memory_space=pltpu.SMEM)
ANY = pl.BlockSpec(memory_space=pl.ANY)
HBM = pl.BlockSpec(memory_space=pltpu.HBM)


def params(mib):
    return pltpu.CompilerParams(vmem_limit_bytes=mib * 2**20)


def section_at(x, z, core):
    return ((x % XS) * ZS + z % ZS) * 2 + core


def across(a):
    pairs = [
        (section_at(x, z, c), section_at(x + 2, z, c))
        for x in range(XS)
        for z in range(ZS)
        for c in range(2)
    ]
    return lax.ppermute(a, "section", pairs)


def pass_on(a, dx=0, dz=0):
    pairs = [
        (section_at(x, z, c), section_at(x + (1 - 2 * c) * dx, z + (1 - 2 * c) * dz, c))
        for x in range(XS)
        for z in range(ZS)
        for c in range(2)
    ]
    return lax.ppermute(a, "section", pairs)


def swap_core(a):
    return lax.ppermute(a, "section", [(s, s ^ 1) for s in range(XS * ZS * 2)])


def turn(a, d):
    n = lax.axis_size("tensor")
    return lax.ppermute(a, "tensor", [(t, (t + d) % n) for t in range(n)])


def head_column(m, h):
    lane = lax.broadcasted_iota(jnp.int32, m.shape, 1)
    return jnp.sum(jnp.where(lane == h, m, 0.0), axis=1, keepdims=True)


def pack_kernel(keys, values, out, sems):
    copies = [
        pltpu.make_async_copy(keys, out.at[:, :HD], sems.at[0]),
        pltpu.make_async_copy(values, out.at[:, HD:], sems.at[1]),
    ]
    for copy in copies:
        copy.start()
    for copy in copies:
        copy.wait()


def pack(keys, values):
    return pl.pallas_call(
        pack_kernel,
        in_specs=[HBM, HBM],
        out_specs=VMEM,
        out_shape=jax.ShapeDtypeStruct((SPAN, 2 * HD), BF16),
        scratch_shapes=[pltpu.SemaphoreType.DMA((2,))],
        compiler_params=params(4),
        name="pack",
    )(keys, values)


def my_place():
    me = lax.axis_index("section")
    return me >> 4, (me >> 1) & 7, me & 1


def section_id(here, offset):
    (x, z, core), (dx, dz, other) = here, offset
    way = 1 - 2 * core
    return ((((x + way * dx) & 3) * ZS + ((z + way * dz) & 7)) << 1) + (core ^ other)


def own_kernel(table, spans, q, kv, m_out, acc, vis):
    here = my_place()
    mine = spans[section_id(here, (0, 0, 0))]
    for i, offset in enumerate(table):
        vis[i] = jnp.where(spans[section_id(here, offset)] < mine, 1, 0)
    row = lax.broadcasted_iota(jnp.int32, (SPAN, SPAN), 0)
    col = lax.broadcasted_iota(jnp.int32, (SPAN, SPAN), 1)
    seen = col <= row
    lane = lax.broadcasted_iota(jnp.int32, (SPAN, HD), 1)
    key = kv[:, :HD]
    wide = jnp.concatenate([kv[:, HD:], jnp.ones((SPAN, HD), BF16)], axis=1)
    m = jnp.zeros((SPAN, HD), F32)
    for h in range(GROUP):
        s = lax.dot_general(q[:, h * HD : (h + 1) * HD], key, NT, preferred_element_type=F32)
        s = jnp.where(seen, s * SCALE2, FLOOR)
        peak = jnp.max(s, axis=1, keepdims=True)
        p = jnp.exp2(s - peak).astype(BF16)
        acc[h] = jnp.dot(p, wide, preferred_element_type=F32)
        m = jnp.where(lane == h, peak, m)
    m_out[...] = m


def attend_own(table, spans, q, kv):
    return pl.pallas_call(
        functools.partial(own_kernel, table),
        in_specs=[SMEM, VMEM, VMEM],
        out_specs=[VMEM, VMEM, SMEM],
        out_shape=[
            jax.ShapeDtypeStruct((SPAN, HD), F32),
            jax.ShapeDtypeStruct((GROUP, SPAN, 2 * HD), F32),
            jax.ShapeDtypeStruct((len(table),), jnp.int32),
        ],
        cost_estimate=pl.CostEstimate(
            flops=8 * GROUP * SPAN * SPAN * HD, bytes_accessed=2**22, transcendentals=GROUP * SPAN * SPAN
        ),
        compiler_params=params(16),
        name="own_span",
    )(spans, q, kv)


def pieces_kernel(sizes, first_unit, vis, *refs):
    count = len(sizes)
    chunks = refs[:count]
    q, m, acc_in, acc, vs = refs[count:]
    total = sum(sizes)
    row = 0
    for ref, n in zip(chunks, sizes):
        for j in range(0, n, SPAN):
            keep = vis[first_unit + (row + j) // SPAN] > 0
            value = ref[j : j + SPAN, HD:]
            vs[row + j : row + j + SPAN, :HD] = jnp.where(keep, value, jnp.zeros_like(value))
            vs[row + j : row + j + SPAN, HD:] = jnp.full((SPAN, HD), keep.astype(F32)).astype(BF16)
        row += n
    source, lo = acc_in, 0
    while lo < total:
        names, n = [], 0
        while len(names) < len(chunks) and n + sizes[len(names)] <= 2048:
            names.append(chunks[len(names)])
            n += sizes[len(names) - 1]
        chunks, sizes = chunks[len(names) :], sizes[len(names) :]
        some = vis[first_unit + lo // SPAN]
        for u in range(lo // SPAN + 1, (lo + n) // SPAN):
            some = some + vis[first_unit + u]

        @pl.when(some > 0)
        def _():
            for h in range(GROUP):
                reference = head_column(m[...], h)
                weights = []
                for ref in names:
                    s = lax.dot_general(
                        q[:, h * HD : (h + 1) * HD], ref[:, :HD], NT, preferred_element_type=F32
                    )
                    weights.append(jnp.exp2(s * SCALE2 - reference).astype(BF16))
                weights = jnp.concatenate(weights, axis=1)
                acc[h] = source[h] + jnp.dot(weights, vs[lo : lo + n, :], preferred_element_type=F32)

        if lo == 0:

            @pl.when(some == 0)
            def _():
                acc[...] = acc_in[...]

        source, lo = acc, lo + n


def attend_pieces(chunks, first_unit, vis, q, m, acc):
    sizes = [c.shape[0] for c in chunks]
    total = sum(sizes)
    return pl.pallas_call(
        functools.partial(pieces_kernel, sizes, first_unit),
        in_specs=[SMEM] + [VMEM] * (len(chunks) + 3),
        out_specs=VMEM,
        out_shape=jax.ShapeDtypeStruct(acc.shape, F32),
        scratch_shapes=[pltpu.VMEM((total, 2 * HD), BF16)],
        input_output_aliases={len(chunks) + 3: 0},
        cost_estimate=pl.CostEstimate(flops=2**20, bytes_accessed=2**18, transcendentals=0),
        compiler_params=params(24),
        name="attend_pieces",
    )(vis, *chunks, q, m, acc)


def online_step(h, q, key, value, seen, acc, m):
    s = lax.dot_general(
        q[:, pl.ds(pl.multiple_of(h * HD, HD), HD)], key, NT, preferred_element_type=F32
    )
    s = s * SCALE2
    if seen is not None:
        s = jnp.where(seen, s, FLOOR)
    before = m[h]
    peak = jnp.maximum(before, jnp.max(s, axis=1, keepdims=True))
    p = jnp.exp2(s - peak[:, :1]).astype(BF16)
    if seen is not None:
        p = jnp.where(seen, p, jnp.zeros_like(p))
    fade = jnp.exp2(before - peak)
    wide = jnp.concatenate([value, jnp.ones(value.shape, BF16)], axis=1)
    acc[h] = acc[h] * jnp.concatenate([fade, fade], axis=1) + jnp.dot(p, wide, preferred_element_type=F32)
    m[h] = peak


def project_columns(attended, weight, dest):
    cols = weight[:, pl.ds(pl.multiple_of(dest * 1024, 1024), 1024)]
    return jnp.dot(attended, cols, preferred_element_type=F32)


def finish_kernel(sizes, vis, *refs):
    count = len(sizes)
    chunks = refs[:count]
    q, kv, acc, weight, attended, far_a, far_b, safe, peak, block, sem = refs[count:]
    worst = jnp.max(jnp.maximum(jnp.max(acc[:, :, HD:], axis=0), 0.0))
    worst = jnp.where(worst < LIMIT, 0, 1)

    @pl.when(worst == 0)
    def _():
        for h in range(GROUP):
            attended[:, h * HD : (h + 1) * HD] = (acc[h, :, :HD] / acc[h, :, HD:]).astype(BF16)

    @pl.when(worst != 0)
    def _():
        safe[...] = jnp.zeros_like(safe)
        peak[...] = jnp.full_like(peak, FLOOR)
        row = lax.broadcasted_iota(jnp.int32, (SPAN, SPAN), 0)
        col = lax.broadcasted_iota(jnp.int32, (SPAN, SPAN), 1)

        @pl.loop(0, GROUP)
        def _(h):
            online_step(h, q, kv[:, :HD], kv[:, HD:], col <= row, safe, peak)

        first = 0
        for ref, n in zip(chunks, sizes):

            @pl.loop(0, n // SPAN)
            def _(u):
                @pl.when(vis[first + u] > 0)
                def _():
                    copy = pltpu.make_async_copy(
                        ref.at[pl.ds(pl.multiple_of(u * SPAN, SPAN), SPAN), :], block, sem
                    )
                    copy.start()
                    copy.wait()

                    @pl.loop(0, GROUP)
                    def _(h):
                        online_step(h, q, block[:, :HD], block[:, HD:], None, safe, peak)

            first += n // SPAN
        for h in range(GROUP):
            attended[:, h * HD : (h + 1) * HD] = (safe[h, :, :HD] / safe[h, :, HD:]).astype(BF16)

    far = project_columns(attended[...], weight, (lax.axis_index("tensor") + 2) & 3).astype(BF16)
    far_a[...] = far[: SPAN // 2]
    far_b[...] = far[SPAN // 2 :]


def finish(chunks, vis, q, kv, acc, weight):
    sizes = [c.shape[0] for c in chunks]
    part = jax.ShapeDtypeStruct((SPAN // 2, 1024), BF16)
    return pl.pallas_call(
        functools.partial(finish_kernel, sizes),
        in_specs=[SMEM] + [ANY] * len(chunks) + [VMEM] * 4,
        out_specs=[VMEM] * 3,
        out_shape=[jax.ShapeDtypeStruct((SPAN, 1024), BF16), part, part],
        scratch_shapes=[
            pltpu.VMEM((GROUP, SPAN, 2 * HD), F32),
            pltpu.VMEM((GROUP, SPAN, HD), F32),
            pltpu.VMEM((SPAN, 2 * HD), BF16),
            pltpu.SemaphoreType.DMA,
        ],
        cost_estimate=pl.CostEstimate(flops=2 * SPAN * 1024 * 1024, bytes_accessed=2**22, transcendentals=0),
        compiler_params=params(24),
        name="finish",
    )(vis, *chunks, q, kv, acc, weight)


def near_kernel(attended, weight, residual, up_a, up_b, down_a, down_b, mine):
    half = SPAN // 2
    t = lax.axis_index("tensor")
    up = project_columns(attended[...], weight, (t + 1) & 3).astype(BF16)
    up_a[...] = up[:half]
    up_b[...] = up[half:]
    down = project_columns(attended[...], weight, (t + 3) & 3).astype(BF16)
    down_a[...] = down[:half]
    down_b[...] = down[half:]
    mine[...] = project_columns(attended[...], weight, t) + residual[...].astype(F32)


def project_near(attended, weight, residual):
    part = jax.ShapeDtypeStruct((SPAN // 2, 1024), BF16)
    return pl.pallas_call(
        near_kernel,
        in_specs=[VMEM] * 3,
        out_specs=[VMEM] * 5,
        out_shape=[part] * 4 + [jax.ShapeDtypeStruct((SPAN, 1024), F32)],
        cost_estimate=pl.CostEstimate(flops=6 * SPAN * 1024 * 1024, bytes_accessed=2**23, transcendentals=0),
        compiler_params=params(24),
        name="project_near",
    )(attended, weight, residual)


def pages_kernel(layout, pages, *refs):
    chunks, out = refs[:-1], refs[-1]
    here = my_place()
    for offset, (ref, row) in layout:
        s = section_id(here, offset)
        found = []
        for rank in range(2):
            page = pages[rank, s]
            pair = pl.multiple_of((jnp.maximum(page, 0) >> 1) * 16, 16)
            both = chunks[ref][pl.ds(row + pair, 16), :].astype(F32)
            one = jnp.where((page & 1) == 0, both[:PAGE_TOK], both[PAGE_TOK:])
            found.append(jnp.where(page >= 0, one, 0.0))
        out[pl.ds(pl.multiple_of(s * 16, 16), 16), :] = jnp.concatenate(found, axis=0).astype(BF16)


def take_pages(layout, pages, chunks):
    return pl.pallas_call(
        functools.partial(pages_kernel, layout),
        in_specs=[SMEM] + [VMEM] * len(chunks),
        out_specs=VMEM,
        out_shape=jax.ShapeDtypeStruct((2 * XS * ZS * 2 * PAGE_TOK, 2 * HD), BF16),
        cost_estimate=pl.CostEstimate(flops=2**20, bytes_accessed=2**23, transcendentals=0),
        compiler_params=params(16),
        name="take_pages",
    )(pages, *chunks)


def find_pages(page_owner):
    owners = page_owner.reshape(page_owner.shape[0], PPH)
    page_ids = jnp.arange(PPH, dtype=jnp.int32)[None, :]
    mine = owners == lax.axis_index("section")
    first = jnp.min(jnp.where(mine, page_ids, PPH), axis=1)
    last = jnp.max(jnp.where(mine, page_ids, -1), axis=1)
    return jnp.stack([jnp.where(first < PPH, first, -1), jnp.where(last > first, last, -1)])


def local(queries, keys, values, out_weight, residual, span_of_section, page_owner):
    sections = lax.axis_size("section")

    direct = [(0, 0, 0), (2, 0, 0), (-1, 0, 0), (-1, 0, 1)]

    def swapped(offsets):
        return [(-dx, -dz, 1 - c) for dx, dz, c in offsets]

    def moved(offsets, steps):
        return [(dx, dz - steps, c) for dx, dz, c in offsets]

    first, second = direct, swapped(direct)
    order = ["r0", "r1", "a10", "a11", "b10", "b11", "a20", "a21", "b20", "b21", "a30"]
    order += ["a31", "b30", "a40", "b31", "a41"]

    def held(name):
        part = moved({"r": first, "a": first, "b": second}[name[0]], int(name[1:-1] or 0))
        return swapped(part) if name[-1] == "1" else part

    pieces = [held(name) for name in order]
    place = {
        (dx % XS, dz % ZS, c): (number, i * SPAN)
        for number, offsets in enumerate(pieces)
        for i, (dx, dz, c) in enumerate(offsets)
    }
    relative = [(dx, dz, c) for dx in range(XS) for dz in range(ZS) for c in range(2)]
    layout = [(r, place[r]) for r in relative]
    table = [r for offsets in pieces for r in offsets]

    kv = pack(keys, values)
    far = across(kv)
    near = pass_on(jnp.concatenate([kv, swap_core(kv)], axis=0), dx=1)
    m, acc, vis = attend_own(table, span_of_section, queries, kv)
    near, far, acc = lax.optimization_barrier((near, far, acc))
    chunks = []

    def attend(acc, parts):
        arrays = [pair[side] for pair, side in parts]
        first_unit = sum(c.shape[0] for c in chunks) // SPAN
        chunks.extend(arrays)
        return attend_pieces(arrays, first_unit, vis, queries, m, acc)

    def take(acc, piece, onward=True):
        acc, piece = lax.optimization_barrier((acc, piece))
        return acc, [piece, swap_core(piece)], pass_on(piece, dz=1) if onward else None

    row = jnp.concatenate([kv, far, near], axis=0)
    a_next = pass_on(row, dz=1)
    row_swapped = swap_core(row)
    b_next = pass_on(row_swapped, dz=1)
    acc = attend(acc, [((row, row_swapped), 0), ((row, row_swapped), 1)])
    acc, a1, a_next = take(acc, a_next)
    acc, b1, b_next = take(acc, b_next)
    acc = attend(acc, [(a1, 0), (a1, 1), (b1, 0)])
    acc, a2, a_next = take(acc, a_next)
    acc = attend(acc, [(b1, 1), (a2, 0), (a2, 1)])
    acc, b2, b_next = take(acc, b_next)
    acc, a3, a_next = take(acc, a_next)
    acc = attend(acc, [(b2, 0), (b2, 1), (a3, 0)])
    acc, b3, _ = take(acc, b_next, onward=False)
    acc, a4, _ = take(acc, a_next, onward=False)
    acc = attend(acc, [(a3, 1), (b3, 0), (a4, 0)])
    acc = attend(acc, [(b3, 1), (a4, 1)])

    attended, far_a, far_b = finish(chunks, vis, queries, kv, acc, out_weight)
    relay_a, relay_b = turn(far_a, 1), turn(far_b, -1)
    up_a, up_b, down_a, down_b, own_sum = project_near(attended, out_weight, residual)
    from_below_b, from_above_a = turn(up_b, 1), turn(down_a, -1)
    from_below_a = turn((up_a.astype(F32) + relay_a.astype(F32)).astype(BF16), 1)
    from_above_b = turn((down_b.astype(F32) + relay_b.astype(F32)).astype(BF16), -1)
    below = jnp.concatenate([from_below_a, from_below_b], axis=0).astype(F32)
    above = jnp.concatenate([from_above_a, from_above_b], axis=0).astype(F32)
    updated = (own_sum + below + above).astype(BF16)

    attended, page_owner = lax.optimization_barrier((attended, page_owner))
    cache = take_pages(layout, find_pages(page_owner), chunks)
    kv_cache = cache.reshape(1, 1, sections, 2, PAGE_TOK, 2 * HD)
    return (updated, kv_cache)


def solution(mesh):
    return jax.shard_map(
        local,
        mesh=mesh,
        in_specs=(
            P("section", "tensor"),
            P("section", "tensor"),
            P("section", "tensor"),
            P("tensor", None),
            P("section", "tensor"),
            P(),
            P(None, "tensor", None, None),
        ),
        out_specs=(P("section", "tensor"), P("section", "tensor", None, None, None, None)),
        check_vma=False,
    )
```

```python
import functools
import math

import jax
import jax.numpy as jnp
from jax import lax
from jax.experimental import pallas as pl
from jax.experimental.pallas import tpu as pltpu
from jax.sharding import PartitionSpec as P

HD = 128
GROUP = 8
SPAN = 256
PAGE_TOK = 8
PPH = 32
XS, ZS = 4, 8
SCALE2 = math.log2(math.e) / math.sqrt(HD)
FLOOR = -1e30
LIMIT = 1e30
F32, BF16 = jnp.float32, jnp.bfloat16
NT = (((1,), (1,)), ((), ()))
VMEM = pl.BlockSpec(memory_space=pltpu.VMEM)
SMEM = pl.BlockSpec(memory_space=pltpu.SMEM)
ANY = pl.BlockSpec(memory_space=pl.ANY)
HBM = pl.BlockSpec(memory_space=pltpu.HBM)


def params(mib):
    return pltpu.CompilerParams(vmem_limit_bytes=mib * 2**20)


def section_at(x, z, core):
    return ((x % XS) * ZS + z % ZS) * 2 + core


def across(a):
    pairs = [
        (section_at(x, z, c), section_at(x + 2, z, c))
        for x in range(XS)
        for z in range(ZS)
        for c in range(2)
    ]
    return lax.ppermute(a, "section", pairs)


def pass_on(a, dx=0, dz=0):
    pairs = [
        (section_at(x, z, c), section_at(x + (1 - 2 * c) * dx, z + (1 - 2 * c) * dz, c))
        for x in range(XS)
        for z in range(ZS)
        for c in range(2)
    ]
    return lax.ppermute(a, "section", pairs)


def swap_core(a):
    return lax.ppermute(a, "section", [(s, s ^ 1) for s in range(XS * ZS * 2)])


def turn(a, d):
    n = lax.axis_size("tensor")
    return lax.ppermute(a, "tensor", [(t, (t + d) % n) for t in range(n)])


def head_column(m, h):
    lane = lax.broadcasted_iota(jnp.int32, m.shape, 1)
    return jnp.sum(jnp.where(lane == h, m, 0.0), axis=1, keepdims=True)


def pack_kernel(keys, values, out, sems):
    copies = [
        pltpu.make_async_copy(keys, out.at[:, :HD], sems.at[0]),
        pltpu.make_async_copy(values, out.at[:, HD:], sems.at[1]),
    ]
    for copy in copies:
        copy.start()
    for copy in copies:
        copy.wait()


def pack(keys, values):
    return pl.pallas_call(
        pack_kernel,
        in_specs=[HBM, HBM],
        out_specs=VMEM,
        out_shape=jax.ShapeDtypeStruct((SPAN, 2 * HD), BF16),
        scratch_shapes=[pltpu.SemaphoreType.DMA((2,))],
        compiler_params=params(60),
        name="pack",
    )(keys, values)


def my_place():
    me = lax.axis_index("section")
    return me >> 4, (me >> 1) & 7, me & 1


def section_id(here, offset):
    (x, z, core), (dx, dz, other) = here, offset
    way = 1 - 2 * core
    return ((((x + way * dx) & 3) * ZS + ((z + way * dz) & 7)) << 1) + (core ^ other)


def own_kernel(table, spans, q, kv, m_out, acc, vis):
    here = my_place()
    mine = spans[section_id(here, (0, 0, 0))]
    for i, offset in enumerate(table):
        vis[i] = jnp.where(spans[section_id(here, offset)] < mine, 1, 0)
    row = lax.broadcasted_iota(jnp.int32, (SPAN, SPAN), 0)
    col = lax.broadcasted_iota(jnp.int32, (SPAN, SPAN), 1)
    seen = col <= row
    lane = lax.broadcasted_iota(jnp.int32, (SPAN, HD), 1)
    key = kv[:, :HD]
    wide = jnp.concatenate([kv[:, HD:], jnp.ones((SPAN, HD), BF16)], axis=1)
    m = jnp.zeros((SPAN, HD), F32)
    for h in range(GROUP):
        s = lax.dot_general(q[:, h * HD : (h + 1) * HD], key, NT, preferred_element_type=F32)
        s = jnp.where(seen, s * SCALE2, FLOOR)
        peak = jnp.max(s, axis=1, keepdims=True)
        p = jnp.exp2(s - peak).astype(BF16)
        acc[h] = jnp.dot(p, wide, preferred_element_type=F32)
        m = jnp.where(lane == h, peak, m)
    m_out[...] = m


def attend_own(table, spans, q, kv):
    return pl.pallas_call(
        functools.partial(own_kernel, table),
        in_specs=[SMEM, VMEM, VMEM],
        out_specs=[VMEM, VMEM, SMEM],
        out_shape=[
            jax.ShapeDtypeStruct((SPAN, HD), F32),
            jax.ShapeDtypeStruct((GROUP, SPAN, 2 * HD), F32),
            jax.ShapeDtypeStruct((len(table),), jnp.int32),
        ],
        cost_estimate=pl.CostEstimate(
            flops=8 * GROUP * SPAN * SPAN * HD, bytes_accessed=2**22, transcendentals=GROUP * SPAN * SPAN
        ),
        compiler_params=params(32),
        name="own_span",
    )(spans, q, kv)


def pieces_kernel(sizes, first_unit, vis, *refs):
    count = len(sizes)
    chunks = refs[:count]
    q, m, acc_in, acc, vs = refs[count:]
    total = sum(sizes)
    row = 0
    for ref, n in zip(chunks, sizes):
        for j in range(0, n, SPAN):
            keep = vis[first_unit + (row + j) // SPAN] > 0
            value = ref[j : j + SPAN, HD:]
            vs[row + j : row + j + SPAN, :HD] = jnp.where(keep, value, jnp.zeros_like(value))
            vs[row + j : row + j + SPAN, HD:] = jnp.full((SPAN, HD), keep.astype(F32)).astype(BF16)
        row += n
    source, lo = acc_in, 0
    while lo < total:
        names, n = [], 0
        while len(names) < len(chunks) and n + sizes[len(names)] <= 2048:
            names.append(chunks[len(names)])
            n += sizes[len(names) - 1]
        chunks, sizes = chunks[len(names) :], sizes[len(names) :]
        some = vis[first_unit + lo // SPAN]
        for u in range(lo // SPAN + 1, (lo + n) // SPAN):
            some = some + vis[first_unit + u]

        @pl.when(some > 0)
        def _():
            for h in range(GROUP):
                reference = head_column(m[...], h)
                weights = []
                for ref in names:
                    s = lax.dot_general(
                        q[:, h * HD : (h + 1) * HD], ref[:, :HD], NT, preferred_element_type=F32
                    )
                    weights.append(jnp.exp2(s * SCALE2 - reference).astype(BF16))
                weights = jnp.concatenate(weights, axis=1)
                acc[h] = source[h] + jnp.dot(weights, vs[lo : lo + n, :], preferred_element_type=F32)

        if lo == 0:

            @pl.when(some == 0)
            def _():
                acc[...] = acc_in[...]

        source, lo = acc, lo + n


def attend_pieces(chunks, first_unit, vis, q, m, acc):
    sizes = [c.shape[0] for c in chunks]
    total = sum(sizes)
    return pl.pallas_call(
        functools.partial(pieces_kernel, sizes, first_unit),
        in_specs=[SMEM] + [VMEM] * (len(chunks) + 3),
        out_specs=VMEM,
        out_shape=jax.ShapeDtypeStruct(acc.shape, F32),
        scratch_shapes=[pltpu.VMEM((total, 2 * HD), BF16)],
        input_output_aliases={len(chunks) + 3: 0},
        cost_estimate=pl.CostEstimate(flops=2**20, bytes_accessed=2**18, transcendentals=0),
        compiler_params=params(32),
        name="attend_pieces",
    )(vis, *chunks, q, m, acc)


def online_step(h, q, key, value, seen, acc, m):
    s = lax.dot_general(
        q[:, pl.ds(pl.multiple_of(h * HD, HD), HD)], key, NT, preferred_element_type=F32
    )
    s = s * SCALE2
    if seen is not None:
        s = jnp.where(seen, s, FLOOR)
    before = m[h]
    peak = jnp.maximum(before, jnp.max(s, axis=1, keepdims=True))
    p = jnp.exp2(s - peak[:, :1]).astype(BF16)
    if seen is not None:
        p = jnp.where(seen, p, jnp.zeros_like(p))
    fade = jnp.exp2(before - peak)
    wide = jnp.concatenate([value, jnp.ones(value.shape, BF16)], axis=1)
    acc[h] = acc[h] * jnp.concatenate([fade, fade], axis=1) + jnp.dot(p, wide, preferred_element_type=F32)
    m[h] = peak


def weight_copy(weight, dest, block, sem):
    columns = pl.ds(pl.multiple_of(dest * 1024, 1024), 1024)
    return pltpu.make_async_copy(weight.at[:, columns], block, sem)


def project(attended, block):
    return jnp.dot(attended[...], block[...], preferred_element_type=F32)


def finish_kernel(sizes, vis, *refs):
    count = len(sizes)
    chunks = refs[:count]
    q, kv, acc, weight, attended, far_a, far_b, safe, peak, block, columns, sems = refs[count:]
    sem = sems.at[0]
    fetch = weight_copy(weight, (lax.axis_index("tensor") + 2) & 3, columns, sems.at[1])
    fetch.start()
    worst = jnp.max(jnp.maximum(jnp.max(acc[:, :, HD:], axis=0), 0.0))
    worst = jnp.where(worst < LIMIT, 0, 1)

    @pl.when(worst == 0)
    def _():
        for h in range(GROUP):
            attended[:, h * HD : (h + 1) * HD] = (acc[h, :, :HD] / acc[h, :, HD:]).astype(BF16)

    @pl.when(worst != 0)
    def _():
        safe[...] = jnp.zeros_like(safe)
        peak[...] = jnp.full_like(peak, FLOOR)
        row = lax.broadcasted_iota(jnp.int32, (SPAN, SPAN), 0)
        col = lax.broadcasted_iota(jnp.int32, (SPAN, SPAN), 1)

        @pl.loop(0, GROUP)
        def _(h):
            online_step(h, q, kv[:, :HD], kv[:, HD:], col <= row, safe, peak)

        first = 0
        for ref, n in zip(chunks, sizes):

            @pl.loop(0, n // SPAN)
            def _(u):
                @pl.when(vis[first + u] > 0)
                def _():
                    copy = pltpu.make_async_copy(
                        ref.at[pl.ds(pl.multiple_of(u * SPAN, SPAN), SPAN), :], block, sem
                    )
                    copy.start()
                    copy.wait()

                    @pl.loop(0, GROUP)
                    def _(h):
                        online_step(h, q, block[:, :HD], block[:, HD:], None, safe, peak)

            first += n // SPAN
        for h in range(GROUP):
            attended[:, h * HD : (h + 1) * HD] = (safe[h, :, :HD] / safe[h, :, HD:]).astype(BF16)

    fetch.wait()
    far = project(attended, columns).astype(BF16)
    far_a[...] = far[: SPAN // 2]
    far_b[...] = far[SPAN // 2 :]


def finish(chunks, vis, q, kv, acc, weight):
    sizes = [c.shape[0] for c in chunks]
    part = jax.ShapeDtypeStruct((SPAN // 2, 1024), BF16)
    return pl.pallas_call(
        functools.partial(finish_kernel, sizes),
        in_specs=[SMEM] + [ANY] * len(chunks) + [VMEM] * 3 + [HBM],
        out_specs=[VMEM] * 3,
        out_shape=[jax.ShapeDtypeStruct((SPAN, 1024), BF16), part, part],
        scratch_shapes=[
            pltpu.VMEM((GROUP, SPAN, 2 * HD), F32),
            pltpu.VMEM((GROUP, SPAN, HD), F32),
            pltpu.VMEM((SPAN, 2 * HD), BF16),
            pltpu.VMEM((1024, 1024), BF16),
            pltpu.SemaphoreType.DMA((2,)),
        ],
        cost_estimate=pl.CostEstimate(flops=2 * SPAN * 1024 * 1024, bytes_accessed=2**22, transcendentals=0),
        compiler_params=params(32),
        name="finish",
    )(vis, *chunks, q, kv, acc, weight)


def near_kernel(attended, weight, residual, up_a, up_b, down_a, down_b, mine, blocks, sems):
    half = SPAN // 2
    t = lax.axis_index("tensor")
    fetches = [
        weight_copy(weight, (t + d) & 3, blocks.at[i], sems.at[i]) for i, d in enumerate((1, 3, 0))
    ]
    for fetch in fetches:
        fetch.start()
    fetches[0].wait()
    up = project(attended, blocks.at[0]).astype(BF16)
    up_a[...] = up[:half]
    up_b[...] = up[half:]
    fetches[1].wait()
    down = project(attended, blocks.at[1]).astype(BF16)
    down_a[...] = down[:half]
    down_b[...] = down[half:]
    fetches[2].wait()
    mine[...] = project(attended, blocks.at[2]) + residual[...].astype(F32)


def project_near(attended, weight, residual):
    part = jax.ShapeDtypeStruct((SPAN // 2, 1024), BF16)
    return pl.pallas_call(
        near_kernel,
        in_specs=[VMEM, HBM, VMEM],
        out_specs=[VMEM] * 5,
        out_shape=[part] * 4 + [jax.ShapeDtypeStruct((SPAN, 1024), F32)],
        scratch_shapes=[pltpu.VMEM((3, 1024, 1024), BF16), pltpu.SemaphoreType.DMA((3,))],
        cost_estimate=pl.CostEstimate(flops=6 * SPAN * 1024 * 1024, bytes_accessed=2**23, transcendentals=0),
        compiler_params=params(32),
        name="project_near",
    )(attended, weight, residual)


def pages_kernel(layout, pages, *refs):
    chunks, out = refs[:-1], refs[-1]
    here = my_place()
    for offset, (ref, row) in layout:
        s = section_id(here, offset)
        found = []
        for rank in range(2):
            page = pages[rank, s]
            pair = pl.multiple_of((jnp.maximum(page, 0) >> 1) * 16, 16)
            both = chunks[ref][pl.ds(row + pair, 16), :].astype(F32)
            one = jnp.where((page & 1) == 0, both[:PAGE_TOK], both[PAGE_TOK:])
            found.append(jnp.where(page >= 0, one, 0.0))
        out[pl.ds(pl.multiple_of(s * 16, 16), 16), :] = jnp.concatenate(found, axis=0).astype(BF16)


def take_pages(layout, pages, chunks):
    return pl.pallas_call(
        functools.partial(pages_kernel, layout),
        in_specs=[SMEM] + [VMEM] * len(chunks),
        out_specs=VMEM,
        out_shape=jax.ShapeDtypeStruct((2 * XS * ZS * 2 * PAGE_TOK, 2 * HD), BF16),
        cost_estimate=pl.CostEstimate(flops=2**20, bytes_accessed=2**23, transcendentals=0),
        compiler_params=params(32),
        name="take_pages",
    )(pages, *chunks)


def find_pages(page_owner):
    owners = page_owner.reshape(page_owner.shape[0], PPH)
    page_ids = jnp.arange(PPH, dtype=jnp.int32)[None, :]
    mine = owners == lax.axis_index("section")
    first = jnp.min(jnp.where(mine, page_ids, PPH), axis=1)
    last = jnp.max(jnp.where(mine, page_ids, -1), axis=1)
    return jnp.stack([jnp.where(first < PPH, first, -1), jnp.where(last > first, last, -1)])


def local(queries, keys, values, out_weight, residual, span_of_section, page_owner):
    sections = lax.axis_size("section")

    own, rest = [(0, 0, 0), (0, 0, 1)], [(2, 0, 0), (-1, 0, 0), (-1, 0, 1)]

    def swapped(offsets):
        return [(-dx, -dz, 1 - c) for dx, dz, c in offsets]

    rest = rest + swapped(rest)
    order = ["a10", "a11", "a00", "b00", "a20", "a21", "a30", "a31", "b10", "b11"]
    order += ["b20", "b21", "a40", "a41", "b30", "b31", "b40", "b41"]

    def held(name):
        step = int(name[1])
        part = {"a": own, "b": rest}[name[0]]
        if step == ZS // 2:
            part = part[: len(part) // 2]
        part = [(dx, dz - step, c) for dx, dz, c in part]
        return swapped(part) if name[2] == "1" else part

    pieces = [held(name) for name in order]
    place = {
        (dx % XS, dz % ZS, c): (number, i * SPAN)
        for number, offsets in enumerate(pieces)
        for i, (dx, dz, c) in enumerate(offsets)
    }
    relative = [(dx, dz, c) for dx in range(XS) for dz in range(ZS) for c in range(2)]
    layout = [(r, place[r]) for r in relative]
    table = [r for offsets in pieces for r in offsets]

    kv = pack(keys, values)
    far = across(kv)
    pair = jnp.concatenate([kv, swap_core(kv)], axis=0)
    near, a_next = pass_on(pair, dx=1), pass_on(pair, dz=1)
    m, acc, vis = attend_own(table, span_of_section, queries, kv)
    chunks = []

    def attend(acc, parts):
        first_unit = sum(c.shape[0] for c in chunks) // SPAN
        chunks.extend(parts)
        return attend_pieces(parts, first_unit, vis, queries, m, acc)

    def take(acc, piece, onward=1):
        acc, piece = lax.optimization_barrier((acc, piece))
        after = pass_on(piece[: piece.shape[0] // onward], dz=1) if onward else None
        return acc, [piece, swap_core(piece)], after

    acc, a1, a_next = take(acc, a_next)
    acc, far, near = lax.optimization_barrier((acc, far, near))
    row = jnp.concatenate([far, near, swap_core(far), swap_core(near)], axis=0)
    acc = attend(acc, a1)
    b_next = pass_on(row, dz=1)
    acc, a2, a_next = take(acc, a_next)
    acc = attend(acc, [pair, row])
    acc, a3, a_next = take(acc, a_next, onward=2)
    acc, b1, b_next = take(acc, b_next)
    acc = attend(acc, a2 + a3)
    acc = attend(acc, b1)
    acc, b2, b_next = take(acc, b_next)
    acc, a4, _ = take(acc, a_next, onward=0)
    acc = attend(acc, b2 + a4)
    acc, b3, b_next = take(acc, b_next, onward=2)
    acc = attend(acc, b3[:1])
    acc = attend(acc, b3[1:])
    acc, b4, _ = take(acc, b_next, onward=0)
    acc = attend(acc, b4)

    attended, far_a, far_b = finish(chunks, vis, queries, kv, acc, out_weight)
    relay_a, relay_b = turn(far_a, 1), turn(far_b, -1)
    up_a, up_b, down_a, down_b, own_sum = project_near(attended, out_weight, residual)
    from_below_b, from_above_a = turn(up_b, 1), turn(down_a, -1)
    up_sum = (up_a.astype(F32) + relay_a.astype(F32)).astype(BF16)
    up_sum, relay_b = lax.optimization_barrier((up_sum, relay_b))
    from_below_a = turn(up_sum, 1)
    from_above_b = turn((down_b.astype(F32) + relay_b.astype(F32)).astype(BF16), -1)
    below = jnp.concatenate([from_below_a, from_below_b], axis=0).astype(F32)
    above = jnp.concatenate([from_above_a, from_above_b], axis=0).astype(F32)
    updated = (own_sum + below + above).astype(BF16)

    attended, page_owner = lax.optimization_barrier((attended, page_owner))
    cache = take_pages(layout, find_pages(page_owner), chunks)
    kv_cache = cache.reshape(1, 1, sections, 2, PAGE_TOK, 2 * HD)
    return (updated, kv_cache)


def solution(mesh):
    return jax.shard_map(
        local,
        mesh=mesh,
        in_specs=(
            P("section", "tensor"),
            P("section", "tensor"),
            P("section", "tensor"),
            P("tensor", None),
            P("section", "tensor"),
            P(),
            P(None, "tensor", None, None),
        ),
        out_specs=(P("section", "tensor"), P("section", "tensor", None, None, None, None)),
        check_vma=False,
    )
```

```python
import functools
import math

import jax
import jax.numpy as jnp
from jax import lax
from jax.experimental import pallas as pl
from jax.experimental.pallas import tpu as pltpu
from jax.sharding import PartitionSpec as P

HD = 128
GROUP = 8
SPAN = 256
PAGE_TOK = 8
PPH = 32
XS, ZS = 4, 8
SCALE2 = math.log2(math.e) / math.sqrt(HD)
FLOOR = -1e30
LIMIT = 1e30
F32, BF16 = jnp.float32, jnp.bfloat16
NT = (((1,), (1,)), ((), ()))
VMEM = pl.BlockSpec(memory_space=pltpu.VMEM)
SMEM = pl.BlockSpec(memory_space=pltpu.SMEM)
ANY = pl.BlockSpec(memory_space=pl.ANY)
HBM = pl.BlockSpec(memory_space=pltpu.HBM)


def params(mib):
    return pltpu.CompilerParams(vmem_limit_bytes=mib * 2**20)


def section_at(x, z, core):
    return ((x % XS) * ZS + z % ZS) * 2 + core


def across(a):
    pairs = [
        (section_at(x, z, c), section_at(x + 2, z, c))
        for x in range(XS)
        for z in range(ZS)
        for c in range(2)
    ]
    return lax.ppermute(a, "section", pairs)


def pass_on(a, dx=0, dz=0):
    pairs = [
        (section_at(x, z, c), section_at(x + (1 - 2 * c) * dx, z + (1 - 2 * c) * dz, c))
        for x in range(XS)
        for z in range(ZS)
        for c in range(2)
    ]
    return lax.ppermute(a, "section", pairs)


def swap_core(a):
    return lax.ppermute(a, "section", [(s, s ^ 1) for s in range(XS * ZS * 2)])


def turn(a, d):
    n = lax.axis_size("tensor")
    return lax.ppermute(a, "tensor", [(t, (t + d) % n) for t in range(n)])


def head_column(m, h):
    lane = lax.broadcasted_iota(jnp.int32, m.shape, 1)
    return jnp.sum(jnp.where(lane == h, m, 0.0), axis=1, keepdims=True)


def pack_kernel(keys, values, out, sems):
    copies = [
        pltpu.make_async_copy(keys, out.at[:, :HD], sems.at[0]),
        pltpu.make_async_copy(values, out.at[:, HD:], sems.at[1]),
    ]
    for copy in copies:
        copy.start()
    for copy in copies:
        copy.wait()


def pack(keys, values):
    return pl.pallas_call(
        pack_kernel,
        in_specs=[HBM, HBM],
        out_specs=VMEM,
        out_shape=jax.ShapeDtypeStruct((SPAN, 2 * HD), BF16),
        scratch_shapes=[pltpu.SemaphoreType.DMA((2,))],
        compiler_params=params(60),
        name="pack",
    )(keys, values)


def my_place():
    me = lax.axis_index("section")
    return me >> 4, (me >> 1) & 7, me & 1


def section_id(here, offset):
    (x, z, core), (dx, dz, other) = here, offset
    way = 1 - 2 * core
    return ((((x + way * dx) & 3) * ZS + ((z + way * dz) & 7)) << 1) + (core ^ other)


def own_kernel(table, spans, q, kv, m_out, acc, vis):
    here = my_place()
    mine = spans[section_id(here, (0, 0, 0))]
    for i, offset in enumerate(table):
        vis[i] = jnp.where(spans[section_id(here, offset)] < mine, 1, 0)
    row = lax.broadcasted_iota(jnp.int32, (SPAN, SPAN), 0)
    col = lax.broadcasted_iota(jnp.int32, (SPAN, SPAN), 1)
    seen = col <= row
    lane = lax.broadcasted_iota(jnp.int32, (SPAN, HD), 1)
    key = kv[:, :HD]
    wide = jnp.concatenate([kv[:, HD:], jnp.ones((SPAN, HD), BF16)], axis=1)
    m = jnp.zeros((SPAN, HD), F32)
    for h in range(GROUP):
        s = lax.dot_general(q[:, h * HD : (h + 1) * HD], key, NT, preferred_element_type=F32)
        s = jnp.where(seen, s * SCALE2, FLOOR)
        peak = jnp.max(s, axis=1, keepdims=True)
        p = jnp.exp2(s - peak).astype(BF16)
        acc[h] = jnp.dot(p, wide, preferred_element_type=F32)
        m = jnp.where(lane == h, peak, m)
    m_out[...] = m


def attend_own(table, spans, q, kv):
    return pl.pallas_call(
        functools.partial(own_kernel, table),
        in_specs=[SMEM, VMEM, VMEM],
        out_specs=[VMEM, VMEM, SMEM],
        out_shape=[
            jax.ShapeDtypeStruct((SPAN, HD), F32),
            jax.ShapeDtypeStruct((GROUP, SPAN, 2 * HD), F32),
            jax.ShapeDtypeStruct((len(table),), jnp.int32),
        ],
        cost_estimate=pl.CostEstimate(
            flops=8 * GROUP * SPAN * SPAN * HD, bytes_accessed=2**22, transcendentals=GROUP * SPAN * SPAN
        ),
        compiler_params=params(16),
        name="own_span",
    )(spans, q, kv)


def pieces_kernel(sizes, first_unit, vis, *refs):
    count = len(sizes)
    chunks = refs[:count]
    q, m, acc_in, acc, vs = refs[count:]
    total = sum(sizes)
    row = 0
    for ref, n in zip(chunks, sizes):
        for j in range(0, n, SPAN):
            keep = vis[first_unit + (row + j) // SPAN] > 0
            value = ref[j : j + SPAN, HD:]
            vs[row + j : row + j + SPAN, :HD] = jnp.where(keep, value, jnp.zeros_like(value))
            vs[row + j : row + j + SPAN, HD:] = jnp.full((SPAN, HD), keep.astype(F32)).astype(BF16)
        row += n
    source, lo = acc_in, 0
    while lo < total:
        names, n = [], 0
        while len(names) < len(chunks) and n + sizes[len(names)] <= 2048:
            names.append(chunks[len(names)])
            n += sizes[len(names) - 1]
        chunks, sizes = chunks[len(names) :], sizes[len(names) :]
        some = vis[first_unit + lo // SPAN]
        for u in range(lo // SPAN + 1, (lo + n) // SPAN):
            some = some + vis[first_unit + u]

        @pl.when(some > 0)
        def _():
            for h in range(GROUP):
                reference = head_column(m[...], h)
                weights = []
                for ref in names:
                    s = lax.dot_general(
                        q[:, h * HD : (h + 1) * HD], ref[:, :HD], NT, preferred_element_type=F32
                    )
                    weights.append(jnp.exp2(s * SCALE2 - reference).astype(BF16))
                weights = jnp.concatenate(weights, axis=1)
                acc[h] = source[h] + jnp.dot(weights, vs[lo : lo + n, :], preferred_element_type=F32)

        if lo == 0:

            @pl.when(some == 0)
            def _():
                acc[...] = acc_in[...]

        source, lo = acc, lo + n


def attend_pieces(chunks, first_unit, vis, q, m, acc):
    sizes = [c.shape[0] for c in chunks]
    total = sum(sizes)
    return pl.pallas_call(
        functools.partial(pieces_kernel, sizes, first_unit),
        in_specs=[SMEM] + [VMEM] * (len(chunks) + 3),
        out_specs=VMEM,
        out_shape=jax.ShapeDtypeStruct(acc.shape, F32),
        scratch_shapes=[pltpu.VMEM((total, 2 * HD), BF16)],
        input_output_aliases={len(chunks) + 3: 0},
        cost_estimate=pl.CostEstimate(flops=2**20, bytes_accessed=2**18, transcendentals=0),
        compiler_params=params(16),
        name="attend_pieces",
    )(vis, *chunks, q, m, acc)


def online_step(h, q, key, value, seen, acc, m):
    s = lax.dot_general(
        q[:, pl.ds(pl.multiple_of(h * HD, HD), HD)], key, NT, preferred_element_type=F32
    )
    s = s * SCALE2
    if seen is not None:
        s = jnp.where(seen, s, FLOOR)
    before = m[h]
    peak = jnp.maximum(before, jnp.max(s, axis=1, keepdims=True))
    p = jnp.exp2(s - peak[:, :1]).astype(BF16)
    if seen is not None:
        p = jnp.where(seen, p, jnp.zeros_like(p))
    fade = jnp.exp2(before - peak)
    wide = jnp.concatenate([value, jnp.ones(value.shape, BF16)], axis=1)
    acc[h] = acc[h] * jnp.concatenate([fade, fade], axis=1) + jnp.dot(p, wide, preferred_element_type=F32)
    m[h] = peak


def project_columns(attended, weight, dest):
    cols = weight[:, pl.ds(pl.multiple_of(dest * 1024, 1024), 1024)]
    return jnp.dot(attended, cols, preferred_element_type=F32)


def finish_kernel(sizes, vis, *refs):
    count = len(sizes)
    chunks = refs[:count]
    q, kv, acc, weight, attended, far_a, far_b, safe, peak, block, sem = refs[count:]
    worst = jnp.max(jnp.maximum(jnp.max(acc[:, :, HD:], axis=0), 0.0))
    worst = jnp.where(worst < LIMIT, 0, 1)

    @pl.when(worst == 0)
    def _():
        for h in range(GROUP):
            attended[:, h * HD : (h + 1) * HD] = (acc[h, :, :HD] / acc[h, :, HD:]).astype(BF16)

    @pl.when(worst != 0)
    def _():
        safe[...] = jnp.zeros_like(safe)
        peak[...] = jnp.full_like(peak, FLOOR)
        row = lax.broadcasted_iota(jnp.int32, (SPAN, SPAN), 0)
        col = lax.broadcasted_iota(jnp.int32, (SPAN, SPAN), 1)

        @pl.loop(0, GROUP)
        def _(h):
            online_step(h, q, kv[:, :HD], kv[:, HD:], col <= row, safe, peak)

        first = 0
        for ref, n in zip(chunks, sizes):

            @pl.loop(0, n // SPAN)
            def _(u):
                @pl.when(vis[first + u] > 0)
                def _():
                    copy = pltpu.make_async_copy(
                        ref.at[pl.ds(pl.multiple_of(u * SPAN, SPAN), SPAN), :], block, sem
                    )
                    copy.start()
                    copy.wait()

                    @pl.loop(0, GROUP)
                    def _(h):
                        online_step(h, q, block[:, :HD], block[:, HD:], None, safe, peak)

            first += n // SPAN
        for h in range(GROUP):
            attended[:, h * HD : (h + 1) * HD] = (safe[h, :, :HD] / safe[h, :, HD:]).astype(BF16)

    far = project_columns(attended[...], weight, (lax.axis_index("tensor") + 2) & 3).astype(BF16)
    far_a[...] = far[: SPAN // 2]
    far_b[...] = far[SPAN // 2 :]


def finish(chunks, vis, q, kv, acc, weight):
    sizes = [c.shape[0] for c in chunks]
    part = jax.ShapeDtypeStruct((SPAN // 2, 1024), BF16)
    return pl.pallas_call(
        functools.partial(finish_kernel, sizes),
        in_specs=[SMEM] + [ANY] * len(chunks) + [VMEM] * 4,
        out_specs=[VMEM] * 3,
        out_shape=[jax.ShapeDtypeStruct((SPAN, 1024), BF16), part, part],
        scratch_shapes=[
            pltpu.VMEM((GROUP, SPAN, 2 * HD), F32),
            pltpu.VMEM((GROUP, SPAN, HD), F32),
            pltpu.VMEM((SPAN, 2 * HD), BF16),
            pltpu.SemaphoreType.DMA,
        ],
        cost_estimate=pl.CostEstimate(flops=2 * SPAN * 1024 * 1024, bytes_accessed=2**22, transcendentals=0),
        compiler_params=params(16),
        name="finish",
    )(vis, *chunks, q, kv, acc, weight)


def near_kernel(attended, weight, residual, up_a, up_b, down_a, down_b, mine):
    half = SPAN // 2
    t = lax.axis_index("tensor")
    up = project_columns(attended[...], weight, (t + 1) & 3).astype(BF16)
    up_a[...] = up[:half]
    up_b[...] = up[half:]
    down = project_columns(attended[...], weight, (t + 3) & 3).astype(BF16)
    down_a[...] = down[:half]
    down_b[...] = down[half:]
    mine[...] = project_columns(attended[...], weight, t) + residual[...].astype(F32)


def project_near(attended, weight, residual):
    part = jax.ShapeDtypeStruct((SPAN // 2, 1024), BF16)
    return pl.pallas_call(
        near_kernel,
        in_specs=[VMEM] * 3,
        out_specs=[VMEM] * 5,
        out_shape=[part] * 4 + [jax.ShapeDtypeStruct((SPAN, 1024), F32)],
        cost_estimate=pl.CostEstimate(flops=6 * SPAN * 1024 * 1024, bytes_accessed=2**23, transcendentals=0),
        compiler_params=params(16),
        name="project_near",
    )(attended, weight, residual)


def pages_kernel(layout, pages, *refs):
    chunks, out = refs[:-1], refs[-1]
    here = my_place()
    for offset, (ref, row) in layout:
        s = section_id(here, offset)
        found = []
        for rank in range(2):
            page = pages[rank, s]
            pair = pl.multiple_of((jnp.maximum(page, 0) >> 1) * 16, 16)
            both = chunks[ref][pl.ds(row + pair, 16), :].astype(F32)
            one = jnp.where((page & 1) == 0, both[:PAGE_TOK], both[PAGE_TOK:])
            found.append(jnp.where(page >= 0, one, 0.0))
        out[pl.ds(pl.multiple_of(s * 16, 16), 16), :] = jnp.concatenate(found, axis=0).astype(BF16)


def take_pages(layout, pages, chunks):
    return pl.pallas_call(
        functools.partial(pages_kernel, layout),
        in_specs=[SMEM] + [VMEM] * len(chunks),
        out_specs=VMEM,
        out_shape=jax.ShapeDtypeStruct((2 * XS * ZS * 2 * PAGE_TOK, 2 * HD), BF16),
        cost_estimate=pl.CostEstimate(flops=2**20, bytes_accessed=2**23, transcendentals=0),
        compiler_params=params(16),
        name="take_pages",
    )(pages, *chunks)


def find_pages(page_owner):
    owners = page_owner.reshape(page_owner.shape[0], PPH)
    page_ids = jnp.arange(PPH, dtype=jnp.int32)[None, :]
    mine = owners == lax.axis_index("section")
    first = jnp.min(jnp.where(mine, page_ids, PPH), axis=1)
    last = jnp.max(jnp.where(mine, page_ids, -1), axis=1)
    return jnp.stack([jnp.where(first < PPH, first, -1), jnp.where(last > first, last, -1)])


def local(queries, keys, values, out_weight, residual, span_of_section, page_owner):
    sections = lax.axis_size("section")

    direct = [(0, 0, 0), (2, 0, 0), (-1, 0, 0), (-1, 0, 1)]

    def swapped(offsets):
        return [(-dx, -dz, 1 - c) for dx, dz, c in offsets]

    def moved(offsets, steps):
        return [(dx, dz - steps, c) for dx, dz, c in offsets]

    first, second = direct, swapped(direct)
    order = ["r0", "r1", "a10", "a11", "b10", "b11", "a20", "a21", "b20", "b21", "a30"]
    order += ["a31", "b30", "a40", "b31", "a41"]

    def held(name):
        part = moved({"r": first, "a": first, "b": second}[name[0]], int(name[1:-1] or 0))
        return swapped(part) if name[-1] == "1" else part

    pieces = [held(name) for name in order]
    place = {
        (dx % XS, dz % ZS, c): (number, i * SPAN)
        for number, offsets in enumerate(pieces)
        for i, (dx, dz, c) in enumerate(offsets)
    }
    relative = [(dx, dz, c) for dx in range(XS) for dz in range(ZS) for c in range(2)]
    layout = [(r, place[r]) for r in relative]
    table = [r for offsets in pieces for r in offsets]

    kv = pack(keys, values)
    far = across(kv)
    near = pass_on(jnp.concatenate([kv, swap_core(kv)], axis=0), dx=1)
    m, acc, vis = attend_own(table, span_of_section, queries, kv)
    near, far, acc = lax.optimization_barrier((near, far, acc))
    chunks = []

    def attend(acc, parts):
        arrays = [pair[side] for pair, side in parts]
        first_unit = sum(c.shape[0] for c in chunks) // SPAN
        chunks.extend(arrays)
        return attend_pieces(arrays, first_unit, vis, queries, m, acc)

    def take(acc, piece, onward=True):
        acc, piece = lax.optimization_barrier((acc, piece))
        return acc, [piece, swap_core(piece)], pass_on(piece, dz=1) if onward else None

    row = jnp.concatenate([kv, far, near], axis=0)
    a_next = pass_on(row, dz=1)
    row_swapped = swap_core(row)
    b_next = pass_on(row_swapped, dz=1)
    acc = attend(acc, [((row, row_swapped), 0), ((row, row_swapped), 1)])
    acc, a1, a_next = take(acc, a_next)
    acc, b1, b_next = take(acc, b_next)
    acc = attend(acc, [(a1, 0), (a1, 1), (b1, 0)])
    acc, a2, a_next = take(acc, a_next)
    acc = attend(acc, [(b1, 1), (a2, 0), (a2, 1)])
    acc, b2, b_next = take(acc, b_next)
    acc, a3, a_next = take(acc, a_next)
    acc = attend(acc, [(b2, 0), (b2, 1), (a3, 0)])
    acc, b3, _ = take(acc, b_next, onward=False)
    acc, a4, _ = take(acc, a_next, onward=False)
    acc = attend(acc, [(a3, 1), (b3, 0), (a4, 0)])
    acc = attend(acc, [(b3, 1), (a4, 1)])

    attended, far_a, far_b = finish(chunks, vis, queries, kv, acc, out_weight)
    relay_a, relay_b = turn(far_a, 1), turn(far_b, -1)
    up_a, up_b, down_a, down_b, own_sum = project_near(attended, out_weight, residual)
    from_below_b, from_above_a = turn(up_b, 1), turn(down_a, -1)
    up_sum = (up_a.astype(F32) + relay_a.astype(F32)).astype(BF16)
    up_sum, relay_b = lax.optimization_barrier((up_sum, relay_b))
    from_below_a = turn(up_sum, 1)
    from_above_b = turn((down_b.astype(F32) + relay_b.astype(F32)).astype(BF16), -1)
    below = jnp.concatenate([from_below_a, from_below_b], axis=0).astype(F32)
    above = jnp.concatenate([from_above_a, from_above_b], axis=0).astype(F32)
    updated = (own_sum + below + above).astype(BF16)

    attended, page_owner = lax.optimization_barrier((attended, page_owner))
    cache = take_pages(layout, find_pages(page_owner), chunks)
    kv_cache = cache.reshape(1, 1, sections, 2, PAGE_TOK, 2 * HD)
    return (updated, kv_cache)


def solution(mesh):
    return jax.shard_map(
        local,
        mesh=mesh,
        in_specs=(
            P("section", "tensor"),
            P("section", "tensor"),
            P("section", "tensor"),
            P("tensor", None),
            P("section", "tensor"),
            P(),
            P(None, "tensor", None, None),
        ),
        out_specs=(P("section", "tensor"), P("section", "tensor", None, None, None, None)),
        check_vma=False,
    )
```

```python
import functools
import math

import jax
import jax.numpy as jnp
from jax import lax
from jax.experimental import pallas as pl
from jax.experimental.pallas import tpu as pltpu
from jax.sharding import PartitionSpec as P

HD = 128
GROUP = 8
SPAN = 256
PAGE_TOK = 8
PPH = 32
XS, ZS = 4, 8
SCALE2 = math.log2(math.e) / math.sqrt(HD)
FLOOR = -1e30
LIMIT = 1e30
F32, BF16 = jnp.float32, jnp.bfloat16
NT = (((1,), (1,)), ((), ()))
VMEM = pl.BlockSpec(memory_space=pltpu.VMEM)
SMEM = pl.BlockSpec(memory_space=pltpu.SMEM)
ANY = pl.BlockSpec(memory_space=pl.ANY)
HBM = pl.BlockSpec(memory_space=pltpu.HBM)


def params(mib):
    return pltpu.CompilerParams(vmem_limit_bytes=mib * 2**20)


def section_at(x, z, core):
    return ((x % XS) * ZS + z % ZS) * 2 + core


def across(a):
    pairs = [
        (section_at(x, z, c), section_at(x + 2, z, c))
        for x in range(XS)
        for z in range(ZS)
        for c in range(2)
    ]
    return lax.ppermute(a, "section", pairs)


def pass_on(a, dx=0, dz=0):
    pairs = [
        (section_at(x, z, c), section_at(x + (1 - 2 * c) * dx, z + (1 - 2 * c) * dz, c))
        for x in range(XS)
        for z in range(ZS)
        for c in range(2)
    ]
    return lax.ppermute(a, "section", pairs)


def swap_core(a):
    return lax.ppermute(a, "section", [(s, s ^ 1) for s in range(XS * ZS * 2)])


def turn(a, d):
    n = lax.axis_size("tensor")
    return lax.ppermute(a, "tensor", [(t, (t + d) % n) for t in range(n)])


def head_column(m, h):
    lane = lax.broadcasted_iota(jnp.int32, m.shape, 1)
    return jnp.sum(jnp.where(lane == h, m, 0.0), axis=1, keepdims=True)


def pack_kernel(keys, values, out, sems):
    copies = [
        pltpu.make_async_copy(keys, out.at[:, :HD], sems.at[0]),
        pltpu.make_async_copy(values, out.at[:, HD:], sems.at[1]),
    ]
    for copy in copies:
        copy.start()
    for copy in copies:
        copy.wait()


def pack(keys, values):
    return pl.pallas_call(
        pack_kernel,
        in_specs=[HBM, HBM],
        out_specs=VMEM,
        out_shape=jax.ShapeDtypeStruct((SPAN, 2 * HD), BF16),
        scratch_shapes=[pltpu.SemaphoreType.DMA((2,))],
        compiler_params=params(60),
        name="pack",
    )(keys, values)


def my_place():
    me = lax.axis_index("section")
    return me >> 4, (me >> 1) & 7, me & 1


def section_id(here, offset):
    (x, z, core), (dx, dz, other) = here, offset
    way = 1 - 2 * core
    return ((((x + way * dx) & 3) * ZS + ((z + way * dz) & 7)) << 1) + (core ^ other)


def own_kernel(table, spans, q, kv, m_out, acc, vis):
    here = my_place()
    mine = spans[section_id(here, (0, 0, 0))]
    for i, offset in enumerate(table):
        vis[i] = jnp.where(spans[section_id(here, offset)] < mine, 1, 0)
    row = lax.broadcasted_iota(jnp.int32, (SPAN, SPAN), 0)
    col = lax.broadcasted_iota(jnp.int32, (SPAN, SPAN), 1)
    seen = col <= row
    lane = lax.broadcasted_iota(jnp.int32, (SPAN, HD), 1)
    key = kv[:, :HD]
    wide = jnp.concatenate([kv[:, HD:], jnp.ones((SPAN, HD), BF16)], axis=1)
    m = jnp.zeros((SPAN, HD), F32)
    for h in range(GROUP):
        s = lax.dot_general(q[:, h * HD : (h + 1) * HD], key, NT, preferred_element_type=F32)
        s = jnp.where(seen, s * SCALE2, FLOOR)
        peak = jnp.max(s, axis=1, keepdims=True)
        p = jnp.exp2(s - peak).astype(BF16)
        acc[h] = jnp.dot(p, wide, preferred_element_type=F32)
        m = jnp.where(lane == h, peak, m)
    m_out[...] = m


def attend_own(table, spans, q, kv):
    return pl.pallas_call(
        functools.partial(own_kernel, table),
        in_specs=[SMEM, VMEM, VMEM],
        out_specs=[VMEM, VMEM, SMEM],
        out_shape=[
            jax.ShapeDtypeStruct((SPAN, HD), F32),
            jax.ShapeDtypeStruct((GROUP, SPAN, 2 * HD), F32),
            jax.ShapeDtypeStruct((len(table),), jnp.int32),
        ],
        cost_estimate=pl.CostEstimate(
            flops=8 * GROUP * SPAN * SPAN * HD, bytes_accessed=2**22, transcendentals=GROUP * SPAN * SPAN
        ),
        compiler_params=params(16),
        name="own_span",
    )(spans, q, kv)


def pieces_kernel(sizes, first_unit, vis, *refs):
    count = len(sizes)
    chunks = refs[:count]
    q, m, acc_in, acc, vs = refs[count:]
    total = sum(sizes)
    row = 0
    for ref, n in zip(chunks, sizes):
        for j in range(0, n, SPAN):
            keep = vis[first_unit + (row + j) // SPAN] > 0
            value = ref[j : j + SPAN, HD:]
            vs[row + j : row + j + SPAN, :HD] = jnp.where(keep, value, jnp.zeros_like(value))
            vs[row + j : row + j + SPAN, HD:] = jnp.full((SPAN, HD), keep.astype(F32)).astype(BF16)
        row += n
    source, lo = acc_in, 0
    while lo < total:
        names, n = [], 0
        while len(names) < len(chunks) and n + sizes[len(names)] <= 2048:
            names.append(chunks[len(names)])
            n += sizes[len(names) - 1]
        chunks, sizes = chunks[len(names) :], sizes[len(names) :]
        some = vis[first_unit + lo // SPAN]
        for u in range(lo // SPAN + 1, (lo + n) // SPAN):
            some = some + vis[first_unit + u]

        @pl.when(some > 0)
        def _():
            for h in range(GROUP):
                reference = head_column(m[...], h)
                weights = []
                for ref in names:
                    s = lax.dot_general(
                        q[:, h * HD : (h + 1) * HD], ref[:, :HD], NT, preferred_element_type=F32
                    )
                    weights.append(jnp.exp2(s * SCALE2 - reference).astype(BF16))
                weights = jnp.concatenate(weights, axis=1)
                acc[h] = source[h] + jnp.dot(weights, vs[lo : lo + n, :], preferred_element_type=F32)

        if lo == 0:

            @pl.when(some == 0)
            def _():
                acc[...] = acc_in[...]

        source, lo = acc, lo + n


def attend_pieces(chunks, first_unit, vis, q, m, acc):
    sizes = [c.shape[0] for c in chunks]
    total = sum(sizes)
    return pl.pallas_call(
        functools.partial(pieces_kernel, sizes, first_unit),
        in_specs=[SMEM] + [VMEM] * (len(chunks) + 3),
        out_specs=VMEM,
        out_shape=jax.ShapeDtypeStruct(acc.shape, F32),
        scratch_shapes=[pltpu.VMEM((total, 2 * HD), BF16)],
        input_output_aliases={len(chunks) + 3: 0},
        cost_estimate=pl.CostEstimate(
            flops=8 * GROUP * SPAN * total * HD,
            bytes_accessed=total * 512 + 2**22,
            transcendentals=GROUP * SPAN * total,
        ),
        compiler_params=params(16),
        name="attend_pieces",
    )(vis, *chunks, q, m, acc)


def online_step(h, q, key, value, seen, acc, m):
    s = lax.dot_general(
        q[:, pl.ds(pl.multiple_of(h * HD, HD), HD)], key, NT, preferred_element_type=F32
    )
    s = s * SCALE2
    if seen is not None:
        s = jnp.where(seen, s, FLOOR)
    before = m[h]
    peak = jnp.maximum(before, jnp.max(s, axis=1, keepdims=True))
    p = jnp.exp2(s - peak[:, :1]).astype(BF16)
    if seen is not None:
        p = jnp.where(seen, p, jnp.zeros_like(p))
    fade = jnp.exp2(before - peak)
    wide = jnp.concatenate([value, jnp.ones(value.shape, BF16)], axis=1)
    acc[h] = acc[h] * jnp.concatenate([fade, fade], axis=1) + jnp.dot(p, wide, preferred_element_type=F32)
    m[h] = peak


def project_columns(attended, weight, dest):
    cols = weight[:, pl.ds(pl.multiple_of(dest * 1024, 1024), 1024)]
    return jnp.dot(attended, cols, preferred_element_type=F32)


def finish_kernel(sizes, vis, *refs):
    count = len(sizes)
    chunks = refs[:count]
    q, kv, acc, weight, attended, far_a, far_b, safe, peak, block, sem = refs[count:]
    worst = jnp.max(jnp.maximum(jnp.max(acc[:, :, HD:], axis=0), 0.0))
    worst = jnp.where(worst < LIMIT, 0, 1)

    @pl.when(worst == 0)
    def _():
        for h in range(GROUP):
            attended[:, h * HD : (h + 1) * HD] = (acc[h, :, :HD] / acc[h, :, HD:]).astype(BF16)

    @pl.when(worst != 0)
    def _():
        safe[...] = jnp.zeros_like(safe)
        peak[...] = jnp.full_like(peak, FLOOR)
        row = lax.broadcasted_iota(jnp.int32, (SPAN, SPAN), 0)
        col = lax.broadcasted_iota(jnp.int32, (SPAN, SPAN), 1)

        @pl.loop(0, GROUP)
        def _(h):
            online_step(h, q, kv[:, :HD], kv[:, HD:], col <= row, safe, peak)

        first = 0
        for ref, n in zip(chunks, sizes):

            @pl.loop(0, n // SPAN)
            def _(u):
                @pl.when(vis[first + u] > 0)
                def _():
                    copy = pltpu.make_async_copy(
                        ref.at[pl.ds(pl.multiple_of(u * SPAN, SPAN), SPAN), :], block, sem
                    )
                    copy.start()
                    copy.wait()

                    @pl.loop(0, GROUP)
                    def _(h):
                        online_step(h, q, block[:, :HD], block[:, HD:], None, safe, peak)

            first += n // SPAN
        for h in range(GROUP):
            attended[:, h * HD : (h + 1) * HD] = (safe[h, :, :HD] / safe[h, :, HD:]).astype(BF16)

    far = project_columns(attended[...], weight, (lax.axis_index("tensor") + 2) & 3).astype(BF16)
    far_a[...] = far[: SPAN // 2]
    far_b[...] = far[SPAN // 2 :]


def finish(chunks, vis, q, kv, acc, weight):
    sizes = [c.shape[0] for c in chunks]
    part = jax.ShapeDtypeStruct((SPAN // 2, 1024), BF16)
    return pl.pallas_call(
        functools.partial(finish_kernel, sizes),
        in_specs=[SMEM] + [ANY] * len(chunks) + [VMEM] * 4,
        out_specs=[VMEM] * 3,
        out_shape=[jax.ShapeDtypeStruct((SPAN, 1024), BF16), part, part],
        scratch_shapes=[
            pltpu.VMEM((GROUP, SPAN, 2 * HD), F32),
            pltpu.VMEM((GROUP, SPAN, HD), F32),
            pltpu.VMEM((SPAN, 2 * HD), BF16),
            pltpu.SemaphoreType.DMA,
        ],
        cost_estimate=pl.CostEstimate(flops=2 * SPAN * 1024 * 1024, bytes_accessed=2**22, transcendentals=0),
        compiler_params=params(16),
        name="finish",
    )(vis, *chunks, q, kv, acc, weight)


def near_kernel(attended, weight, residual, up_a, up_b, down_a, down_b, mine):
    half = SPAN // 2
    t = lax.axis_index("tensor")
    up = project_columns(attended[...], weight, (t + 1) & 3).astype(BF16)
    up_a[...] = up[:half]
    up_b[...] = up[half:]
    down = project_columns(attended[...], weight, (t + 3) & 3).astype(BF16)
    down_a[...] = down[:half]
    down_b[...] = down[half:]
    mine[...] = project_columns(attended[...], weight, t) + residual[...].astype(F32)


def project_near(attended, weight, residual):
    part = jax.ShapeDtypeStruct((SPAN // 2, 1024), BF16)
    return pl.pallas_call(
        near_kernel,
        in_specs=[VMEM] * 3,
        out_specs=[VMEM] * 5,
        out_shape=[part] * 4 + [jax.ShapeDtypeStruct((SPAN, 1024), F32)],
        cost_estimate=pl.CostEstimate(flops=6 * SPAN * 1024 * 1024, bytes_accessed=2**23, transcendentals=0),
        compiler_params=params(16),
        name="project_near",
    )(attended, weight, residual)


def pages_kernel(layout, pages, *refs):
    chunks, out = refs[:-1], refs[-1]
    here = my_place()
    for offset, (ref, row) in layout:
        s = section_id(here, offset)
        found = []
        for rank in range(2):
            page = pages[rank, s]
            pair = pl.multiple_of((jnp.maximum(page, 0) >> 1) * 16, 16)
            both = chunks[ref][pl.ds(row + pair, 16), :].astype(F32)
            one = jnp.where((page & 1) == 0, both[:PAGE_TOK], both[PAGE_TOK:])
            found.append(jnp.where(page >= 0, one, 0.0))
        out[pl.ds(pl.multiple_of(s * 16, 16), 16), :] = jnp.concatenate(found, axis=0).astype(BF16)


def take_pages(layout, pages, chunks):
    return pl.pallas_call(
        functools.partial(pages_kernel, layout),
        in_specs=[SMEM] + [VMEM] * len(chunks),
        out_specs=VMEM,
        out_shape=jax.ShapeDtypeStruct((2 * XS * ZS * 2 * PAGE_TOK, 2 * HD), BF16),
        cost_estimate=pl.CostEstimate(flops=2**20, bytes_accessed=2**23, transcendentals=0),
        compiler_params=params(16),
        name="take_pages",
    )(pages, *chunks)


def find_pages(page_owner):
    owners = page_owner.reshape(page_owner.shape[0], PPH)
    page_ids = jnp.arange(PPH, dtype=jnp.int32)[None, :]
    mine = owners == lax.axis_index("section")
    first = jnp.min(jnp.where(mine, page_ids, PPH), axis=1)
    last = jnp.max(jnp.where(mine, page_ids, -1), axis=1)
    return jnp.stack([jnp.where(first < PPH, first, -1), jnp.where(last > first, last, -1)])


def local(queries, keys, values, out_weight, residual, span_of_section, page_owner):
    sections = lax.axis_size("section")

    direct = [(0, 0, 0), (2, 0, 0), (-1, 0, 0), (-1, 0, 1)]

    def swapped(offsets):
        return [(-dx, -dz, 1 - c) for dx, dz, c in offsets]

    def moved(offsets, steps):
        return [(dx, dz - steps, c) for dx, dz, c in offsets]

    first, second = direct, swapped(direct)
    order = ["r0", "r1", "a10", "a11", "b10", "b11", "a20", "a21", "b20", "b21", "a30", "a31"]
    order += ["b30", "b31", "a40", "a41"]

    def held(name):
        part = moved({"r": first, "a": first, "b": second}[name[0]], int(name[1:-1] or 0))
        return swapped(part) if name[-1] == "1" else part

    pieces = [held(name) for name in order]
    place = {
        (dx % XS, dz % ZS, c): (number, i * SPAN)
        for number, offsets in enumerate(pieces)
        for i, (dx, dz, c) in enumerate(offsets)
    }
    relative = [(dx, dz, c) for dx in range(XS) for dz in range(ZS) for c in range(2)]
    layout = [(r, place[r]) for r in relative]
    table = [r for offsets in pieces for r in offsets]

    kv = pack(keys, values)
    far = across(kv)
    near = pass_on(jnp.concatenate([kv, swap_core(kv)], axis=0), dx=1)
    m, acc, vis = attend_own(table, span_of_section, queries, kv)
    near, far, acc = lax.optimization_barrier((near, far, acc))
    chunks = []

    def attend(acc, parts):
        arrays = [pair[side] for pair, side in parts]
        first_unit = sum(c.shape[0] for c in chunks) // SPAN
        chunks.extend(arrays)
        return attend_pieces(arrays, first_unit, vis, queries, m, acc)

    def take(acc, piece, onward=True):
        acc, piece = lax.optimization_barrier((acc, piece))
        return acc, [piece, swap_core(piece)], pass_on(piece, dz=1) if onward else None

    row = jnp.concatenate([kv, far, near], axis=0)
    a_next = pass_on(row, dz=1)
    row_swapped = swap_core(row)
    b_next = pass_on(row_swapped, dz=1)
    acc = attend(acc, [((row, row_swapped), 0), ((row, row_swapped), 1)])
    acc, a1, a_next = take(acc, a_next)
    acc, b1, b_next = take(acc, b_next)
    acc = attend(acc, [(a1, 0), (a1, 1), (b1, 0)])
    acc, a2, a_next = take(acc, a_next)
    acc, b2, b_next = take(acc, b_next)
    acc = attend(acc, [(b1, 1), (a2, 0), (a2, 1), (b2, 0)])
    acc, a3, a_next = take(acc, a_next)
    acc, b3, _ = take(acc, b_next, onward=False)
    acc = attend(acc, [(b2, 1), (a3, 0), (a3, 1), (b3, 0)])
    acc, a4, _ = take(acc, a_next, onward=False)
    acc = attend(acc, [(b3, 1), (a4, 0)])
    acc = attend(acc, [(a4, 1)])

    attended, far_a, far_b = finish(chunks, vis, queries, kv, acc, out_weight)
    relay_a, relay_b = turn(far_a, 1), turn(far_b, -1)
    up_a, up_b, down_a, down_b, own_sum = project_near(attended, out_weight, residual)
    from_below_b, from_above_a = turn(up_b, 1), turn(down_a, -1)
    up_sum = (up_a.astype(F32) + relay_a.astype(F32)).astype(BF16)
    up_sum, relay_b = lax.optimization_barrier((up_sum, relay_b))
    from_below_a = turn(up_sum, 1)
    from_above_b = turn((down_b.astype(F32) + relay_b.astype(F32)).astype(BF16), -1)
    below = jnp.concatenate([from_below_a, from_below_b], axis=0).astype(F32)
    above = jnp.concatenate([from_above_a, from_above_b], axis=0).astype(F32)
    updated = (own_sum + below + above).astype(BF16)

    attended, page_owner = lax.optimization_barrier((attended, page_owner))
    cache = take_pages(layout, find_pages(page_owner), chunks)
    kv_cache = cache.reshape(1, 1, sections, 2, PAGE_TOK, 2 * HD)
    return (updated, kv_cache)


def solution(mesh):
    return jax.shard_map(
        local,
        mesh=mesh,
        in_specs=(
            P("section", "tensor"),
            P("section", "tensor"),
            P("section", "tensor"),
            P("tensor", None),
            P("section", "tensor"),
            P(),
            P(None, "tensor", None, None),
        ),
        out_specs=(P("section", "tensor"), P("section", "tensor", None, None, None, None)),
        check_vma=False,
    )
```

```python
import functools
import math

import jax
import jax.numpy as jnp
from jax import lax
from jax.experimental import pallas as pl
from jax.experimental.pallas import tpu as pltpu
from jax.sharding import PartitionSpec as P

HD = 128
GROUP = 8
SPAN = 256
PAGE_TOK = 8
PPH = 32
XS, ZS = 4, 8
SCALE2 = math.log2(math.e) / math.sqrt(HD)
FLOOR = -1e30
LIMIT = 1e30
F32, BF16 = jnp.float32, jnp.bfloat16
NT = (((1,), (1,)), ((), ()))
VMEM = pl.BlockSpec(memory_space=pltpu.VMEM)
SMEM = pl.BlockSpec(memory_space=pltpu.SMEM)
ANY = pl.BlockSpec(memory_space=pl.ANY)
HBM = pl.BlockSpec(memory_space=pltpu.HBM)


def params(mib):
    return pltpu.CompilerParams(vmem_limit_bytes=mib * 2**20)


def section_at(x, z, core):
    return ((x % XS) * ZS + z % ZS) * 2 + core


def across(a):
    pairs = [
        (section_at(x, z, c), section_at(x + 2, z, c))
        for x in range(XS)
        for z in range(ZS)
        for c in range(2)
    ]
    return lax.ppermute(a, "section", pairs)


def pass_on(a, dx=0, dz=0):
    pairs = [
        (section_at(x, z, c), section_at(x + (1 - 2 * c) * dx, z + (1 - 2 * c) * dz, c))
        for x in range(XS)
        for z in range(ZS)
        for c in range(2)
    ]
    return lax.ppermute(a, "section", pairs)


def swap_core(a):
    return lax.ppermute(a, "section", [(s, s ^ 1) for s in range(XS * ZS * 2)])


def turn(a, d):
    n = lax.axis_size("tensor")
    return lax.ppermute(a, "tensor", [(t, (t + d) % n) for t in range(n)])


def head_column(m, h):
    lane = lax.broadcasted_iota(jnp.int32, m.shape, 1)
    return jnp.sum(jnp.where(lane == h, m, 0.0), axis=1, keepdims=True)


def pack_kernel(keys, values, out, sems):
    copies = [
        pltpu.make_async_copy(keys, out.at[:, :HD], sems.at[0]),
        pltpu.make_async_copy(values, out.at[:, HD:], sems.at[1]),
    ]
    for copy in copies:
        copy.start()
    for copy in copies:
        copy.wait()


def pack(keys, values):
    return pl.pallas_call(
        pack_kernel,
        in_specs=[HBM, HBM],
        out_specs=VMEM,
        out_shape=jax.ShapeDtypeStruct((SPAN, 2 * HD), BF16),
        scratch_shapes=[pltpu.SemaphoreType.DMA((2,))],
        compiler_params=params(60),
        name="pack",
    )(keys, values)


def stack_kernel(*refs):
    out, row = refs[-1], 0
    for ref in refs[:-1]:
        out[row : row + ref.shape[0], :] = ref[...]
        row += ref.shape[0]


def stack(*parts):
    rows = sum(p.shape[0] for p in parts)
    return pl.pallas_call(
        stack_kernel,
        in_specs=[VMEM] * len(parts),
        out_specs=VMEM,
        out_shape=jax.ShapeDtypeStruct((rows, parts[0].shape[1]), parts[0].dtype),
        compiler_params=params(16),
        name="stack",
    )(*parts)


def my_place():
    me = lax.axis_index("section")
    return me >> 4, (me >> 1) & 7, me & 1


def section_id(here, offset):
    (x, z, core), (dx, dz, other) = here, offset
    way = 1 - 2 * core
    return ((((x + way * dx) & 3) * ZS + ((z + way * dz) & 7)) << 1) + (core ^ other)


def own_kernel(table, spans, q, kv, owners, m_out, acc, vis, pages):
    here = my_place()
    page = lax.broadcasted_iota(jnp.int32, owners.shape, 1).astype(F32)
    hit = owners[...] == section_id(here, (0, 0, 0))
    first = jnp.min(jnp.where(hit, page, PPH), axis=1, keepdims=True)
    last = jnp.max(jnp.where(hit, page, -1.0), axis=1, keepdims=True)
    none = jnp.full(first.shape, -1.0, F32)
    found = jnp.where(
        lax.broadcasted_iota(jnp.int32, pages.shape, 1) == 0,
        jnp.where(first < PPH, first, none),
        jnp.where(last > first, last, none),
    )
    pages[...] = found.astype(jnp.int32)
    mine = spans[section_id(here, (0, 0, 0))]
    for i, offset in enumerate(table):
        vis[i] = jnp.where(spans[section_id(here, offset)] < mine, 1, 0)
    row = lax.broadcasted_iota(jnp.int32, (SPAN, SPAN), 0)
    col = lax.broadcasted_iota(jnp.int32, (SPAN, SPAN), 1)
    seen = col <= row
    lane = lax.broadcasted_iota(jnp.int32, (SPAN, HD), 1)
    key = kv[:, :HD]
    wide = jnp.concatenate([kv[:, HD:], jnp.ones((SPAN, HD), BF16)], axis=1)
    m = jnp.zeros((SPAN, HD), F32)
    for h in range(GROUP):
        s = lax.dot_general(q[:, h * HD : (h + 1) * HD], key, NT, preferred_element_type=F32)
        s = jnp.where(seen, s * SCALE2, FLOOR)
        peak = jnp.max(s, axis=1, keepdims=True)
        p = jnp.exp2(s - peak).astype(BF16)
        acc[h] = jnp.dot(p, wide, preferred_element_type=F32)
        m = jnp.where(lane == h, peak, m)
    m_out[...] = m


def attend_own(table, spans, q, kv, owners):
    return pl.pallas_call(
        functools.partial(own_kernel, table),
        in_specs=[SMEM, VMEM, VMEM, VMEM],
        out_specs=[VMEM, VMEM, SMEM, VMEM],
        out_shape=[
            jax.ShapeDtypeStruct((SPAN, HD), F32),
            jax.ShapeDtypeStruct((GROUP, SPAN, 2 * HD), F32),
            jax.ShapeDtypeStruct((len(table),), jnp.int32),
            jax.ShapeDtypeStruct((owners.shape[0], HD), jnp.int32),
        ],
        cost_estimate=pl.CostEstimate(
            flops=8 * GROUP * SPAN * SPAN * HD, bytes_accessed=2**22, transcendentals=GROUP * SPAN * SPAN
        ),
        compiler_params=params(16),
        name="own_span",
    )(spans, q, kv, owners)


def pieces_kernel(sizes, first_unit, vis, *refs):
    count = len(sizes)
    chunks = refs[:count]
    q, m, acc_in, acc, vs = refs[count:]
    total = sum(sizes)
    row = 0
    for ref, n in zip(chunks, sizes):
        for j in range(0, n, SPAN):
            keep = vis[first_unit + (row + j) // SPAN] > 0
            value = ref[j : j + SPAN, HD:]
            vs[row + j : row + j + SPAN, :HD] = jnp.where(keep, value, jnp.zeros_like(value))
            vs[row + j : row + j + SPAN, HD:] = jnp.full((SPAN, HD), keep.astype(F32)).astype(BF16)
        row += n
    source, lo = acc_in, 0
    while lo < total:
        names, n = [], 0
        while len(names) < len(chunks) and n + sizes[len(names)] <= 2048:
            names.append(chunks[len(names)])
            n += sizes[len(names) - 1]
        chunks, sizes = chunks[len(names) :], sizes[len(names) :]
        some = vis[first_unit + lo // SPAN]
        for u in range(lo // SPAN + 1, (lo + n) // SPAN):
            some = some + vis[first_unit + u]

        @pl.when(some > 0)
        def _():
            for h in range(GROUP):
                reference = head_column(m[...], h)
                weights = []
                for ref in names:
                    s = lax.dot_general(
                        q[:, h * HD : (h + 1) * HD], ref[:, :HD], NT, preferred_element_type=F32
                    )
                    weights.append(jnp.exp2(s * SCALE2 - reference).astype(BF16))
                weights = jnp.concatenate(weights, axis=1)
                acc[h] = source[h] + jnp.dot(weights, vs[lo : lo + n, :], preferred_element_type=F32)

        if lo == 0:

            @pl.when(some == 0)
            def _():
                acc[...] = acc_in[...]

        source, lo = acc, lo + n


def attend_pieces(chunks, first_unit, vis, q, m, acc):
    sizes = [c.shape[0] for c in chunks]
    total = sum(sizes)
    return pl.pallas_call(
        functools.partial(pieces_kernel, sizes, first_unit),
        in_specs=[SMEM] + [VMEM] * (len(chunks) + 3),
        out_specs=VMEM,
        out_shape=jax.ShapeDtypeStruct(acc.shape, F32),
        scratch_shapes=[pltpu.VMEM((total, 2 * HD), BF16)],
        input_output_aliases={len(chunks) + 3: 0},
        cost_estimate=pl.CostEstimate(
            flops=8 * GROUP * SPAN * total * HD,
            bytes_accessed=total * 512 + 2**22,
            transcendentals=GROUP * SPAN * total,
        ),
        compiler_params=params(16),
        name="attend_pieces",
    )(vis, *chunks, q, m, acc)


def online_step(h, q, key, value, seen, acc, m):
    s = lax.dot_general(
        q[:, pl.ds(pl.multiple_of(h * HD, HD), HD)], key, NT, preferred_element_type=F32
    )
    s = s * SCALE2
    if seen is not None:
        s = jnp.where(seen, s, FLOOR)
    before = m[h]
    peak = jnp.maximum(before, jnp.max(s, axis=1, keepdims=True))
    p = jnp.exp2(s - peak[:, :1]).astype(BF16)
    if seen is not None:
        p = jnp.where(seen, p, jnp.zeros_like(p))
    fade = jnp.exp2(before - peak)
    wide = jnp.concatenate([value, jnp.ones(value.shape, BF16)], axis=1)
    acc[h] = acc[h] * jnp.concatenate([fade, fade], axis=1) + jnp.dot(p, wide, preferred_element_type=F32)
    m[h] = peak


def project_columns(attended, weight, dest):
    cols = weight[:, pl.ds(pl.multiple_of(dest * 1024, 1024), 1024)]
    return jnp.dot(attended, cols, preferred_element_type=F32)


def finish_kernel(sizes, vis, *refs):
    count = len(sizes)
    chunks = refs[:count]
    q, kv, acc, weight, attended, far_a, far_b, safe, peak, block, sem = refs[count:]
    worst = jnp.max(jnp.maximum(jnp.max(acc[:, :, HD:], axis=0), 0.0))
    worst = jnp.where(worst < LIMIT, 0, 1)

    @pl.when(worst == 0)
    def _():
        for h in range(GROUP):
            attended[:, h * HD : (h + 1) * HD] = (acc[h, :, :HD] / acc[h, :, HD:]).astype(BF16)

    @pl.when(worst != 0)
    def _():
        safe[...] = jnp.zeros_like(safe)
        peak[...] = jnp.full_like(peak, FLOOR)
        row = lax.broadcasted_iota(jnp.int32, (SPAN, SPAN), 0)
        col = lax.broadcasted_iota(jnp.int32, (SPAN, SPAN), 1)

        @pl.loop(0, GROUP)
        def _(h):
            online_step(h, q, kv[:, :HD], kv[:, HD:], col <= row, safe, peak)

        first = 0
        for ref, n in zip(chunks, sizes):

            @pl.loop(0, n // SPAN)
            def _(u):
                @pl.when(vis[first + u] > 0)
                def _():
                    copy = pltpu.make_async_copy(
                        ref.at[pl.ds(pl.multiple_of(u * SPAN, SPAN), SPAN), :], block, sem
                    )
                    copy.start()
                    copy.wait()

                    @pl.loop(0, GROUP)
                    def _(h):
                        online_step(h, q, block[:, :HD], block[:, HD:], None, safe, peak)

            first += n // SPAN
        for h in range(GROUP):
            attended[:, h * HD : (h + 1) * HD] = (safe[h, :, :HD] / safe[h, :, HD:]).astype(BF16)

    far = project_columns(attended[...], weight, (lax.axis_index("tensor") + 2) & 3).astype(BF16)
    far_a[...] = far[: SPAN // 2]
    far_b[...] = far[SPAN // 2 :]


def finish(chunks, vis, q, kv, acc, weight):
    sizes = [c.shape[0] for c in chunks]
    part = jax.ShapeDtypeStruct((SPAN // 2, 1024), BF16)
    return pl.pallas_call(
        functools.partial(finish_kernel, sizes),
        in_specs=[SMEM] + [ANY] * len(chunks) + [VMEM] * 4,
        out_specs=[VMEM] * 3,
        out_shape=[jax.ShapeDtypeStruct((SPAN, 1024), BF16), part, part],
        scratch_shapes=[
            pltpu.VMEM((GROUP, SPAN, 2 * HD), F32),
            pltpu.VMEM((GROUP, SPAN, HD), F32),
            pltpu.VMEM((SPAN, 2 * HD), BF16),
            pltpu.SemaphoreType.DMA,
        ],
        cost_estimate=pl.CostEstimate(flops=2 * SPAN * 1024 * 1024, bytes_accessed=2**22, transcendentals=0),
        compiler_params=params(16),
        name="finish",
    )(vis, *chunks, q, kv, acc, weight)


def near_kernel(attended, weight, residual, up_a, up_b, down_a, down_b, mine):
    half = SPAN // 2
    t = lax.axis_index("tensor")
    up = project_columns(attended[...], weight, (t + 1) & 3).astype(BF16)
    up_a[...] = up[:half]
    up_b[...] = up[half:]
    down = project_columns(attended[...], weight, (t + 3) & 3).astype(BF16)
    down_a[...] = down[:half]
    down_b[...] = down[half:]
    mine[...] = project_columns(attended[...], weight, t) + residual[...].astype(F32)


def project_near(attended, weight, residual):
    part = jax.ShapeDtypeStruct((SPAN // 2, 1024), BF16)
    return pl.pallas_call(
        near_kernel,
        in_specs=[VMEM] * 3,
        out_specs=[VMEM] * 5,
        out_shape=[part] * 4 + [jax.ShapeDtypeStruct((SPAN, 1024), F32)],
        cost_estimate=pl.CostEstimate(flops=6 * SPAN * 1024 * 1024, bytes_accessed=2**23, transcendentals=0),
        compiler_params=params(16),
        name="project_near",
    )(attended, weight, residual)


def pages_kernel(layout, table, *refs):
    chunks, out, pages, sem = refs[:-3], refs[-3], refs[-2], refs[-1]
    copy = pltpu.make_async_copy(table, pages, sem)
    copy.start()
    copy.wait()
    here = my_place()
    for offset, (ref, row) in layout:
        s = section_id(here, offset)
        found = []
        for rank in range(2):
            page = pages[s, rank]
            pair = pl.multiple_of((jnp.maximum(page, 0) >> 1) * 16, 16)
            both = chunks[ref][pl.ds(row + pair, 16), :].astype(F32)
            one = jnp.where((page & 1) == 0, both[:PAGE_TOK], both[PAGE_TOK:])
            found.append(jnp.where(page >= 0, one, 0.0))
        out[pl.ds(pl.multiple_of(s * 16, 16), 16), :] = jnp.concatenate(found, axis=0).astype(BF16)


def take_pages(layout, pages, chunks):
    return pl.pallas_call(
        functools.partial(pages_kernel, layout),
        in_specs=[VMEM] + [VMEM] * len(chunks),
        out_specs=VMEM,
        scratch_shapes=[pltpu.SMEM(pages.shape, jnp.int32), pltpu.SemaphoreType.DMA],
        out_shape=jax.ShapeDtypeStruct((2 * XS * ZS * 2 * PAGE_TOK, 2 * HD), BF16),
        cost_estimate=pl.CostEstimate(flops=2**20, bytes_accessed=2**23, transcendentals=0),
        compiler_params=params(16),
        name="take_pages",
    )(pages, *chunks)


def add_kernel(a, b, out):
    out[...] = (a[...].astype(F32) + b[...].astype(F32)).astype(BF16)


def add(a, b):
    return pl.pallas_call(
        add_kernel,
        in_specs=[VMEM, VMEM],
        out_specs=VMEM,
        out_shape=jax.ShapeDtypeStruct(a.shape, BF16),
        compiler_params=params(16),
        name="add",
    )(a, b)


def total_kernel(mine, below_a, below_b, above_a, above_b, out):
    half = SPAN // 2
    for rows, below, above in ((slice(0, half), below_a, above_a), (slice(half, SPAN), below_b, above_b)):
        out[rows, :] = (mine[rows, :] + below[...].astype(F32) + above[...].astype(F32)).astype(BF16)


def total_of(mine, *parts):
    return pl.pallas_call(
        total_kernel,
        in_specs=[VMEM] * 5,
        out_specs=VMEM,
        out_shape=jax.ShapeDtypeStruct(mine.shape, BF16),
        compiler_params=params(16),
        name="total",
    )(mine, *parts)


def local(queries, keys, values, out_weight, residual, span_of_section, page_owner):
    sections = lax.axis_size("section")

    direct = [(0, 0, 0), (2, 0, 0), (-1, 0, 0), (-1, 0, 1)]

    def swapped(offsets):
        return [(-dx, -dz, 1 - c) for dx, dz, c in offsets]

    def moved(offsets, steps):
        return [(dx, dz - steps, c) for dx, dz, c in offsets]

    first, second = direct, swapped(direct)
    order = ["r0", "r1", "a10", "a11", "b10", "b11", "a20", "a21", "b20", "b21", "a30", "a31"]
    order += ["b30", "b31", "a40", "a41"]

    def held(name):
        part = moved({"r": first, "a": first, "b": second}[name[0]], int(name[1:-1] or 0))
        return swapped(part) if name[-1] == "1" else part

    pieces = [held(name) for name in order]
    place = {
        (dx % XS, dz % ZS, c): (number, i * SPAN)
        for number, offsets in enumerate(pieces)
        for i, (dx, dz, c) in enumerate(offsets)
    }
    relative = [(dx, dz, c) for dx in range(XS) for dz in range(ZS) for c in range(2)]
    layout = [(r, place[r]) for r in relative]
    table = [r for offsets in pieces for r in offsets]

    kv = pack(keys, values)
    far = across(kv)
    near = pass_on(stack(kv, swap_core(kv)), dx=1)
    owners = page_owner.reshape(sections, PPH)
    m, acc, vis, pages = attend_own(table, span_of_section, queries, kv, owners)
    near, far, acc = lax.optimization_barrier((near, far, acc))
    chunks = []

    def attend(acc, parts):
        arrays = [pair[side] for pair, side in parts]
        first_unit = sum(c.shape[0] for c in chunks) // SPAN
        chunks.extend(arrays)
        return attend_pieces(arrays, first_unit, vis, queries, m, acc)

    def take(acc, piece, onward=True):
        acc, piece = lax.optimization_barrier((acc, piece))
        return acc, [piece, swap_core(piece)], pass_on(piece, dz=1) if onward else None

    row = stack(kv, far, near)
    a_next = pass_on(row, dz=1)
    row_swapped = swap_core(row)
    b_next = pass_on(row_swapped, dz=1)
    acc = attend(acc, [((row, row_swapped), 0), ((row, row_swapped), 1)])
    acc, a1, a_next = take(acc, a_next)
    acc, b1, b_next = take(acc, b_next)
    acc = attend(acc, [(a1, 0), (a1, 1), (b1, 0)])
    acc, a2, a_next = take(acc, a_next)
    acc, b2, b_next = take(acc, b_next)
    acc = attend(acc, [(b1, 1), (a2, 0), (a2, 1), (b2, 0)])
    acc, a3, a_next = take(acc, a_next)
    acc, b3, _ = take(acc, b_next, onward=False)
    acc = attend(acc, [(b2, 1), (a3, 0), (a3, 1), (b3, 0)])
    acc, a4, _ = take(acc, a_next, onward=False)
    acc = attend(acc, [(b3, 1), (a4, 0)])
    acc = attend(acc, [(a4, 1)])

    attended, far_a, far_b = finish(chunks, vis, queries, kv, acc, out_weight)
    relay_a, relay_b = turn(far_a, 1), turn(far_b, -1)
    up_a, up_b, down_a, down_b, own_sum = project_near(attended, out_weight, residual)
    from_below_b, from_above_a = turn(up_b, 1), turn(down_a, -1)
    up_sum = add(up_a, relay_a)
    up_sum, relay_b = lax.optimization_barrier((up_sum, relay_b))
    from_below_a = turn(up_sum, 1)
    from_above_b = turn(add(down_b, relay_b), -1)
    pages, _ = lax.optimization_barrier((pages, far_a))
    cache = take_pages(layout, pages, chunks)
    updated = total_of(own_sum, from_below_a, from_below_b, from_above_a, from_above_b)
    kv_cache = cache.reshape(1, 1, sections, 2, PAGE_TOK, 2 * HD)
    return (updated, kv_cache)


def solution(mesh):
    return jax.shard_map(
        local,
        mesh=mesh,
        in_specs=(
            P("section", "tensor"),
            P("section", "tensor"),
            P("section", "tensor"),
            P("tensor", None),
            P("section", "tensor"),
            P(),
            P(None, "tensor", None, None),
        ),
        out_specs=(P("section", "tensor"), P("section", "tensor", None, None, None, None)),
        check_vma=False,
    )
```

```python
import functools
import math

import jax
import jax.numpy as jnp
from jax import lax
from jax.experimental import pallas as pl
from jax.experimental.pallas import tpu as pltpu
from jax.sharding import PartitionSpec as P

HD = 128
GROUP = 8
SPAN = 256
PAGE_TOK = 8
PPH = 32
XS, ZS = 4, 8
SCALE2 = math.log2(math.e) / math.sqrt(HD)
FLOOR = -1e30
LIMIT = 1e30
F32, BF16 = jnp.float32, jnp.bfloat16
NT = (((1,), (1,)), ((), ()))
VMEM = pl.BlockSpec(memory_space=pltpu.VMEM)
SMEM = pl.BlockSpec(memory_space=pltpu.SMEM)
ANY = pl.BlockSpec(memory_space=pl.ANY)
HBM = pl.BlockSpec(memory_space=pltpu.HBM)


def params(mib):
    return pltpu.CompilerParams(vmem_limit_bytes=mib * 2**20)


def section_at(x, z, core):
    return ((x % XS) * ZS + z % ZS) * 2 + core


def across(a):
    pairs = [
        (section_at(x, z, c), section_at(x + 2, z, c))
        for x in range(XS)
        for z in range(ZS)
        for c in range(2)
    ]
    return lax.ppermute(a, "section", pairs)


def pass_on(a, dx=0, dz=0):
    pairs = [
        (section_at(x, z, c), section_at(x + (1 - 2 * c) * dx, z + (1 - 2 * c) * dz, c))
        for x in range(XS)
        for z in range(ZS)
        for c in range(2)
    ]
    return lax.ppermute(a, "section", pairs)


def swap_core(a):
    return lax.ppermute(a, "section", [(s, s ^ 1) for s in range(XS * ZS * 2)])


def turn(a, d):
    n = lax.axis_size("tensor")
    return lax.ppermute(a, "tensor", [(t, (t + d) % n) for t in range(n)])


def head_column(m, h):
    lane = lax.broadcasted_iota(jnp.int32, m.shape, 1)
    return jnp.sum(jnp.where(lane == h, m, 0.0), axis=1, keepdims=True)


def pack_kernel(keys, values, out, sems):
    copies = [
        pltpu.make_async_copy(keys, out.at[:, :HD], sems.at[0]),
        pltpu.make_async_copy(values, out.at[:, HD:], sems.at[1]),
    ]
    for copy in copies:
        copy.start()
    for copy in copies:
        copy.wait()


def pack(keys, values):
    return pl.pallas_call(
        pack_kernel,
        in_specs=[HBM, HBM],
        out_specs=VMEM,
        out_shape=jax.ShapeDtypeStruct((SPAN, 2 * HD), BF16),
        scratch_shapes=[pltpu.SemaphoreType.DMA((2,))],
        compiler_params=params(60),
        name="pack",
    )(keys, values)


def stack_kernel(*refs):
    out, row = refs[-1], 0
    for ref in refs[:-1]:
        out[row : row + ref.shape[0], :] = ref[...]
        row += ref.shape[0]


def stack(*parts):
    rows = sum(p.shape[0] for p in parts)
    return pl.pallas_call(
        stack_kernel,
        in_specs=[VMEM] * len(parts),
        out_specs=VMEM,
        out_shape=jax.ShapeDtypeStruct((rows, parts[0].shape[1]), parts[0].dtype),
        compiler_params=params(16),
        name="stack",
    )(*parts)


def my_place():
    me = lax.axis_index("section")
    return me >> 4, (me >> 1) & 7, me & 1


def section_id(here, offset):
    (x, z, core), (dx, dz, other) = here, offset
    way = 1 - 2 * core
    return ((((x + way * dx) & 3) * ZS + ((z + way * dz) & 7)) << 1) + (core ^ other)


def own_kernel(table, spans, q, kv, owners, m_out, acc, vis, pages):
    here = my_place()
    page = lax.broadcasted_iota(jnp.int32, owners.shape, 1).astype(F32)
    hit = owners[...] == section_id(here, (0, 0, 0))
    first = jnp.min(jnp.where(hit, page, PPH), axis=1, keepdims=True)
    last = jnp.max(jnp.where(hit, page, -1.0), axis=1, keepdims=True)
    none = jnp.full(first.shape, -1.0, F32)
    found = jnp.where(
        lax.broadcasted_iota(jnp.int32, pages.shape, 1) == 0,
        jnp.where(first < PPH, first, none),
        jnp.where(last > first, last, none),
    )
    pages[...] = found.astype(jnp.int32)
    mine = spans[section_id(here, (0, 0, 0))]
    for i, offset in enumerate(table):
        vis[i] = jnp.where(spans[section_id(here, offset)] < mine, 1, 0)
    row = lax.broadcasted_iota(jnp.int32, (SPAN, SPAN), 0)
    col = lax.broadcasted_iota(jnp.int32, (SPAN, SPAN), 1)
    seen = col <= row
    lane = lax.broadcasted_iota(jnp.int32, (SPAN, HD), 1)
    key = kv[:, :HD]
    wide = jnp.concatenate([kv[:, HD:], jnp.ones((SPAN, HD), BF16)], axis=1)
    m = jnp.zeros((SPAN, HD), F32)
    for h in range(GROUP):
        s = lax.dot_general(q[:, h * HD : (h + 1) * HD], key, NT, preferred_element_type=F32)
        s = jnp.where(seen, s * SCALE2, FLOOR)
        peak = jnp.max(s, axis=1, keepdims=True)
        p = jnp.exp2(s - peak).astype(BF16)
        acc[h] = jnp.dot(p, wide, preferred_element_type=F32)
        m = jnp.where(lane == h, peak, m)
    m_out[...] = m


def attend_own(table, spans, q, kv, owners):
    return pl.pallas_call(
        functools.partial(own_kernel, table),
        in_specs=[SMEM, VMEM, VMEM, VMEM],
        out_specs=[VMEM, VMEM, SMEM, VMEM],
        out_shape=[
            jax.ShapeDtypeStruct((SPAN, HD), F32),
            jax.ShapeDtypeStruct((GROUP, SPAN, 2 * HD), F32),
            jax.ShapeDtypeStruct((len(table),), jnp.int32),
            jax.ShapeDtypeStruct((owners.shape[0], HD), jnp.int32),
        ],
        cost_estimate=pl.CostEstimate(
            flops=8 * GROUP * SPAN * SPAN * HD, bytes_accessed=2**22, transcendentals=GROUP * SPAN * SPAN
        ),
        compiler_params=params(16),
        name="own_span",
    )(spans, q, kv, owners)


def pieces_kernel(sizes, first_unit, vis, *refs):
    count = len(sizes)
    chunks = refs[:count]
    q, m, acc_in, acc, vs = refs[count:]
    total = sum(sizes)
    row = 0
    for ref, n in zip(chunks, sizes):
        for j in range(0, n, SPAN):
            keep = vis[first_unit + (row + j) // SPAN] > 0
            value = ref[j : j + SPAN, HD:]
            vs[row + j : row + j + SPAN, :HD] = jnp.where(keep, value, jnp.zeros_like(value))
            vs[row + j : row + j + SPAN, HD:] = jnp.full((SPAN, HD), keep.astype(F32)).astype(BF16)
        row += n
    source, lo = acc_in, 0
    while lo < total:
        names, n = [], 0
        while len(names) < len(chunks) and n + sizes[len(names)] <= 2048:
            names.append(chunks[len(names)])
            n += sizes[len(names) - 1]
        chunks, sizes = chunks[len(names) :], sizes[len(names) :]
        some = vis[first_unit + lo // SPAN]
        for u in range(lo // SPAN + 1, (lo + n) // SPAN):
            some = some + vis[first_unit + u]

        @pl.when(some > 0)
        def _():
            for h in range(GROUP):
                reference = head_column(m[...], h)
                weights = []
                for ref in names:
                    s = lax.dot_general(
                        q[:, h * HD : (h + 1) * HD], ref[:, :HD], NT, preferred_element_type=F32
                    )
                    weights.append(jnp.exp2(s * SCALE2 - reference).astype(BF16))
                weights = jnp.concatenate(weights, axis=1)
                acc[h] = source[h] + jnp.dot(weights, vs[lo : lo + n, :], preferred_element_type=F32)

        if lo == 0:

            @pl.when(some == 0)
            def _():
                acc[...] = acc_in[...]

        source, lo = acc, lo + n


def attend_pieces(chunks, first_unit, vis, q, m, acc):
    sizes = [c.shape[0] for c in chunks]
    total = sum(sizes)
    return pl.pallas_call(
        functools.partial(pieces_kernel, sizes, first_unit),
        in_specs=[SMEM] + [VMEM] * (len(chunks) + 3),
        out_specs=VMEM,
        out_shape=jax.ShapeDtypeStruct(acc.shape, F32),
        scratch_shapes=[pltpu.VMEM((total, 2 * HD), BF16)],
        input_output_aliases={len(chunks) + 3: 0},
        cost_estimate=pl.CostEstimate(
            flops=8 * GROUP * SPAN * total * HD,
            bytes_accessed=total * 512 + 2**22,
            transcendentals=GROUP * SPAN * total,
        ),
        compiler_params=params(16),
        name="attend_pieces",
    )(vis, *chunks, q, m, acc)


def online_step(h, q, key, value, seen, acc, m):
    s = lax.dot_general(
        q[:, pl.ds(pl.multiple_of(h * HD, HD), HD)], key, NT, preferred_element_type=F32
    )
    s = s * SCALE2
    if seen is not None:
        s = jnp.where(seen, s, FLOOR)
    before = m[h]
    peak = jnp.maximum(before, jnp.max(s, axis=1, keepdims=True))
    p = jnp.exp2(s - peak[:, :1]).astype(BF16)
    if seen is not None:
        p = jnp.where(seen, p, jnp.zeros_like(p))
    fade = jnp.exp2(before - peak)
    wide = jnp.concatenate([value, jnp.ones(value.shape, BF16)], axis=1)
    acc[h] = acc[h] * jnp.concatenate([fade, fade], axis=1) + jnp.dot(p, wide, preferred_element_type=F32)
    m[h] = peak


def project_columns(attended, weight, dest):
    cols = weight[:, pl.ds(pl.multiple_of(dest * 1024, 1024), 1024)]
    return jnp.dot(attended, cols, preferred_element_type=F32)


def finish_kernel(sizes, vis, *refs):
    count = len(sizes)
    chunks = refs[:count]
    q, kv, acc, weight, attended, far_a, far_b, safe, peak, block, sem = refs[count:]
    worst = jnp.max(jnp.maximum(jnp.max(acc[:, :, HD:], axis=0), 0.0))
    worst = jnp.where(worst < LIMIT, 0, 1)

    @pl.when(worst == 0)
    def _():
        for h in range(GROUP):
            attended[:, h * HD : (h + 1) * HD] = (acc[h, :, :HD] / acc[h, :, HD:]).astype(BF16)

    @pl.when(worst != 0)
    def _():
        safe[...] = jnp.zeros_like(safe)
        peak[...] = jnp.full_like(peak, FLOOR)
        row = lax.broadcasted_iota(jnp.int32, (SPAN, SPAN), 0)
        col = lax.broadcasted_iota(jnp.int32, (SPAN, SPAN), 1)

        @pl.loop(0, GROUP)
        def _(h):
            online_step(h, q, kv[:, :HD], kv[:, HD:], col <= row, safe, peak)

        first = 0
        for ref, n in zip(chunks, sizes):

            @pl.loop(0, n // SPAN)
            def _(u):
                @pl.when(vis[first + u] > 0)
                def _():
                    copy = pltpu.make_async_copy(
                        ref.at[pl.ds(pl.multiple_of(u * SPAN, SPAN), SPAN), :], block, sem
                    )
                    copy.start()
                    copy.wait()

                    @pl.loop(0, GROUP)
                    def _(h):
                        online_step(h, q, block[:, :HD], block[:, HD:], None, safe, peak)

            first += n // SPAN
        for h in range(GROUP):
            attended[:, h * HD : (h + 1) * HD] = (safe[h, :, :HD] / safe[h, :, HD:]).astype(BF16)

    far = project_columns(attended[...], weight, (lax.axis_index("tensor") + 2) & 3).astype(BF16)
    far_a[...] = far[: SPAN // 2]
    far_b[...] = far[SPAN // 2 :]


def finish(chunks, vis, q, kv, acc, weight):
    sizes = [c.shape[0] for c in chunks]
    part = jax.ShapeDtypeStruct((SPAN // 2, 1024), BF16)
    return pl.pallas_call(
        functools.partial(finish_kernel, sizes),
        in_specs=[SMEM] + [ANY] * len(chunks) + [VMEM] * 4,
        out_specs=[VMEM] * 3,
        out_shape=[jax.ShapeDtypeStruct((SPAN, 1024), BF16), part, part],
        scratch_shapes=[
            pltpu.VMEM((GROUP, SPAN, 2 * HD), F32),
            pltpu.VMEM((GROUP, SPAN, HD), F32),
            pltpu.VMEM((SPAN, 2 * HD), BF16),
            pltpu.SemaphoreType.DMA,
        ],
        cost_estimate=pl.CostEstimate(flops=2 * SPAN * 1024 * 1024, bytes_accessed=2**22, transcendentals=0),
        compiler_params=params(16),
        name="finish",
    )(vis, *chunks, q, kv, acc, weight)


def near_kernel(attended, weight, residual, up_a, up_b, down_a, down_b, mine):
    half = SPAN // 2
    t = lax.axis_index("tensor")
    up = project_columns(attended[...], weight, (t + 1) & 3).astype(BF16)
    up_a[...] = up[:half]
    up_b[...] = up[half:]
    down = project_columns(attended[...], weight, (t + 3) & 3).astype(BF16)
    down_a[...] = down[:half]
    down_b[...] = down[half:]
    mine[...] = project_columns(attended[...], weight, t) + residual[...].astype(F32)


def project_near(attended, weight, residual):
    part = jax.ShapeDtypeStruct((SPAN // 2, 1024), BF16)
    return pl.pallas_call(
        near_kernel,
        in_specs=[VMEM] * 3,
        out_specs=[VMEM] * 5,
        out_shape=[part] * 4 + [jax.ShapeDtypeStruct((SPAN, 1024), F32)],
        cost_estimate=pl.CostEstimate(flops=6 * SPAN * 1024 * 1024, bytes_accessed=2**23, transcendentals=0),
        compiler_params=params(16),
        name="project_near",
    )(attended, weight, residual)


def pages_kernel(layout, table, *refs):
    chunks, out, pages, sem = refs[:-3], refs[-3], refs[-2], refs[-1]
    copy = pltpu.make_async_copy(table, pages, sem)
    copy.start()
    copy.wait()
    here = my_place()
    for offset, (ref, row) in layout:
        s = section_id(here, offset)
        found = []
        for rank in range(2):
            page = pages[s, rank]
            pair = pl.multiple_of((jnp.maximum(page, 0) >> 1) * 16, 16)
            both = chunks[ref][pl.ds(row + pair, 16), :].astype(F32)
            one = jnp.where((page & 1) == 0, both[:PAGE_TOK], both[PAGE_TOK:])
            found.append(jnp.where(page >= 0, one, 0.0))
        out[pl.ds(pl.multiple_of(s * 16, 16), 16), :] = jnp.concatenate(found, axis=0).astype(BF16)


def take_pages(layout, pages, chunks):
    return pl.pallas_call(
        functools.partial(pages_kernel, layout),
        in_specs=[VMEM] + [VMEM] * len(chunks),
        out_specs=VMEM,
        scratch_shapes=[pltpu.SMEM(pages.shape, jnp.int32), pltpu.SemaphoreType.DMA],
        out_shape=jax.ShapeDtypeStruct((2 * XS * ZS * 2 * PAGE_TOK, 2 * HD), BF16),
        cost_estimate=pl.CostEstimate(flops=2**20, bytes_accessed=2**23, transcendentals=0),
        compiler_params=params(16),
        name="take_pages",
    )(pages, *chunks)


def add_kernel(a, b, out):
    out[...] = (a[...].astype(F32) + b[...].astype(F32)).astype(BF16)


def add(a, b):
    return pl.pallas_call(
        add_kernel,
        in_specs=[VMEM, VMEM],
        out_specs=VMEM,
        out_shape=jax.ShapeDtypeStruct(a.shape, BF16),
        compiler_params=params(16),
        name="add",
    )(a, b)


def total_kernel(mine, below_a, below_b, above_a, above_b, out):
    half = SPAN // 2
    for rows, below, above in ((slice(0, half), below_a, above_a), (slice(half, SPAN), below_b, above_b)):
        out[rows, :] = (mine[rows, :] + below[...].astype(F32) + above[...].astype(F32)).astype(BF16)


def total_of(mine, *parts):
    return pl.pallas_call(
        total_kernel,
        in_specs=[VMEM] * 5,
        out_specs=VMEM,
        out_shape=jax.ShapeDtypeStruct(mine.shape, BF16),
        compiler_params=params(16),
        name="total",
    )(mine, *parts)


def local(queries, keys, values, out_weight, residual, span_of_section, page_owner):
    sections = lax.axis_size("section")

    direct = [(0, 0, 0), (2, 0, 0), (-1, 0, 0), (1, 0, 0)]

    def swapped(offsets):
        return [(-dx, -dz, 1 - c) for dx, dz, c in offsets]

    def moved(offsets, steps):
        return [(dx, dz - steps, c) for dx, dz, c in offsets]

    first, second = direct, swapped(direct)
    order = ["r0", "r1", "a10", "a11", "b10", "b11", "a20", "a21", "b20", "b21", "a30", "a31"]
    order += ["b30", "b31", "a40", "a41"]

    def held(name):
        part = moved({"r": first, "a": first, "b": second}[name[0]], int(name[1:-1] or 0))
        return swapped(part) if name[-1] == "1" else part

    pieces = [held(name) for name in order]
    place = {
        (dx % XS, dz % ZS, c): (number, i * SPAN)
        for number, offsets in enumerate(pieces)
        for i, (dx, dz, c) in enumerate(offsets)
    }
    relative = [(dx, dz, c) for dx in range(XS) for dz in range(ZS) for c in range(2)]
    layout = [(r, place[r]) for r in relative]
    table = [r for offsets in pieces for r in offsets]

    kv = pack(keys, values)
    far = across(kv)
    before, after = pass_on(kv, dx=1), pass_on(kv, dx=-1)
    owners = page_owner.reshape(sections, PPH)
    m, acc, vis, pages = attend_own(table, span_of_section, queries, kv, owners)
    before, after, far, acc = lax.optimization_barrier((before, after, far, acc))
    chunks = []

    def attend(acc, parts):
        arrays = [pair[side] for pair, side in parts]
        first_unit = sum(c.shape[0] for c in chunks) // SPAN
        chunks.extend(arrays)
        return attend_pieces(arrays, first_unit, vis, queries, m, acc)

    def take(acc, piece, onward=True):
        acc, piece = lax.optimization_barrier((acc, piece))
        return acc, [piece, swap_core(piece)], pass_on(piece, dz=1) if onward else None

    row = stack(kv, far, before, after)
    a_next = pass_on(row, dz=1)
    row_swapped = swap_core(row)
    b_next = pass_on(row_swapped, dz=1)
    acc = attend(acc, [((row, row_swapped), 0), ((row, row_swapped), 1)])
    acc, a1, a_next = take(acc, a_next)
    acc, b1, b_next = take(acc, b_next)
    acc = attend(acc, [(a1, 0), (a1, 1), (b1, 0)])
    acc, a2, a_next = take(acc, a_next)
    acc, b2, b_next = take(acc, b_next)
    acc = attend(acc, [(b1, 1), (a2, 0), (a2, 1), (b2, 0)])
    acc, a3, a_next = take(acc, a_next)
    acc, b3, _ = take(acc, b_next, onward=False)
    acc = attend(acc, [(b2, 1), (a3, 0), (a3, 1), (b3, 0)])
    acc, a4, _ = take(acc, a_next, onward=False)
    acc = attend(acc, [(b3, 1), (a4, 0)])
    acc = attend(acc, [(a4, 1)])

    attended, far_a, far_b = finish(chunks, vis, queries, kv, acc, out_weight)
    relay_a, relay_b = turn(far_a, 1), turn(far_b, -1)
    up_a, up_b, down_a, down_b, own_sum = project_near(attended, out_weight, residual)
    from_below_b, from_above_a = turn(up_b, 1), turn(down_a, -1)
    up_sum = add(up_a, relay_a)
    up_sum, relay_b = lax.optimization_barrier((up_sum, relay_b))
    from_below_a = turn(up_sum, 1)
    from_above_b = turn(add(down_b, relay_b), -1)
    pages, _ = lax.optimization_barrier((pages, far_a))
    cache = take_pages(layout, pages, chunks)
    updated = total_of(own_sum, from_below_a, from_below_b, from_above_a, from_above_b)
    kv_cache = cache.reshape(1, 1, sections, 2, PAGE_TOK, 2 * HD)
    return (updated, kv_cache)


def solution(mesh):
    return jax.shard_map(
        local,
        mesh=mesh,
        in_specs=(
            P("section", "tensor"),
            P("section", "tensor"),
            P("section", "tensor"),
            P("tensor", None),
            P("section", "tensor"),
            P(),
            P(None, "tensor", None, None),
        ),
        out_specs=(P("section", "tensor"), P("section", "tensor", None, None, None, None)),
        check_vma=False,
    )
```

```python
import functools
import math

import jax
import jax.numpy as jnp
from jax import lax
from jax.experimental import pallas as pl
from jax.experimental.pallas import tpu as pltpu
from jax.sharding import PartitionSpec as P

HD = 128
GROUP = 8
SPAN = 256
PAGE_TOK = 8
PPH = 32
XS, ZS = 4, 8
SCALE2 = math.log2(math.e) / math.sqrt(HD)
FLOOR = -1e30
LIMIT = 1e30
F32, BF16 = jnp.float32, jnp.bfloat16
NT = (((1,), (1,)), ((), ()))
VMEM = pl.BlockSpec(memory_space=pltpu.VMEM)
SMEM = pl.BlockSpec(memory_space=pltpu.SMEM)
ANY = pl.BlockSpec(memory_space=pl.ANY)
HBM = pl.BlockSpec(memory_space=pltpu.HBM)


def params(mib):
    return pltpu.CompilerParams(vmem_limit_bytes=mib * 2**20)


def section_at(x, z, core):
    return ((x % XS) * ZS + z % ZS) * 2 + core


def across(a):
    pairs = [
        (section_at(x, z, c), section_at(x + 2, z, c))
        for x in range(XS)
        for z in range(ZS)
        for c in range(2)
    ]
    return lax.ppermute(a, "section", pairs)


def pass_on(a, dx=0, dz=0):
    pairs = [
        (section_at(x, z, c), section_at(x + (1 - 2 * c) * dx, z + (1 - 2 * c) * dz, c))
        for x in range(XS)
        for z in range(ZS)
        for c in range(2)
    ]
    return lax.ppermute(a, "section", pairs)


def swap_core(a):
    return lax.ppermute(a, "section", [(s, s ^ 1) for s in range(XS * ZS * 2)])


def turn(a, d):
    n = lax.axis_size("tensor")
    return lax.ppermute(a, "tensor", [(t, (t + d) % n) for t in range(n)])


def head_column(m, h):
    lane = lax.broadcasted_iota(jnp.int32, m.shape, 1)
    return jnp.sum(jnp.where(lane == h, m, 0.0), axis=1, keepdims=True)


def pack_kernel(keys, values, out, sems):
    copies = [
        pltpu.make_async_copy(keys, out.at[:, :HD], sems.at[0]),
        pltpu.make_async_copy(values, out.at[:, HD:], sems.at[1]),
    ]
    for copy in copies:
        copy.start()
    for copy in copies:
        copy.wait()


def pack(keys, values):
    return pl.pallas_call(
        pack_kernel,
        in_specs=[HBM, HBM],
        out_specs=VMEM,
        out_shape=jax.ShapeDtypeStruct((SPAN, 2 * HD), BF16),
        scratch_shapes=[pltpu.SemaphoreType.DMA((2,))],
        compiler_params=params(60),
        name="pack",
    )(keys, values)


def stack_kernel(*refs):
    out, row = refs[-1], 0
    for ref in refs[:-1]:
        out[row : row + ref.shape[0], :] = ref[...]
        row += ref.shape[0]


def stack(*parts):
    rows = sum(p.shape[0] for p in parts)
    return pl.pallas_call(
        stack_kernel,
        in_specs=[VMEM] * len(parts),
        out_specs=VMEM,
        out_shape=jax.ShapeDtypeStruct((rows, parts[0].shape[1]), parts[0].dtype),
        compiler_params=params(16),
        name="stack",
    )(*parts)


def my_place():
    me = lax.axis_index("section")
    return me >> 4, (me >> 1) & 7, me & 1


def section_id(here, offset):
    (x, z, core), (dx, dz, other) = here, offset
    way = 1 - 2 * core
    return ((((x + way * dx) & 3) * ZS + ((z + way * dz) & 7)) << 1) + (core ^ other)


def own_kernel(table, spans, q, kv, owners, m_out, acc, vis, pages):
    here = my_place()
    page = lax.broadcasted_iota(jnp.int32, owners.shape, 1).astype(F32)
    hit = owners[...] == section_id(here, (0, 0, 0))
    first = jnp.min(jnp.where(hit, page, PPH), axis=1, keepdims=True)
    last = jnp.max(jnp.where(hit, page, -1.0), axis=1, keepdims=True)
    none = jnp.full(first.shape, -1.0, F32)
    found = jnp.where(
        lax.broadcasted_iota(jnp.int32, pages.shape, 1) == 0,
        jnp.where(first < PPH, first, none),
        jnp.where(last > first, last, none),
    )
    pages[...] = found.astype(jnp.int32)
    mine = spans[section_id(here, (0, 0, 0))]
    for i, offset in enumerate(table):
        vis[i] = jnp.where(spans[section_id(here, offset)] < mine, 1, 0)
    row = lax.broadcasted_iota(jnp.int32, (SPAN, SPAN), 0)
    col = lax.broadcasted_iota(jnp.int32, (SPAN, SPAN), 1)
    seen = col <= row
    lane = lax.broadcasted_iota(jnp.int32, (SPAN, HD), 1)
    key = kv[:, :HD]
    wide = jnp.concatenate([kv[:, HD:], jnp.ones((SPAN, HD), BF16)], axis=1)
    m = jnp.zeros((SPAN, HD), F32)
    for h in range(GROUP):
        s = lax.dot_general(q[:, h * HD : (h + 1) * HD], key, NT, preferred_element_type=F32)
        s = jnp.where(seen, s * SCALE2, FLOOR)
        peak = jnp.max(s, axis=1, keepdims=True)
        p = jnp.exp2(s - peak).astype(BF16)
        acc[h] = jnp.dot(p, wide, preferred_element_type=F32)
        m = jnp.where(lane == h, peak, m)
    m_out[...] = m


def attend_own(table, spans, q, kv, owners):
    return pl.pallas_call(
        functools.partial(own_kernel, table),
        in_specs=[SMEM, VMEM, VMEM, VMEM],
        out_specs=[VMEM, VMEM, SMEM, VMEM],
        out_shape=[
            jax.ShapeDtypeStruct((SPAN, HD), F32),
            jax.ShapeDtypeStruct((GROUP, SPAN, 2 * HD), F32),
            jax.ShapeDtypeStruct((len(table),), jnp.int32),
            jax.ShapeDtypeStruct((owners.shape[0], HD), jnp.int32),
        ],
        cost_estimate=pl.CostEstimate(
            flops=8 * GROUP * SPAN * SPAN * HD, bytes_accessed=2**22, transcendentals=GROUP * SPAN * SPAN
        ),
        compiler_params=params(16),
        name="own_span",
    )(spans, q, kv, owners)


def pieces_kernel(sizes, first_unit, vis, *refs):
    count = len(sizes)
    chunks = refs[:count]
    q, m, acc_in, acc, vs = refs[count:]
    total = sum(sizes)
    row = 0
    for ref, n in zip(chunks, sizes):
        for j in range(0, n, SPAN):
            keep = vis[first_unit + (row + j) // SPAN] > 0
            value = ref[j : j + SPAN, HD:]
            vs[row + j : row + j + SPAN, :HD] = jnp.where(keep, value, jnp.zeros_like(value))
            vs[row + j : row + j + SPAN, HD:] = jnp.full((SPAN, HD), keep.astype(F32)).astype(BF16)
        row += n
    source, lo = acc_in, 0
    while lo < total:
        names, n = [], 0
        while len(names) < len(chunks) and n + sizes[len(names)] <= 2048:
            names.append(chunks[len(names)])
            n += sizes[len(names) - 1]
        chunks, sizes = chunks[len(names) :], sizes[len(names) :]
        some = vis[first_unit + lo // SPAN]
        for u in range(lo // SPAN + 1, (lo + n) // SPAN):
            some = some + vis[first_unit + u]

        @pl.when(some > 0)
        def _():
            for h in range(GROUP):
                reference = head_column(m[...], h)
                weights = []
                for ref in names:
                    s = lax.dot_general(
                        q[:, h * HD : (h + 1) * HD], ref[:, :HD], NT, preferred_element_type=F32
                    )
                    weights.append(jnp.exp2(s * SCALE2 - reference).astype(BF16))
                weights = jnp.concatenate(weights, axis=1)
                acc[h] = source[h] + jnp.dot(weights, vs[lo : lo + n, :], preferred_element_type=F32)

        if lo == 0:

            @pl.when(some == 0)
            def _():
                acc[...] = acc_in[...]

        source, lo = acc, lo + n


def attend_pieces(chunks, first_unit, vis, q, m, acc):
    sizes = [c.shape[0] for c in chunks]
    total = sum(sizes)
    return pl.pallas_call(
        functools.partial(pieces_kernel, sizes, first_unit),
        in_specs=[SMEM] + [VMEM] * (len(chunks) + 3),
        out_specs=VMEM,
        out_shape=jax.ShapeDtypeStruct(acc.shape, F32),
        scratch_shapes=[pltpu.VMEM((total, 2 * HD), BF16)],
        input_output_aliases={len(chunks) + 3: 0},
        cost_estimate=pl.CostEstimate(
            flops=8 * GROUP * SPAN * total * HD,
            bytes_accessed=total * 512 + 2**22,
            transcendentals=GROUP * SPAN * total,
        ),
        compiler_params=params(16),
        name="attend_pieces",
    )(vis, *chunks, q, m, acc)


def online_step(h, q, key, value, seen, acc, m):
    s = lax.dot_general(
        q[:, pl.ds(pl.multiple_of(h * HD, HD), HD)], key, NT, preferred_element_type=F32
    )
    s = s * SCALE2
    if seen is not None:
        s = jnp.where(seen, s, FLOOR)
    before = m[h]
    peak = jnp.maximum(before, jnp.max(s, axis=1, keepdims=True))
    p = jnp.exp2(s - peak[:, :1]).astype(BF16)
    if seen is not None:
        p = jnp.where(seen, p, jnp.zeros_like(p))
    fade = jnp.exp2(before - peak)
    wide = jnp.concatenate([value, jnp.ones(value.shape, BF16)], axis=1)
    acc[h] = acc[h] * jnp.concatenate([fade, fade], axis=1) + jnp.dot(p, wide, preferred_element_type=F32)
    m[h] = peak


def project_columns(attended, weight, dest):
    cols = weight[:, pl.ds(pl.multiple_of(dest * 1024, 1024), 1024)]
    return jnp.dot(attended, cols, preferred_element_type=F32)


def finish_kernel(sizes, vis, *refs):
    count = len(sizes)
    chunks = refs[:count]
    q, kv, acc, weight, attended, far_a, far_b, safe, peak, block, sem = refs[count:]
    worst = jnp.max(jnp.where(acc[:, :, HD:] < LIMIT, 0.0, 1.0))

    @pl.when(worst < 0.5)
    def _():
        for h in range(GROUP):
            attended[:, h * HD : (h + 1) * HD] = (acc[h, :, :HD] / acc[h, :, HD:]).astype(BF16)

    @pl.when(worst > 0.5)
    def _():
        safe[...] = jnp.zeros_like(safe)
        peak[...] = jnp.full_like(peak, FLOOR)
        row = lax.broadcasted_iota(jnp.int32, (SPAN, SPAN), 0)
        col = lax.broadcasted_iota(jnp.int32, (SPAN, SPAN), 1)

        @pl.loop(0, GROUP)
        def _(h):
            online_step(h, q, kv[:, :HD], kv[:, HD:], col <= row, safe, peak)

        first = 0
        for ref, n in zip(chunks, sizes):

            @pl.loop(0, n // SPAN)
            def _(u):
                @pl.when(vis[first + u] > 0)
                def _():
                    copy = pltpu.make_async_copy(
                        ref.at[pl.ds(pl.multiple_of(u * SPAN, SPAN), SPAN), :], block, sem
                    )
                    copy.start()
                    copy.wait()

                    @pl.loop(0, GROUP)
                    def _(h):
                        online_step(h, q, block[:, :HD], block[:, HD:], None, safe, peak)

            first += n // SPAN
        for h in range(GROUP):
            attended[:, h * HD : (h + 1) * HD] = (safe[h, :, :HD] / safe[h, :, HD:]).astype(BF16)

    far = project_columns(attended[...], weight, (lax.axis_index("tensor") + 2) & 3).astype(BF16)
    far_a[...] = far[: SPAN // 2]
    far_b[...] = far[SPAN // 2 :]


def finish(chunks, vis, q, kv, acc, weight):
    sizes = [c.shape[0] for c in chunks]
    part = jax.ShapeDtypeStruct((SPAN // 2, 1024), BF16)
    return pl.pallas_call(
        functools.partial(finish_kernel, sizes),
        in_specs=[SMEM] + [ANY] * len(chunks) + [VMEM] * 4,
        out_specs=[VMEM] * 3,
        out_shape=[jax.ShapeDtypeStruct((SPAN, 1024), BF16), part, part],
        scratch_shapes=[
            pltpu.VMEM((GROUP, SPAN, 2 * HD), F32),
            pltpu.VMEM((GROUP, SPAN, HD), F32),
            pltpu.VMEM((SPAN, 2 * HD), BF16),
            pltpu.SemaphoreType.DMA,
        ],
        cost_estimate=pl.CostEstimate(flops=2 * SPAN * 1024 * 1024, bytes_accessed=2**22, transcendentals=0),
        compiler_params=params(16),
        name="finish",
    )(vis, *chunks, q, kv, acc, weight)


def near_kernel(attended, weight, residual, up_a, up_b, down_a, down_b, mine):
    half = SPAN // 2
    t = lax.axis_index("tensor")
    up = project_columns(attended[...], weight, (t + 1) & 3).astype(BF16)
    up_a[...] = up[:half]
    up_b[...] = up[half:]
    down = project_columns(attended[...], weight, (t + 3) & 3).astype(BF16)
    down_a[...] = down[:half]
    down_b[...] = down[half:]
    mine[...] = project_columns(attended[...], weight, t) + residual[...].astype(F32)


def project_near(attended, weight, residual):
    part = jax.ShapeDtypeStruct((SPAN // 2, 1024), BF16)
    return pl.pallas_call(
        near_kernel,
        in_specs=[VMEM] * 3,
        out_specs=[VMEM] * 5,
        out_shape=[part] * 4 + [jax.ShapeDtypeStruct((SPAN, 1024), F32)],
        cost_estimate=pl.CostEstimate(flops=6 * SPAN * 1024 * 1024, bytes_accessed=2**23, transcendentals=0),
        compiler_params=params(16),
        name="project_near",
    )(attended, weight, residual)


def pages_kernel(layout, table, *refs):
    chunks, out, pages, sem = refs[:-3], refs[-3], refs[-2], refs[-1]
    copy = pltpu.make_async_copy(table, pages, sem)
    copy.start()
    copy.wait()
    here = my_place()
    for offset, (ref, row) in layout:
        s = section_id(here, offset)
        found = []
        for rank in range(2):
            page = pages[s, rank]
            pair = pl.multiple_of((jnp.maximum(page, 0) >> 1) * 16, 16)
            both = chunks[ref][pl.ds(row + pair, 16), :].astype(F32)
            one = jnp.where((page & 1) == 0, both[:PAGE_TOK], both[PAGE_TOK:])
            found.append(jnp.where(page >= 0, one, 0.0))
        out[pl.ds(pl.multiple_of(s * 16, 16), 16), :] = jnp.concatenate(found, axis=0).astype(BF16)


def take_pages(layout, pages, chunks):
    return pl.pallas_call(
        functools.partial(pages_kernel, layout),
        in_specs=[VMEM] + [VMEM] * len(chunks),
        out_specs=VMEM,
        scratch_shapes=[pltpu.SMEM(pages.shape, jnp.int32), pltpu.SemaphoreType.DMA],
        out_shape=jax.ShapeDtypeStruct((2 * XS * ZS * 2 * PAGE_TOK, 2 * HD), BF16),
        cost_estimate=pl.CostEstimate(flops=2**20, bytes_accessed=2**23, transcendentals=0),
        compiler_params=params(16),
        name="take_pages",
    )(pages, *chunks)


def add_kernel(a, b, out):
    out[...] = (a[...].astype(F32) + b[...].astype(F32)).astype(BF16)


def add(a, b):
    return pl.pallas_call(
        add_kernel,
        in_specs=[VMEM, VMEM],
        out_specs=VMEM,
        out_shape=jax.ShapeDtypeStruct(a.shape, BF16),
        compiler_params=params(16),
        name="add",
    )(a, b)


def total_kernel(mine, below_a, below_b, above_a, above_b, out):
    half = SPAN // 2
    for rows, below, above in ((slice(0, half), below_a, above_a), (slice(half, SPAN), below_b, above_b)):
        out[rows, :] = (mine[rows, :] + below[...].astype(F32) + above[...].astype(F32)).astype(BF16)


def total_of(mine, *parts):
    return pl.pallas_call(
        total_kernel,
        in_specs=[VMEM] * 5,
        out_specs=VMEM,
        out_shape=jax.ShapeDtypeStruct(mine.shape, BF16),
        compiler_params=params(16),
        name="total",
    )(mine, *parts)


def local(queries, keys, values, out_weight, residual, span_of_section, page_owner):
    sections = lax.axis_size("section")

    direct = [(0, 0, 0), (2, 0, 0), (-1, 0, 0), (1, 0, 0)]

    def swapped(offsets):
        return [(-dx, -dz, 1 - c) for dx, dz, c in offsets]

    def moved(offsets, steps):
        return [(dx, dz - steps, c) for dx, dz, c in offsets]

    first, second = direct, swapped(direct)
    order = ["r0", "r1", "a10", "a11", "b10", "b11", "a20", "a21", "b20", "b21", "a30", "a31"]
    order += ["b30", "b31", "a40", "a41"]

    def held(name):
        part = moved({"r": first, "a": first, "b": second}[name[0]], int(name[1:-1] or 0))
        return swapped(part) if name[-1] == "1" else part

    pieces = [held(name) for name in order]
    place = {
        (dx % XS, dz % ZS, c): (number, i * SPAN)
        for number, offsets in enumerate(pieces)
        for i, (dx, dz, c) in enumerate(offsets)
    }
    relative = [(dx, dz, c) for dx in range(XS) for dz in range(ZS) for c in range(2)]
    layout = [(r, place[r]) for r in relative]
    table = [r for offsets in pieces for r in offsets]

    kv = pack(keys, values)
    far = across(kv)
    before, after = pass_on(kv, dx=1), pass_on(kv, dx=-1)
    owners = page_owner.reshape(sections, PPH)
    m, acc, vis, pages = attend_own(table, span_of_section, queries, kv, owners)
    before, after, far, acc = lax.optimization_barrier((before, after, far, acc))
    chunks = []

    def attend(acc, parts):
        arrays = [pair[side] for pair, side in parts]
        first_unit = sum(c.shape[0] for c in chunks) // SPAN
        chunks.extend(arrays)
        return attend_pieces(arrays, first_unit, vis, queries, m, acc)

    def take(acc, piece, onward=True):
        acc, piece = lax.optimization_barrier((acc, piece))
        return acc, [piece, swap_core(piece)], pass_on(piece, dz=1) if onward else None

    row = stack(kv, far, before, after)
    a_next = pass_on(row, dz=1)
    row_swapped = swap_core(row)
    b_next = pass_on(row_swapped, dz=1)
    acc = attend(acc, [((row, row_swapped), 0), ((row, row_swapped), 1)])
    acc, a1, a_next = take(acc, a_next)
    acc, b1, b_next = take(acc, b_next)
    acc = attend(acc, [(a1, 0), (a1, 1), (b1, 0)])
    acc, a2, a_next = take(acc, a_next)
    acc, b2, b_next = take(acc, b_next)
    acc = attend(acc, [(b1, 1), (a2, 0), (a2, 1), (b2, 0)])
    acc, a3, a_next = take(acc, a_next)
    acc, b3, _ = take(acc, b_next, onward=False)
    acc = attend(acc, [(b2, 1), (a3, 0), (a3, 1), (b3, 0)])
    acc, a4, _ = take(acc, a_next, onward=False)
    acc = attend(acc, [(b3, 1), (a4, 0)])
    acc = attend(acc, [(a4, 1)])

    attended, far_a, far_b = finish(chunks, vis, queries, kv, acc, out_weight)
    relay_a, relay_b = turn(far_a, 1), turn(far_b, -1)
    up_a, up_b, down_a, down_b, own_sum = project_near(attended, out_weight, residual)
    from_below_b, from_above_a = turn(up_b, 1), turn(down_a, -1)
    up_sum = add(up_a, relay_a)
    up_sum, relay_b = lax.optimization_barrier((up_sum, relay_b))
    from_below_a = turn(up_sum, 1)
    from_above_b = turn(add(down_b, relay_b), -1)
    pages, _ = lax.optimization_barrier((pages, far_a))
    cache = take_pages(layout, pages, chunks)
    updated = total_of(own_sum, from_below_a, from_below_b, from_above_a, from_above_b)
    kv_cache = cache.reshape(1, 1, sections, 2, PAGE_TOK, 2 * HD)
    return (updated, kv_cache)


def solution(mesh):
    return jax.shard_map(
        local,
        mesh=mesh,
        in_specs=(
            P("section", "tensor"),
            P("section", "tensor"),
            P("section", "tensor"),
            P("tensor", None),
            P("section", "tensor"),
            P(),
            P(None, "tensor", None, None),
        ),
        out_specs=(P("section", "tensor"), P("section", "tensor", None, None, None, None)),
        check_vma=False,
    )
```
